32 devices in a mesh: section: 2 (over core), dp: 4 (over z), expert: 4 (over y, x).
Axes of the slice: x: 2, y: 2, z: 4, core: 2. Of those that a mesh axis runs over, the one named last changes fastest.
Arguments:
- inputs: bfloat16 [2, 3072, 1152], P(None, ('dp', 'expert')), may hold values from -6 to 6
- cotangent: bfloat16 [2, 3072, 1152], P(None, ('dp', 'expert')), may hold values from -6 to 6
- routes: int32 [2, 2, 3072, 1], P('section', None, ('dp', 'expert')), may hold values from 0 to 3; in each aligned block of 192 rows (0 to 191, 192 to 383, ..., all dimensions but the last counted through in order) at most 96 rows name the same one
- lengths: int32 [2, 4, 4], P(None, 'dp'), may hold values from 1 to 720, 768 in all within a row
- mixer_gain: float32 [2, 1152], P('section', ('dp', 'expert')), may hold values from 0.5 to 1.5
- input_weight: float32 [2, 1152, 4608], P('section', ('dp', 'expert')), may hold values from -0.1875 to 0.1875
- conv_weight: float32 [2, 4, 2304], P('section', None, ('dp', 'expert')), may hold values from -3 to 3
- conv_bias: float32 [2, 2304], P('section', ('dp', 'expert')), may hold values from -3 to 3
- select_weight: float32 [2, 2304, 104], P('section', ('dp', 'expert')), may hold values from -0.125 to 0.125
- step_weight: float32 [2, 72, 2304], P('section', None, ('dp', 'expert')), may hold values from -0.75 to 0.75
- step_bias: float32 [2, 2304], P('section', ('dp', 'expert')), may hold values from -9 to -2
- decay_log: float32 [2, 2304, 16], P('section', ('dp', 'expert')), may hold values from -2 to 2.5
- skip_gain: float32 [2, 2304], P('section', ('dp', 'expert')), may hold values from 0.5 to 1.5
- output_weight: float32 [2, 2304, 1152], P('section', ('dp', 'expert')), may hold values from -0.5 to 0.5
- expert_gain: float32 [2, 1152], P('section', ('dp', 'expert')), may hold values from 0.5 to 1.5
- router_weight: float32 [2, 1152, 4], P('section', ('dp', 'expert')), may hold values from -0.09375 to 0.09375
- up_weight: float32 [2, 4, 1152, 3072], P('section', 'expert', None, 'dp'), may hold values from -0.1875 to 0.1875
- down_weight: float32 [2, 4, 3072, 1152], P('section', 'expert', 'dp'), may hold values from -0.875 to 0.875
Outputs:
- layer_out: bfloat16 [2, 2, 3072, 1152], P('section', None, ('dp', 'expert'))
- input_grad: float32 [2, 2, 3072, 1152], P('section', None, ('dp', 'expert'))
- mixer_gain_grad: float32 [2, 1152], P('section', ('dp', 'expert'))
- input_weight_grad: float32 [2, 1152, 4608], P('section', ('dp', 'expert'))
- conv_weight_grad: float32 [2, 4, 2304], P('section', None, ('dp', 'expert'))
- conv_bias_grad: float32 [2, 2304], P('section', ('dp', 'expert'))
- select_weight_grad: float32 [2, 2304, 104], P('section', ('dp', 'expert'))
- step_weight_grad: float32 [2, 72, 2304], P('section', None, ('dp', 'expert'))
- step_bias_grad: float32 [2, 2304], P('section', ('dp', 'expert'))
- decay_log_grad: float32 [2, 2304, 16], P('section', ('dp', 'expert'))
- skip_gain_grad: float32 [2, 2304], P('section', ('dp', 'expert'))
- output_weight_grad: float32 [2, 2304, 1152], P('section', ('dp', 'expert'))
- expert_gain_grad: float32 [2, 1152], P('section', ('dp', 'expert'))
- router_weight_grad: float32 [2, 1152, 4], P('section', ('dp', 'expert'))
- up_weight_grad: float32 [2, 4, 1152, 3072], P('section', 'expert', None, 'dp')
- down_weight_grad: float32 [2, 4, 3072, 1152], P('section', 'expert', 'dp')
The draws below stay inside these ranges and needn't reach their ends.
Inputs may be any that keep to these rules, and one draw needn't show every extreme that they name: `routes`: within one layer and micro-batch, the 192 tokens of one device send at most 96 tokens to any one expert, and some expert receives exactly 96 of some device's tokens. Each row holds the 4 sequence lengths of one group in order; they sum to 768, and the longest is exactly 720.
All inputs are finite; a program needn't handle non-finite values.
Results may differ from the reference program's by a relative error of at most 0.025.
The reference program's roundings to bfloat16 on the way count: a program that leaves them out, or rounds other values in their place, can miss the bound.
Values may be sent and summed in bfloat16 or wider, within the bound.
A program may use at most 320 MiB of HBM per device.

```python
import math
import jax
import jax.numpy as jnp
import numpy as np
from jax import lax

D = 1152
DI = 2304
STATE = 16
DT_RANK = 72
CONV = 4
FF = 3072
TOK_DEV = 192
MICRO = 2
SLOTS = 4
EXPERTS = 4
TOKENS = 3072
GROUP_TOK = 768
LONGEST = 720
CAP = 96
N_DP = 4


def level_of(own_key, extent, cuts, smallest, largest):
    loudness, own = 1.0, jax.random.fold_in(own_key, 6)
    for position, blocks in cuts:
        steps = jnp.exp(jax.random.uniform(jax.random.fold_in(own, position), (blocks,), jnp.float32, smallest / len(cuts), largest / len(cuts)))
        loudness = loudness * jnp.repeat(steps, extent[position] // blocks).reshape([-1 if axis == position else 1 for axis in range(len(extent))])
    return loudness


def length_profile(amount, total, limit, slope):
    weights = [(1 << 20) // math.isqrt(grade ** slope) + 1 for grade in range(2, amount + 1)]
    rest, counts = total - limit - (amount - 1), [1] * (amount - 1)
    while rest > 0:
        candidates = [i for i in range(amount - 1) if counts[i] < limit]
        whole, left = sum([weights[i] for i in candidates]), rest
        for i in candidates:
            extra = min(limit - counts[i], max(1, left * weights[i] // whole), rest)
            counts[i] = counts[i] + extra
            rest = rest - extra
    return np.array([limit] + counts)


def uneven(key, amount, total, reach, lean):
    if amount == 2:
        one = jax.random.randint(key, (), max(1, total - reach), min(reach, total - 1) + 1)
        return jnp.stack([one, total - one])
    sizes = jnp.asarray(length_profile(amount, total, reach, lean), jnp.int32)
    pairs = (amount - 1) // 2
    donor, receiver = sizes[1:1 + 2 * pairs:2], sizes[2:2 + 2 * pairs:2]
    margin = jnp.minimum(donor - 1, reach - receiver)
    moved = jax.random.randint(jax.random.fold_in(key, 1), (pairs,), 0, 1 << 20) % (margin + 1)
    sizes = sizes.at[1:1 + 2 * pairs:2].set(donor - moved).at[2:2 + 2 * pairs:2].set(receiver + moved)
    return sizes[jax.random.permutation(jax.random.fold_in(key, 2), amount)]


def routed_block(rng, own, number, rows, count, top, bound, skew):
    sequence = jax.random.permutation(rng, count)
    heavy_load, ordinary = portions_of(count, rows * top, bound, skew, True), portions_of(count, rows * top, bound, skew, False)
    places = jnp.arange(count)

    def named(sizes, offset_by):
        used = int((sizes > 0).sum())
        fixed = max(1, used // 4)
        passed = fixed + (places - fixed + offset_by * (used - fixed)) % max(1, count - fixed)
        return jnp.zeros((count,), jnp.int32).at[sequence[jnp.where(places < fixed, places, passed)]].set(jnp.asarray(sizes, jnp.int32))

    sizes = jnp.where(number % 4 == 0, named(heavy_load, number // 4), named(ordinary, number - number // 4 - 1))
    mixed = jax.random.permutation(jax.random.fold_in(own, 3), count)
    source_of, receiver = mixed[0:count // 2 * 2:2], mixed[1:count // 2 * 2:2]
    slack = jnp.minimum(sizes[source_of] - 1, bound - sizes[receiver]) // 2
    slack = jnp.where((source_of == sequence[0]) | (receiver == sequence[0]) | (sizes[receiver] == 0), 0, jnp.maximum(slack, 0))
    passed = jax.random.randint(jax.random.fold_in(own, 4), (count // 2,), 0, 1 << 20) % (slack + 1)
    sizes = sizes.at[source_of].add(-passed).at[receiver].add(passed)
    items = jnp.searchsorted(jnp.cumsum(sizes), jnp.arange(rows * top), side="right").astype(jnp.int32)
    table = items.reshape(top, rows).T
    table = table[jax.random.permutation(jax.random.fold_in(own, 1), rows)]
    offset_by = jax.random.randint(jax.random.fold_in(own, 2), (rows, 1), 0, top)
    return jnp.take_along_axis(table, (jnp.arange(top)[None, :] + offset_by) % top, axis=1)


def portions_of(amount, total, reach, skew, full):
    weights = [(1 << 20) // math.isqrt(standing ** skew) + 1 for standing in range(1, amount + 1)]
    largest = reach if full else min(reach, max(-(-total // amount), total * weights[0] // sum(weights)))
    least = 1 if total - largest >= amount - 1 else 0
    counts, spare = [largest] + [least] * (amount - 1), total - largest - least * (amount - 1)
    while spare > 0:
        candidates = [i for i in range(1, amount) if counts[i] < largest] or [i for i in range(1, amount) if counts[i] < reach]
        pool, budget = sum([weights[i] for i in candidates]), spare
        for i in candidates:
            extra = min(reach - counts[i], max(1, budget * weights[i] // pool), spare)
            counts[i] = counts[i] + extra
            spare = spare - extra
    return np.array(counts)


def centred(stream_key, dims, scale, most, cuts=(), held_as=jnp.bfloat16):
    drawn = jax.random.normal(stream_key, dims, jnp.float32) * scale
    if len(cuts) > 0:
        drawn = level_of(stream_key, dims, cuts, -0.22, 0.18) * drawn
    return jnp.clip(drawn, min=-most, max=most).astype(held_as)


def setup_inputs(seed: int = 0) -> dict:
    key_list = jax.random.split(jax.random.key(seed), 19)
    inputs = centred(key_list[0], (MICRO, TOKENS, D), 1.0, 6.0, ((1, 16),))
    cotangent = centred(key_list[1], (MICRO, TOKENS, D), 1.0, 6.0, ((1, 16),))
    routes_keys = jax.random.split(jax.random.fold_in(key_list[2], 1), 2 * MICRO * TOKENS // TOK_DEV)
    routes_turns = jax.random.permutation(jax.random.fold_in(key_list[2], 3), 2 * MICRO * TOKENS // TOK_DEV)
    routes = jax.vmap(lambda own, number: routed_block(jax.random.fold_in(key_list[2], 2), own, number, TOK_DEV, EXPERTS, 1, CAP, 2))(routes_keys, routes_turns).reshape((2, MICRO, TOKENS, 1))
    lengths = jax.vmap(lambda own: uneven(own, SLOTS, GROUP_TOK, LONGEST, 2))(jax.random.split(key_list[3], MICRO * N_DP)).reshape((MICRO, N_DP, SLOTS)).astype(jnp.int32)
    mixer_gain = jnp.clip(1.0 + 0.1 * jax.random.normal(key_list[4], (2, D), jnp.float32), 0.5, 1.5)
    input_weight = centred(key_list[5], (2, D, 2 * DI), D ** -0.5, 0.1875, ((0, 2), (1, 16)), jnp.float32)
    conv_weight = centred(key_list[6], (2, CONV, DI), CONV ** -0.5, 3.0, ((0, 2), (2, 16)), jnp.float32)
    conv_bias = centred(key_list[7], (2, DI), 0.5, 3.0, ((0, 2), (1, 16)), jnp.float32)
    select_weight = centred(key_list[8], (2, DI, DT_RANK + 2 * STATE), DI ** -0.5, 0.125, ((0, 2), (1, 16)), jnp.float32)
    step_weight = centred(key_list[9], (2, DT_RANK, DI), DT_RANK ** -0.5, 0.75, ((0, 2), (2, 16)), jnp.float32)
    step_bias = jnp.clip(-9.0 + 7.0 * jax.random.uniform(key_list[10], (2, DI), jnp.float32) ** level_of(key_list[10], (2, DI), ((0, 2), (1, 16)), -0.2, 0.2), -9.0, -2.0)
    decay_log = jnp.clip(-2.0 + 4.5 * jax.random.uniform(key_list[11], (2, DI, STATE), jnp.float32) ** level_of(key_list[11], (2, DI, STATE), ((0, 2), (1, 16)), -0.2, 0.2), -2.0, 2.5)
    skip_gain = jnp.clip(0.5 + 1.0 * jax.random.uniform(key_list[12], (2, DI), jnp.float32) ** level_of(key_list[12], (2, DI), ((0, 2), (1, 16)), -0.2, 0.2), 0.5, 1.5)
    output_weight = centred(key_list[13], (2, DI, D), (DI // 16) ** -0.5, 0.5, ((0, 2), (1, 16)), jnp.float32)
    expert_gain = jnp.clip(1.0 + 0.1 * jax.random.normal(key_list[14], (2, D), jnp.float32), 0.5, 1.5)
    router_weight = centred(key_list[15], (2, D, EXPERTS), (4 * D) ** -0.5, 0.09375, ((0, 2), (1, 16)), jnp.float32)
    up_weight = centred(key_list[16], (2, EXPERTS, D, FF), D ** -0.5, 0.1875, ((0, 2), (1, 4), (3, 4)), jnp.float32)
    down_weight = centred(key_list[17], (2, EXPERTS, FF, D), (max(FF // (4 * EXPERTS * EXPERTS), 2)) ** -0.5, 0.875, ((0, 2), (1, 4), (2, 4)), jnp.float32)
    return dict(inputs=inputs, cotangent=cotangent, routes=routes, lengths=lengths, mixer_gain=mixer_gain, input_weight=input_weight, conv_weight=conv_weight, conv_bias=conv_bias, select_weight=select_weight, step_weight=step_weight, step_bias=step_bias, decay_log=decay_log, skip_gain=skip_gain, output_weight=output_weight, expert_gain=expert_gain, router_weight=router_weight, up_weight=up_weight, down_weight=down_weight)


epsilon = 1e-05
highest = lax.Precision.HIGHEST

@jax.custom_vjp
def low(v):
    return lax.optimization_barrier(v.astype(jnp.bfloat16)).astype(jnp.float32)

@jax.custom_vjp
def low_back(v):
    return v

def low_keep(v):
    return (low(v), None)

def low_pass(kept, grad):
    return (grad,)

def back_keep(v):
    return (v, None)

def back_low(kept, grad):
    return (low(grad),)
low.defvjp(low_keep, low_pass)
low_back.defvjp(back_keep, back_low)

def product(left, right):
    return jnp.dot(left, right, precision=highest, preferred_element_type=jnp.float32)

def norm_scale(residual, gain):
    return residual * lax.rsqrt(lax.optimization_barrier(jnp.mean(residual * residual, axis=-1, keepdims=True)) + epsilon) * gain

def group_docs(lengths_row):
    boundaries = jnp.cumsum(lengths_row, dtype=jnp.int32)
    positions = jnp.arange(GROUP_TOK, dtype=jnp.int32)
    documents = lax.optimization_barrier(jnp.sum((positions[:, None] >= boundaries[None, :]).astype(jnp.int32), axis=1, dtype=jnp.int32))
    starting = jnp.concatenate([jnp.ones((1,), bool), documents[1:] != documents[:-1]])
    return (documents.astype(jnp.int32), starting)

def causal_conv(values, documents, taps_weight, taps_bias):
    summed = taps_bias + taps_weight[CONV - 1] * values
    for offset in range(1, CONV):
        lagged = jnp.pad(values, ((offset, 0), (0, 0)))[:GROUP_TOK]
        lagged_docs = jnp.pad(documents, (offset, 0), constant_values=-1)[:GROUP_TOK]
        summed = summed + taps_weight[CONV - 1 - offset] * jnp.where((lagged_docs == documents)[:, None], lagged, 0.0)
    return summed

def selective(activated, step_size, input_map, output_map, starting, decay_rate, skip_gain):
    length = math.gcd(GROUP_TOK, 64)

    def one_block(carried, pieces):

        def one_token(state_now, element):
            act_now, step_now, in_now, out_now, start_now = element
            decays = jnp.exp(step_now[:, None] * decay_rate) * jnp.where(start_now, 0.0, 1.0)
            state_now = decays * state_now + (step_now * act_now)[:, None] * in_now[None, :]
            return (state_now, lax.optimization_barrier(jnp.sum(state_now * out_now[None, :], axis=1)))
        return lax.scan(one_token, carried, pieces)

    def blocked(values):
        return values.reshape((GROUP_TOK // length, length) + values.shape[1:])
    pieces = tuple((blocked(values) for values in (activated, step_size, input_map, output_map, starting)))
    _, outputs = lax.scan(jax.checkpoint(one_block), jnp.zeros(decay_rate.shape, decay_rate.dtype), pieces)
    return outputs.reshape(GROUP_TOK, -1) + skip_gain * activated

def whole_layer(residual, params, routing, documents, starting):
    mixer_gain, input_weight, conv_weight, conv_bias, select_weight, step_weight, step_bias, decay_log, skip_gain, output_weight, expert_gain, router_weight, up_weight, down_weight = tuple((low(master) for master in params))
    inner_width = input_weight.shape[1] // 2
    normed = low(norm_scale(residual, mixer_gain))
    mixed_in = low_back(low(product(normed, input_weight)))
    conv_in = mixed_in[:, :inner_width].reshape(N_DP, GROUP_TOK, inner_width)
    gate_in = mixed_in[:, inner_width:]
    conv_out = jax.vmap(causal_conv, in_axes=(0, 0, None, None))(conv_in, documents, conv_weight, conv_bias)
    activated = low(jax.nn.silu(conv_out)).reshape(-1, inner_width)
    projected = low_back(product(activated, select_weight))
    step_low = low(projected[:, :DT_RANK])
    input_map = projected[:, DT_RANK:DT_RANK + STATE]
    output_map = projected[:, DT_RANK + STATE:]
    step_size = jax.nn.softplus(low_back(product(step_low, step_weight)) + step_bias)
    decay_rate = -jnp.exp(decay_log)

    def grouped(values):
        return values.reshape((N_DP, GROUP_TOK) + values.shape[1:])
    scanned = jax.vmap(selective, in_axes=(0, 0, 0, 0, 0, None, None))(grouped(activated), grouped(step_size), grouped(input_map), grouped(output_map), starting, decay_rate, skip_gain)
    scanned = scanned.reshape(-1, inner_width)
    gated_out = low(scanned * jax.nn.silu(gate_in))
    middle = residual + low_back(product(gated_out, output_weight))
    normed_two = low(norm_scale(middle, expert_gain))
    logits = low_back(product(normed_two, router_weight))
    probability = jax.nn.softmax(logits, axis=-1)
    chosen = routing[:, None] == jnp.arange(EXPERTS, dtype=jnp.int32)[None, :]
    gate_value = lax.optimization_barrier(jnp.sum(jnp.where(chosen, probability, 0.0), axis=1))
    expert_in = low_back(normed_two)
    mixture = jnp.zeros_like(residual)
    for expert in range(EXPERTS):
        pre_act = low_back(product(expert_in, up_weight[expert]))
        hidden = low(jax.nn.gelu(pre_act))
        result = low_back(low(product(hidden, down_weight[expert])))
        mixture = mixture + jnp.where(chosen[:, expert][:, None], result, 0.0)
    return middle + gate_value[:, None] * mixture

def reference(inputs, cotangent, routes, lengths, mixer_gain, input_weight, conv_weight, conv_bias, select_weight, step_weight, step_bias, decay_log, skip_gain, output_weight, expert_gain, router_weight, up_weight, down_weight):
    masters = (mixer_gain, input_weight, conv_weight, conv_bias, select_weight, step_weight, step_bias, decay_log, skip_gain, output_weight, expert_gain, router_weight, up_weight, down_weight)
    betweens, finals, input_grads, between_grads = ([], [], [], [])
    totals = tuple((jnp.zeros_like(master) for master in masters))
    for micro_index in range(MICRO):
        documents, starting = jax.vmap(group_docs)(lengths[micro_index])
        first_params = tuple((master[0] for master in masters))
        second_params = tuple((master[1] for master in masters))
        first_routes = routes[0, micro_index, :, 0]
        second_routes = routes[1, micro_index, :, 0]

        def first_layer(residual, params):
            return low_back(low(whole_layer(residual, params, first_routes, documents, starting)))

        def second_layer(residual, params):
            return low(whole_layer(residual, params, second_routes, documents, starting))
        between, first_back = jax.vjp(first_layer, inputs[micro_index].astype(jnp.float32), first_params)
        final, second_back = jax.vjp(second_layer, between, second_params)
        back_between, second_grads = second_back(cotangent[micro_index].astype(jnp.float32))
        back_input, first_grads = first_back(back_between)
        totals = tuple((summed + jnp.stack([first_part, second_part]) for summed, first_part, second_part in zip(totals, first_grads, second_grads)))
        betweens.append(between)
        finals.append(final)
        input_grads.append(back_input)
        between_grads.append(back_between)
    layer_out = jnp.stack([jnp.stack(betweens), jnp.stack(finals)]).astype(jnp.bfloat16)
    input_grad = jnp.stack([jnp.stack(input_grads), jnp.stack(between_grads)])
    return (layer_out, input_grad, totals[0], totals[1], totals[2], totals[3], totals[4], totals[5], totals[6], totals[7], totals[8], totals[9], totals[10], totals[11], totals[12], totals[13])
```

```python
import functools
from types import SimpleNamespace

import jax
import jax.numpy as jnp
from jax import lax
from jax.experimental import pallas as pl
from jax.experimental.pallas import tpu as pltpu
from jax.sharding import PartitionSpec as P

epsilon = 1e-05
lanes = 128
group = 8
reset = 1e30


def row_of(tile, index, states):
    return jnp.broadcast_to(tile[index : index + 1, :], (states, tile.shape[1]))


def end_kernel(step_ref, act_ref, start_ref, in_ref, rate_ref, end_ref):
    rows, width = step_ref.shape
    states = rate_ref.shape[0]
    tiles = width // lanes
    cols = [slice(j * lanes, (j + 1) * lanes) for j in range(tiles)]

    def body(g, carry):
        state, total = carry
        at = pl.ds(pl.multiple_of(g * group, group), group)
        state = list(state)
        total = list(total)
        begin = start_ref[at, :]
        for j in range(tiles):
            step = step_ref[at, cols[j]]
            drive = step * act_ref[at, cols[j]].astype(jnp.float32)
            fall = step + begin
            total[j] = total[j] + fall
            rate = rate_ref[:, cols[j]]
            for i in range(group):
                decay = jnp.exp(row_of(fall, i, states) * rate)
                state[j] = decay * state[j] + row_of(drive, i, states) * in_ref[g * group + i]
        return tuple(state), tuple(total)

    zero = tuple(jnp.zeros((states, lanes), jnp.float32) for _ in range(tiles))
    none = tuple(jnp.zeros((group, lanes), jnp.float32) for _ in range(tiles))
    state, total = lax.fori_loop(0, rows // group, body, (zero, none))
    for j in range(tiles):
        end_ref[:states, cols[j]] = state[j]
        end_ref[states:, cols[j]] = total[j]


def scan_kernel(step_ref, act_ref, start_ref, in_ref, out_ref, rate_ref, entry_ref, skip_ref, y_ref):
    rows, width = step_ref.shape
    states = rate_ref.shape[0]
    tiles = width // lanes
    cols = [slice(j * lanes, (j + 1) * lanes) for j in range(tiles)]
    which = lax.broadcasted_iota(jnp.int32, (group, lanes), 0)

    def body(g, state):
        at = pl.ds(pl.multiple_of(g * group, group), group)
        state = list(state)
        begin = start_ref[at, :]
        for j in range(tiles):
            step = step_ref[at, cols[j]]
            act = act_ref[at, cols[j]].astype(jnp.float32)
            drive = step * act
            fall = step + begin
            rate = rate_ref[:, cols[j]]
            y = skip_ref[:, cols[j]] * act
            for i in range(group):
                decay = jnp.exp(row_of(fall, i, states) * rate)
                state[j] = decay * state[j] + row_of(drive, i, states) * in_ref[g * group + i]
                part = jnp.sum(state[j] * out_ref[g * group + i], axis=0, keepdims=True)
                y = y + jnp.where(which == i, part, 0.0)
            y_ref[at, cols[j]] = y
        return tuple(state)

    lax.fori_loop(
        0, rows // group, body, tuple(entry_ref[:, cols[j]] for j in range(tiles))
    )


def entry_kernel(step_ref, start_ref, out_ref, rate_ref, grad_ref, end_ref):
    rows, width = step_ref.shape
    states = rate_ref.shape[0]
    tiles = width // lanes
    cols = [slice(j * lanes, (j + 1) * lanes) for j in range(tiles)]
    groups = rows // group

    def body(k, state):
        g = groups - 1 - k
        at = pl.ds(pl.multiple_of(g * group, group), group)
        state = list(state)
        begin = start_ref[at, :]
        for j in range(tiles):
            fall = step_ref[at, cols[j]] + begin
            grad = grad_ref[at, cols[j]]
            rate = rate_ref[:, cols[j]]
            for i in reversed(range(group)):
                decay = jnp.exp(row_of(fall, i, states) * rate)
                state[j] = decay * (state[j] + row_of(grad, i, states) * out_ref[g * group + i])
        return tuple(state)

    zero = tuple(jnp.zeros((states, lanes), jnp.float32) for _ in range(tiles))
    state = lax.fori_loop(0, groups, body, zero)
    for j in range(tiles):
        end_ref[:, cols[j]] = state[j]


def back_kernel(
    step_ref, act_ref, start_ref, in_ref, out_ref, rate_ref, entry_ref, adj_ref, skip_ref, grad_ref,
    back_act_ref, back_step_ref, back_rate_ref, back_in_ref, back_out_ref, kept, decays,
):
    rows, width = step_ref.shape
    states = rate_ref.shape[0]
    tiles = width // lanes
    cols = [slice(j * lanes, (j + 1) * lanes) for j in range(tiles)]
    groups = rows // group
    which = lax.broadcasted_iota(jnp.int32, (group, lanes), 0)

    @pl.when(pl.program_id(0) == 0)
    def _():
        back_in_ref[...] = jnp.zeros_like(back_in_ref)
        back_out_ref[...] = jnp.zeros_like(back_out_ref)

    for j in range(tiles):
        kept[0, :, cols[j]] = entry_ref[:, cols[j]]

    def ahead(g, state):
        at = pl.ds(pl.multiple_of(g * group, group), group)
        state = list(state)
        begin = start_ref[at, :]
        for j in range(tiles):
            step = step_ref[at, cols[j]]
            drive = step * act_ref[at, cols[j]].astype(jnp.float32)
            fall = step + begin
            rate = rate_ref[:, cols[j]]
            for i in range(group):
                decay = jnp.exp(row_of(fall, i, states) * rate)
                decays[g * group + i, :, cols[j]] = decay
                state[j] = decay * state[j] + row_of(drive, i, states) * in_ref[g * group + i]
                kept[g * group + i + 1, :, cols[j]] = state[j]
        return tuple(state)

    lax.fori_loop(0, groups, ahead, tuple(entry_ref[:, cols[j]] for j in range(tiles)))

    def behind(k, carry):
        flow, slope = carry
        g = groups - 1 - k
        at = pl.ds(pl.multiple_of(g * group, group), group)
        flow = list(flow)
        slope = list(slope)
        back_in = [back_in_ref[g * group + i] for i in range(group)]
        back_out = [back_out_ref[g * group + i] for i in range(group)]
        for j in range(tiles):
            step = step_ref[at, cols[j]]
            act = act_ref[at, cols[j]].astype(jnp.float32)
            drive = step * act
            grad = grad_ref[at, cols[j]]
            rate = rate_ref[:, cols[j]]
            back_drive = jnp.zeros((group, lanes), jnp.float32)
            back_fall = jnp.zeros((group, lanes), jnp.float32)
            for i in reversed(range(group)):
                t = g * group + i
                grad_row = row_of(grad, i, states)
                adj = flow[j] + grad_row * out_ref[t]
                back_out[i] = back_out[i] + kept[t + 1, :, cols[j]] * grad_row
                back_in[i] = back_in[i] + adj * row_of(drive, i, states)
                part = jnp.sum(adj * in_ref[t], axis=0, keepdims=True)
                back_drive = back_drive + jnp.where(which == i, part, 0.0)
                flow[j] = adj * decays[t, :, cols[j]]
                turn = flow[j] * kept[t, :, cols[j]]
                part = jnp.sum(turn * rate, axis=0, keepdims=True)
                back_fall = back_fall + jnp.where(which == i, part, 0.0)
                slope[j] = slope[j] + row_of(step, i, states) * turn
            back_act_ref[at, cols[j]] = step * back_drive + skip_ref[:, cols[j]] * grad
            back_step_ref[at, cols[j]] = act * back_drive + back_fall
        for i in range(group):
            back_in_ref[g * group + i] = back_in[i]
            back_out_ref[g * group + i] = back_out[i]
        return tuple(flow), tuple(slope)

    zero = tuple(jnp.zeros((states, lanes), jnp.float32) for _ in range(tiles))
    _, slope = lax.fori_loop(
        0, groups, behind, (tuple(adj_ref[:, cols[j]] for j in range(tiles)), zero)
    )
    for j in range(tiles):
        back_rate_ref[:, cols[j]] = slope[j] * rate_ref[:, cols[j]]


def specs(rows, states, block):
    wide = pl.BlockSpec((rows, block), lambda c: (0, c))
    mark = pl.BlockSpec((rows, lanes), lambda c: (0, 0))
    maps = pl.BlockSpec((rows, states, lanes), lambda c: (0, 0, 0))
    held = pl.BlockSpec((states, block), lambda c: (0, c))
    line = pl.BlockSpec((1, block), lambda c: (0, c))
    total = pl.BlockSpec((states + group, block), lambda c: (0, c))
    return wide, mark, maps, held, line, total


def params(mib):
    return pltpu.CompilerParams(
        dimension_semantics=("arbitrary",), vmem_limit_bytes=mib * 1024 * 1024
    )


def block_of(width, most):
    best = lanes
    for tiles in range(1, most // lanes + 1):
        if width % (tiles * lanes) == 0:
            best = tiles * lanes
    return best


def f32(*shape):
    return jax.ShapeDtypeStruct(shape, jnp.float32)


def end_call(step, act, start, in_map, rate, block=None):
    rows, width = step.shape
    states = rate.shape[0]
    block = block or block_of(width, 384)
    wide, mark, maps, held, line, total = specs(rows, states, block)
    return pl.pallas_call(
        end_kernel,
        grid=(width // block,),
        in_specs=[wide, wide, mark, maps, held],
        out_specs=total,
        out_shape=f32(states + group, width),
        compiler_params=params(40),
        cost_estimate=pl.CostEstimate(flops=8 * rows * states * width, bytes_accessed=6 * rows * width, transcendentals=rows * states * width),
        name="state_end",
    )(step, act, start, in_map, rate)


def scan_call(step, act, start, in_map, out_map, rate, entry, skip, block=None):
    rows, width = step.shape
    states = rate.shape[0]
    block = block or block_of(width, 384)
    wide, mark, maps, held, line, total = specs(rows, states, block)
    return pl.pallas_call(
        scan_kernel,
        grid=(width // block,),
        in_specs=[wide, wide, mark, maps, maps, held, held, line],
        out_specs=wide,
        out_shape=f32(rows, width),
        compiler_params=params(40),
        cost_estimate=pl.CostEstimate(flops=12 * rows * states * width, bytes_accessed=10 * rows * width, transcendentals=rows * states * width),
        name="state_scan",
    )(step, act, start, in_map, out_map, rate, entry, skip)


def entry_call(step, start, out_map, rate, grad, block=None):
    rows, width = step.shape
    states = rate.shape[0]
    block = block or block_of(width, 384)
    wide, mark, maps, held, line, total = specs(rows, states, block)
    return pl.pallas_call(
        entry_kernel,
        grid=(width // block,),
        in_specs=[wide, mark, maps, held, wide],
        out_specs=held,
        out_shape=f32(states, width),
        compiler_params=params(40),
        cost_estimate=pl.CostEstimate(flops=8 * rows * states * width, bytes_accessed=8 * rows * width, transcendentals=rows * states * width),
        name="adjoint_entry",
    )(step, start, out_map, rate, grad)


def back_call(step, act, start, in_map, out_map, rate, entry, adj, skip, grad, block=None):
    rows, width = step.shape
    states = rate.shape[0]
    block = block or block_of(width, 384)
    wide, mark, maps, held, line, total = specs(rows, states, block)
    return pl.pallas_call(
        back_kernel,
        grid=(width // block,),
        in_specs=[wide, wide, mark, maps, maps, held, held, held, line, wide],
        out_specs=[wide, wide, held, maps, maps],
        out_shape=[
            f32(rows, width), f32(rows, width), f32(states, width),
            f32(rows, states, lanes), f32(rows, states, lanes),
        ],
        scratch_shapes=[
            pltpu.VMEM((rows + 1, states, block), jnp.float32),
            pltpu.VMEM((rows, states, block), jnp.float32),
        ],
        compiler_params=params(56),
        cost_estimate=pl.CostEstimate(flops=40 * rows * states * width, bytes_accessed=20 * rows * width, transcendentals=rows * states * width),
        name="scan_back",
    )(step, act, start, in_map, out_map, rate, entry, adj, skip, grad)


def from_behind(array, axis, by):
    length = lax.axis_size(axis)
    pairs = [(i, i + by) for i in range(length) if 0 <= i + by < length]
    return lax.ppermute(array, axis, pairs)


def norm_scale(residual, gain):
    return (
        residual * lax.rsqrt(jnp.mean(residual * residual, axis=-1, keepdims=True) + epsilon) * gain
    )


def product(left, right):
    return jnp.dot(left, right, preferred_element_type=jnp.float32)


def cross_rows(left, right):
    return lax.dot_general(
        left, right, (((0,), (0,)), ((), ())), preferred_element_type=jnp.float32
    )


def cross_cols(left, right):
    return lax.dot_general(
        left, right, (((1,), (1,)), ((), ())), preferred_element_type=jnp.float32
    )


def gate_product(values, gates):
    return values * jax.nn.silu(gates)


def doc_ids(lengths_row, positions):
    boundaries = jnp.cumsum(lengths_row, dtype=jnp.int32)
    counted = jnp.sum(
        (positions[:, None] >= boundaries[None, :]).astype(jnp.int32), axis=1, dtype=jnp.int32
    )
    return jnp.where(positions < 0, -1, counted)


def conv_act(wide_in, taps_weight, taps_bias, documents):
    tap_count = taps_weight.shape[0]
    row_count = wide_in.shape[0] - tap_count + 1
    own_docs = documents[tap_count - 1 :]
    summed = taps_bias + taps_weight[tap_count - 1] * wide_in[tap_count - 1 :]
    for offset in range(1, tap_count):
        start_row = tap_count - 1 - offset
        lagged = wide_in[start_row : start_row + row_count]
        same_doc = (documents[start_row : start_row + row_count] == own_docs)[:, None]
        summed = summed + taps_weight[start_row] * jnp.where(same_doc, lagged, 0.0)
    return jax.nn.silu(summed)


def dispatch_tables(chosen, capacity):
    indicator = chosen.astype(jnp.int32)
    row_count, expert_count = indicator.shape
    earlier_rows = jnp.cumsum(indicator, axis=0, dtype=jnp.int32) - indicator
    slot_rank = jnp.sum(earlier_rows * indicator, axis=1, dtype=jnp.int32)
    expert_of = jnp.sum(
        indicator * jnp.arange(expert_count, dtype=jnp.int32)[None, :], axis=1, dtype=jnp.int32
    )
    slot_index = expert_of * capacity + slot_rank
    all_slots = jnp.arange(expert_count * capacity, dtype=jnp.int32)
    matches = slot_index[None, :] == all_slots[:, None]
    token_index = jnp.sum(
        jnp.where(matches, jnp.arange(row_count, dtype=jnp.int32)[None, :], 0),
        axis=1,
        dtype=jnp.int32,
    )
    token_index = token_index + row_count * (1 - jnp.any(matches, axis=1).astype(jnp.int32))
    return (slot_index, token_index)


def gather_kernel(
    phase, along_dp, along_expert, own_refs, layer_refs,
    here_sem, z_send, z_recv, xy_send, xy_recv, c_send, c_recv,
):
    section = lax.axis_index("section")
    d = lax.axis_index("dp")
    e = lax.axis_index("expert")
    arrays = range(len(layer_refs[0]))
    mesh_id = pl.DeviceIdType.MESH
    ways = (1, -1)
    direct = [m for m in range(1, along_expert) if m != 3]

    def exists(index):
        return jnp.logical_and(index >= 0, index < along_dp)

    barrier = pltpu.get_barrier_semaphore()
    peers = [(section, d, e ^ m) for m in range(1, along_expert)] + [(1 - section, d, e)]
    for peer in peers:
        pl.semaphore_signal(barrier, inc=1, device_id=peer, device_id_type=mesh_id)
    expected = len(peers)
    if phase == 0:
        for way in ways:

            @pl.when(exists(d + way))
            def _():
                pl.semaphore_signal(
                    barrier, inc=1, device_id=(section, d + way, e), device_id_type=mesh_id
                )

        expected = expected + jnp.where(d > 0, 1, 0) + jnp.where(d < along_dp - 1, 1, 0)
    pl.semaphore_wait(barrier, expected)

    items = [(0, 0, 0)] + [
        (1 + 2 * step + (way < 0), way, step) for step in range(along_dp - 1) for way in ways
    ]

    def origin(item):
        index, way, step = item
        return d - way * (step + 1) if way else d

    def mine(item):
        if item[1] == 0:
            return phase == 0
        if item[2] > 0:
            return phase == 1
        return True if item[1] < 0 else phase == 0

    def here_now(item):
        if item[1] < 0 and item[2] == 0:
            return (d == 0) if phase == 0 else (d > 0)
        return d >= 0

    def when(item, *more):
        if item[1] == 0 and not more:
            return lambda work: work()
        alive = exists(origin(item))
        for other in more:
            alive = jnp.logical_and(alive, other)
        return pl.when(alive)

    def work(all_refs, other_refs):
        def place(item, m):
            return origin(item) * along_expert + (e ^ m)

        def copy(item, m, a, peer, send, recv):
            held = all_refs[a].at[place(item, m)]
            own = phase == 0 and item[1] == 0 and m == 0
            return pltpu.make_async_remote_copy(
                src_ref=own_refs[a] if own else held,
                dst_ref=held,
                send_sem=send,
                recv_sem=recv,
                device_id=peer,
                device_id_type=mesh_id,
            )

        def onward(item, way, a):
            step = item[2] + 1 if item[1] else 0
            k = 0 if way > 0 else 1
            peer = (section, d + way, e)
            return copy(item, 0, a, peer, z_send.at[k, step, a], z_recv.at[k, step, a])

        def to_expert(item, m, a):
            peer = (section, d, e ^ m)
            sems = (xy_send.at[item[0], m - 1, a], xy_recv.at[item[0], m - 1, a])
            return copy(item, 0, a, peer, *sems)

        def relayed(item, a):
            return 1 + (a + (item[2] + 1 if a == arrays[-1] else 0)) % 2

        def relay(item, m, a):
            peer = (section, d, e ^ 3 ^ m)
            sems = (xy_send.at[item[0], 2, a], xy_recv.at[item[0], 2, a])
            return copy(item, m, a, peer, *sems)

        def to_core(item, m, a):
            peer = (1 - section, d, e)
            return copy(item, m, a, peer, c_send.at[item[0], m, a], c_recv.at[item[0], m, a])

        def landed(ref, sem):
            pltpu.make_async_copy(ref, ref, sem).wait()

        def here(a):
            return pltpu.make_async_copy(
                own_refs[a], all_refs[a].at[place(items[0], 0)], here_sem.at[a]
            )

        def share(item):
            for a in arrays:
                for m in direct:
                    to_expert(item, m, a).start()

        def gather(item):
            for m in direct:
                for a in arrays:
                    landed(all_refs[a].at[place(item, m)], xy_recv.at[item[0], m - 1, a])
                    if m < 3 and relayed(item, a) == 3 - m:
                        relay(item, m, a).start()
                    to_core(item, m, a).start()

        def gather_last(item):
            for a in arrays:
                landed(all_refs[a].at[place(item, 3)], xy_recv.at[item[0], 2, a])
                to_core(item, 3, a).start()

        def finish_shared(item):
            for a in arrays:
                for m in direct:
                    to_expert(item, m, a).wait_send()
                relay(item, 3 - relayed(item, a), a).wait_send()
                for m in range(1, along_expert):
                    finish_core(item, m, a)

        def finish_core(item, m, a):
            to_core(item, m, a).wait_send()
            landed(other_refs[a].at[place(item, m)], c_recv.at[item[0], m, a])

        if phase == 0:
            for a in arrays:
                here(a).start()
                for way in ways:

                    @pl.when(exists(d + way))
                    def _():
                        onward(items[0], way, a).start()

                for m in direct:
                    to_expert(items[0], m, a).start()
                to_core(items[0], 0, a).start()
            queue = [items[0]]
            for step in range(along_dp - 1):
                for item in [item for item in items[1:] if item[2] == step]:
                    k = 0 if item[1] > 0 else 1

                    @when(item)
                    def _():
                        for a in arrays:
                            landed(all_refs[a].at[place(item, 0)], z_recv.at[k, step, a])

                    if step < along_dp - 2:

                        @when(item, exists(d + item[1]))
                        def _():
                            for a in arrays:
                                onward(item, item[1], a).start()

                    @when(item)
                    def _():
                        for a in arrays:
                            to_core(item, 0, a).start()

                    if mine(item):
                        when(item, here_now(item))(lambda: share(item))
                for item in queue:
                    when(item, here_now(item))(lambda: gather(item))
                queue = [item for item in items[1:] if item[2] == step and mine(item)]
            for item in queue:
                when(item, here_now(item))(lambda: gather(item))
            for item in items:
                if mine(item):
                    when(item, here_now(item))(lambda: gather_last(item))
            for a in arrays:
                here(a).wait()
            for item in items:
                if mine(item):
                    when(item, here_now(item))(lambda: finish_shared(item))

                @when(item)
                def _():
                    for a in arrays:
                        finish_core(item, 0, a)

                for way in ways if item[1] == 0 else (item[1],):
                    if item[1] == 0 or item[2] < along_dp - 2:

                        @when(item, exists(d + way))
                        def _():
                            for a in arrays:
                                onward(item, way, a).wait_send()
        else:
            rest = [item for item in items if mine(item)]
            for step in (share, gather, gather_last, finish_shared):
                for item in rest:
                    when(item, here_now(item))(lambda: step(item))

    @pl.when(section == 0)
    def _():
        work(layer_refs[0], layer_refs[1])

    @pl.when(section == 1)
    def _():
        work(layer_refs[1], layer_refs[0])


def gather_call(phase, parts, held=()):
    along_dp, along_expert = lax.axis_size("dp"), lax.axis_size("expert")
    total = len(parts) if phase == 0 else len(held) // 2
    given = parts if phase == 0 else held
    items = 2 * along_dp - 1

    def body(*refs):
        outs = refs[len(given) : len(given) + 2 * total]
        gather_kernel(
            phase, along_dp, along_expert, refs[: len(given)], (outs[:total], outs[total:]),
            *refs[len(given) + 2 * total :],
        )

    dma = pltpu.SemaphoreType.DMA
    shapes = [
        jax.ShapeDtypeStruct((along_dp * along_expert,) + part.shape, part.dtype)
        for part in parts
    ]
    return pl.pallas_call(
        body,
        in_specs=[pl.BlockSpec(memory_space=pltpu.HBM)] * len(given),
        out_specs=[pl.BlockSpec(memory_space=pltpu.HBM)] * (2 * total),
        out_shape=shapes * 2
        if phase == 0
        else [jax.ShapeDtypeStruct(part.shape, part.dtype) for part in held],
        input_output_aliases={} if phase == 0 else {k: k for k in range(2 * total)},
        scratch_shapes=[
            dma((total,)),
            dma((2, along_dp - 1, total)),
            dma((2, along_dp - 1, total)),
            dma((items, along_expert - 1, total)),
            dma((items, along_expert - 1, total)),
            dma((items, along_expert, total)),
            dma((items, along_expert, total)),
        ],
        compiler_params=pltpu.CompilerParams(collective_id=phase, has_side_effects=True),
        cost_estimate=pl.CostEstimate(flops=0, bytes_accessed=250 * 2**20, transcendentals=0),
        name="weights_along_dp" if phase == 0 else "weights_across",
    )(*given)


def carry_kernel(count, backward, *refs):
    if backward:
        end_ref, totals_ref, rate_ref, entry_ref, ends_ref, send_sem, recv_sem = refs
        shared = [ends_ref]
    else:
        end_ref, rate_ref, entry_ref, totals_ref, ends_ref, send_sem, recv_sem = refs
        shared = [ends_ref, totals_ref]
    states = rate_ref.shape[0]
    e = lax.axis_index("expert")
    mesh_id = pl.DeviceIdType.MESH

    def peer(m):
        return (lax.axis_index("section"), lax.axis_index("dp"), e ^ m)

    barrier = pltpu.get_barrier_semaphore()
    for m in range(1, count):
        pl.semaphore_signal(barrier, inc=1, device_id=peer(m), device_id_type=mesh_id)
    pl.semaphore_wait(barrier, count - 1)
    ends_ref[e] = end_ref[:states].astype(jnp.bfloat16)
    if not backward:
        totals_ref[e] = jnp.sum(end_ref[states:], axis=0, keepdims=True)

    def copy(m, a):
        return pltpu.make_async_remote_copy(
            src_ref=shared[a].at[e],
            dst_ref=shared[a].at[e],
            send_sem=send_sem.at[m - 1, a],
            recv_sem=recv_sem.at[m - 1, a],
            device_id=peer(m),
            device_id_type=mesh_id,
        )

    for m in range(1, count):
        for a in range(len(shared)):
            copy(m, a).start()
    for m in range(1, count):
        for a in range(len(shared)):
            there = shared[a].at[e ^ m]
            pltpu.make_async_copy(there, there, recv_sem.at[m - 1, a]).wait()
    width = rate_ref.shape[1]
    for start in range(0, width, lanes):
        cols = slice(start, start + lanes)
        state = jnp.zeros((states, lanes), jnp.float32)
        for k in range(count - 1, -1, -1) if backward else range(count):
            reached = jnp.where(k > e if backward else k < e, 1.0, 0.0)
            kept = jnp.exp(rate_ref[:, cols] * totals_ref[k, :, cols])
            new = kept * state + ends_ref[k, :, cols].astype(jnp.float32)
            state = state + reached * (new - state)
        entry_ref[:, cols] = state
    for m in range(1, count):
        for a in range(len(shared)):
            copy(m, a).wait_send()


def carry_call(end, rate, totals=None):
    count = lax.axis_size("expert")
    states, width = rate.shape
    backward = totals is not None
    dma = pltpu.SemaphoreType.DMA
    vmem = pl.BlockSpec(memory_space=pltpu.VMEM)
    operands = (end, totals, rate) if backward else (end, rate)
    total_shape = jax.ShapeDtypeStruct((count, 1, width), jnp.float32)
    out = pl.pallas_call(
        functools.partial(carry_kernel, count, backward),
        in_specs=[vmem] * len(operands),
        out_specs=[vmem] if backward else [vmem, vmem],
        out_shape=[f32(states, width)] + ([] if backward else [total_shape]),
        scratch_shapes=[
            pltpu.VMEM((count, states, width), jnp.bfloat16),
            dma((count - 1, 2)),
            dma((count - 1, 2)),
        ],
        compiler_params=pltpu.CompilerParams(
            collective_id=3 if backward else 2, has_side_effects=True
        ),
        name="adjoint_carry" if backward else "state_carry",
    )(*operands)
    return out


def swap(array):
    return lax.ppermute(array, "section", [(0, 1), (1, 0)])


def pick(first, left, right):
    return jnp.where(first, left, right), jnp.where(first, right, left)


def halves(array, first, axis):
    width = array.shape[axis] // 2
    low = lax.slice_in_dim(array, 0, width, axis=axis)
    high = lax.slice_in_dim(array, width, 2 * width, axis=axis)
    return pick(first, low, high)


def turned(array, axis, hop):
    length = lax.axis_size(axis)
    return lax.ppermute(array, axis, [(i, (i + hop) % length) for i in range(length)])


def crossed(array, axis, mask):
    length = lax.axis_size(axis)
    return lax.ppermute(array, axis, [(i, i ^ mask) for i in range(length)])


def expert_parts(up, down, first):
    pairs = [
        halves(master.astype(jnp.bfloat16), first, axis)
        for axis, master in enumerate((down, up))
    ]
    others = [swap(sent) for _, sent in pairs]
    down, up = [pick(first, own, got) for (own, _), got in zip(pairs, others)]
    return [up[0], down[0], up[1], down[1]]


def expert_spread(up, down):
    return tuple(
        lax.all_gather(part, ("section", "dp"), axis=axis, tiled=True)
        for axis, part in ((1, up), (0, down))
    )


def tie(values, after):
    count = len(values)

    def body(*refs):
        del refs

    return pl.pallas_call(
        body,
        in_specs=[pl.BlockSpec(memory_space=pl.ANY)] * (count + len(after)),
        out_specs=[pl.BlockSpec(memory_space=pl.ANY)] * count,
        out_shape=[jax.ShapeDtypeStruct(value.shape, value.dtype) for value in values],
        input_output_aliases={k: k for k in range(count)},
        name="order",
    )(*values, *after)


class LineSum:
    def __init__(self, up, down):
        self.parts = (up, down)
        self.here, self.count = lax.axis_index("dp"), lax.axis_size("dp")
        self.width = up.shape[0] // self.count
        self.step, self.moving = 0, (None, None)

    def chunk(self, index):
        start = jnp.clip(index, 0, self.count - 1) * self.width
        cuts = [lax.dynamic_slice_in_dim(part, start, self.width, 0) for part in self.parts]
        return jnp.stack(cuts).astype(jnp.float32)

    def advance(self, steps=1):
        for _ in range(steps):
            ahead = self.count - 1 - self.step
            if ahead == 0:
                break
            moved = []
            for way, moving in zip((1, -1), self.moving):
                held = self.chunk(self.here + way * ahead)
                if moving is not None:
                    held = held + moving.astype(jnp.float32)
                pairs = [
                    (i, i + way) for i in range(self.count) if 0 <= i + way * ahead < self.count
                ]
                moved.append(lax.ppermute(held.astype(jnp.bfloat16), "dp", pairs))
            self.moving = tuple(moved)
            self.step += 1
        return self.moving

    def total(self):
        up, down = self.advance(self.count)
        summed = self.chunk(self.here) + up.astype(jnp.float32) + down.astype(jnp.float32)
        return summed.astype(jnp.bfloat16)


def joined(pair, product_of):
    sent = swap(product_of(pair[1]).astype(jnp.bfloat16))
    return (product_of(pair[0]) + sent.astype(jnp.float32)).astype(jnp.bfloat16)


def by_expert(array, split):
    rows, width = array.shape
    across, along = lax.axis_size("dp"), lax.axis_size("expert")
    parts = array.reshape(rows, across, along, split, width // (across * along * split))
    return parts.transpose(0, 3, 2, 1, 4).reshape(rows, width)


def settle(total):
    part = lax.psum_scatter(total, "expert", scatter_dimension=0, tiled=True)
    return lax.psum_scatter(part, "dp", scatter_dimension=0, tiled=True)


def settle_direct(total):
    here, along = lax.axis_index("expert"), lax.axis_size("expert")
    width = total.shape[0] // along

    def chunk(array, index, size):
        return lax.dynamic_slice_in_dim(array, index * size, size, 0)

    summed = chunk(total, here, width).astype(jnp.float32)
    for mask in range(1, along):
        summed = summed + crossed(chunk(total, here ^ mask, width), "expert", mask).astype(
            jnp.float32
        )
    total = summed.astype(jnp.bfloat16)
    here, across = lax.axis_index("dp"), lax.axis_size("dp")
    width = width // across
    summed = chunk(total, here, width).astype(jnp.float32)
    for hop in range(1, across):
        there = lax.rem(here + hop, across)
        summed = summed + turned(chunk(total, there, width), "dp", hop).astype(jnp.float32)
    return summed.astype(jnp.bfloat16)


def hand_back(parts, first, cut):
    own, sent = pick(first, parts[0], parts[1])
    low, high = pick(first, own, swap(sent))
    return jnp.concatenate([low, high], axis=cut).astype(jnp.float32)


def widen(array):
    return jnp.pad(array, ((0, 0), (0, lanes - array.shape[1])))


def pack(select, step, rows, model):
    model = jnp.pad(model, ((0, 0), (0, rows.shape[1] - model.shape[1])))
    thin = jnp.concatenate([rows, model], axis=0).T
    return jnp.stack([widen(select), widen(step), widen(thin)])


def layer_forward(residual, small, big, routing, documents, mark, low_rank):
    conv_part, gate_part, output_weight, up_weight, down_weight = big
    row_count, model_width = residual.shape
    tap_count = small.conv.shape[0]
    states = small.rate.shape[0]
    expert_count = small.router.shape[0]
    capacity = 2 * row_count // expert_count
    normed = norm_scale(residual, small.mixer_gain).astype(jnp.bfloat16)
    conv_in = product(normed, conv_part).astype(jnp.bfloat16)
    gate_in = product(normed, gate_part).astype(jnp.bfloat16)
    rim_rows = from_behind(conv_in[row_count - tap_count + 1 :], "expert", 1)
    wide_in = jnp.concatenate([rim_rows, conv_in], axis=0)
    activated = conv_act(
        wide_in.astype(jnp.float32), small.conv, small.conv_bias, documents
    ).astype(jnp.bfloat16)
    projected = product(activated, small.select)
    step_low = jnp.where(jnp.arange(lanes) < low_rank, projected, 0.0).astype(jnp.bfloat16)
    in_wide = jnp.broadcast_to(
        projected[:, low_rank : low_rank + states, None], (row_count, states, lanes)
    )
    out_wide = jnp.broadcast_to(
        projected[:, low_rank + states : low_rank + 2 * states, None], (row_count, states, lanes)
    )
    step_pre = cross_cols(step_low, small.step) + small.step_bias
    step_size = jax.nn.softplus(step_pre)
    ends = end_call(step_size, activated, mark, in_wide, small.rate)
    entry_state, totals = carry_call(ends, small.rate)
    scanned = scan_call(
        step_size, activated, mark, in_wide, out_wide, small.rate, entry_state, small.skip
    )
    gated_out = gate_product(scanned, gate_in.astype(jnp.float32)).astype(jnp.bfloat16)
    middle = residual + product(gated_out, output_weight)
    normed_two = norm_scale(middle, small.expert_gain).astype(jnp.bfloat16)
    logits = cross_cols(normed_two, small.router)
    probability = jax.nn.softmax(logits, axis=-1)
    chosen = routing[:, None] == jnp.arange(expert_count, dtype=jnp.int32)[None, :]
    gate_value = jnp.sum(jnp.where(chosen, probability, 0.0), axis=1)
    slot_index, token_index = dispatch_tables(chosen, capacity)
    padded = jnp.concatenate([normed_two, jnp.zeros((1, model_width), jnp.bfloat16)], axis=0)
    outgoing = padded[token_index].reshape(expert_count, capacity, model_width)
    arrived = lax.all_to_all(outgoing, "expert", split_axis=0, concat_axis=0, tiled=True)
    flat_rows = arrived.reshape(-1, model_width)
    pre_act = product(flat_rows, up_weight)
    hidden = jax.nn.gelu(pre_act).astype(jnp.bfloat16)
    result = product(hidden, down_weight).astype(jnp.bfloat16).reshape(arrived.shape)
    returned = lax.all_to_all(result, "expert", split_axis=0, concat_axis=0, tiled=True)
    mixture = returned.reshape(-1, model_width)[slot_index].astype(jnp.float32)
    out_residual = middle + gate_value[:, None] * mixture
    stored = SimpleNamespace(
        residual=residual, normed=normed, wide_in=wide_in, gate_in=gate_in, activated=activated,
        step_low=step_low, step_pre=step_pre, step_size=step_size, in_wide=in_wide,
        out_wide=out_wide, totals=totals, entry_state=entry_state, scanned=scanned,
        gated_out=gated_out, middle=middle, normed_two=normed_two, probability=probability,
        chosen=chosen, gate_value=gate_value, slot_index=slot_index, token_index=token_index,
        pre_act=pre_act, hidden=hidden, flat_rows=flat_rows, mixture=mixture,
        documents=documents, mark=mark,
    )
    return out_residual, stored


def layer_backward(grad_out, kept, small, big, section, earlier, pending, ranks):
    conv_part, gate_part, output_weight, up_weight, down_weight = big
    first = section == 0
    row_count, model_width = grad_out.shape
    tap_count = small.conv.shape[0]
    expert_count = small.router.shape[0]
    capacity = 2 * row_count // expert_count
    back_gate = jnp.sum(grad_out * kept.mixture, axis=1)
    back_result = (kept.gate_value[:, None] * grad_out).astype(jnp.bfloat16)
    padded = jnp.concatenate([back_result, jnp.zeros((1, model_width), jnp.bfloat16)], axis=0)
    back_outgoing = padded[kept.token_index].reshape(expert_count, capacity, model_width)
    back_arrived = lax.all_to_all(back_outgoing, "expert", split_axis=0, concat_axis=0, tiled=True)
    back_flat = back_arrived.reshape(-1, model_width)
    back_hidden = cross_cols(back_flat, down_weight)
    back_pre = jax.vjp(jax.nn.gelu, kept.pre_act)[1](back_hidden)[0].astype(jnp.bfloat16)
    back_expert = cross_cols(back_pre, up_weight).astype(jnp.bfloat16).reshape(back_arrived.shape)
    if earlier is not None:
        (back_expert,) = tie([back_expert], earlier.moving)
        earlier.advance()
    back_returned = lax.all_to_all(back_expert, "expert", split_axis=0, concat_axis=0, tiled=True)
    grad_down = joined(halves(kept.hidden, first, 1), lambda half: cross_rows(half, back_flat))
    grad_up = joined(halves(back_pre, first, 1), lambda half: cross_rows(half, kept.flat_rows))
    line = LineSum(grad_up, grad_down)
    line.advance()
    back_tokens = back_returned.reshape(-1, model_width)[kept.slot_index].astype(jnp.float32)
    back_logits = (
        (back_gate * kept.gate_value)[:, None]
        * (kept.chosen.astype(jnp.float32) - kept.probability)
    ).astype(jnp.bfloat16)
    grad_router = cross_rows(back_logits, kept.normed_two)
    back_normed_two = back_tokens + product(back_logits, small.router)
    back_mid_norm, grad_expert_gain = jax.vjp(norm_scale, kept.middle, small.expert_gain)[1](
        back_normed_two
    )
    back_middle = grad_out + back_mid_norm
    back_branch = back_middle.astype(jnp.bfloat16)
    gated_pair = halves(by_expert(kept.gated_out, 2), first, 1)
    grad_output = joined(gated_pair, lambda half: cross_rows(half, back_branch))
    back_gated = cross_cols(back_branch, output_weight)
    back_scanned, back_gate_in = jax.vjp(
        gate_product, kept.scanned, kept.gate_in.astype(jnp.float32)
    )[1](back_gated)
    normed_rows = by_expert(kept.normed, 1)
    back_gate_in = back_gate_in.astype(jnp.bfloat16)
    grad_gate = joined(halves(back_gate_in, first, 1), lambda half: cross_rows(normed_rows, half))
    late = (settle(grad_gate), settle(grad_output))
    (back_scanned,) = tie([back_scanned], (grad_up, grad_down, grad_gate, grad_output))
    rate = small.rate
    back_ends = entry_call(kept.step_size, kept.mark, kept.out_wide, rate, back_scanned)
    (adjoint,) = carry_call(back_ends, rate, kept.totals)
    back_act, back_step, grad_decay, back_in, back_out = back_call(
        kept.step_size, kept.activated, kept.mark, kept.in_wide, kept.out_wide,
        rate, kept.entry_state, adjoint, small.skip, back_scanned,
    )
    (back_step,) = tie(
        [back_step], line.moving + pending + (() if earlier is None else earlier.moving)
    )
    line.advance()
    act_float = kept.activated.astype(jnp.float32)
    grad_skip = jnp.sum(back_scanned * act_float, axis=0, keepdims=True)
    back_step_pre = back_step * jax.nn.sigmoid(kept.step_pre)
    grad_step_bias = jnp.sum(back_step_pre, axis=0, keepdims=True)
    back_step_low = back_step_pre.astype(jnp.bfloat16)
    grad_step = cross_rows(back_step_low, kept.step_low)
    back_rank = product(back_step_low, small.step)
    low_rank = ranks - 2 * rate.shape[0]
    maps = jnp.concatenate([jnp.sum(back_in, axis=2), jnp.sum(back_out, axis=2)], axis=1)
    back_projected = back_rank + jnp.pad(maps, ((0, 0), (low_rank, lanes - ranks)))
    back_projected = back_projected.astype(jnp.bfloat16)
    grad_select = cross_rows(kept.activated, back_projected)
    back_activated = back_act + cross_cols(back_projected, small.select)

    def conv_piece(wide_float, taps_in, bias_in):
        return conv_act(wide_float, taps_in, bias_in, kept.documents)

    back_wide, grad_conv, grad_conv_bias = jax.vjp(
        conv_piece, kept.wide_in.astype(jnp.float32), small.conv, small.conv_bias
    )[1](back_activated)
    rim_back = from_behind(back_wide[: tap_count - 1], "expert", -1)
    back_conv_in = back_wide[tap_count - 1 :] + jnp.pad(
        rim_back, ((row_count - tap_count + 1, 0), (0, 0))
    )
    back_conv_in = back_conv_in.astype(jnp.bfloat16)
    grad_taps_in = joined(halves(back_conv_in, first, 1), lambda half: cross_rows(normed_rows, half))
    back_normed = cross_cols(back_conv_in, conv_part) + cross_cols(back_gate_in, gate_part)
    back_residual_norm, grad_mixer_gain = jax.vjp(
        norm_scale, kept.residual, small.mixer_gain
    )[1](back_normed)
    back_residual = back_middle + back_residual_norm
    lines = jnp.concatenate(
        [grad_conv, grad_decay, grad_conv_bias[None], grad_step_bias, grad_skip], axis=0
    )
    model = jnp.concatenate([grad_mixer_gain[None], grad_expert_gain[None], grad_router], axis=0)
    small_grads = (grad_select, grad_step, lines, model)
    return back_residual, grad_taps_in, late, line, small_grads


def doc_marks(documents, tap_count):
    own = documents[tap_count - 1 :]
    begins = own != documents[tap_count - 2 : -1]
    return jnp.broadcast_to(jnp.where(begins, reset, 0.0)[:, None], (own.shape[0], lanes))


def shards(
    inputs,
    cotangent,
    routes,
    lengths,
    mixer_gain,
    input_weight,
    conv_weight,
    conv_bias,
    select_weight,
    step_weight,
    step_bias,
    decay_log,
    skip_gain,
    output_weight,
    expert_gain,
    router_weight,
    up_weight,
    down_weight,
):
    section = lax.axis_index("section")
    first = section == 0
    count = lax.axis_size("dp") * lax.axis_size("expert")
    row_count, model_width = inputs.shape[1:]
    tap_count = conv_weight.shape[1]
    chan = conv_bias.shape[1]
    low_rank = step_weight.shape[1]
    states = decay_log.shape[2]
    ranks = select_weight.shape[2]
    expert_count = router_weight.shape[2]

    thin = tap_count + states + 3
    packed = pack(
        select_weight[0],
        step_weight[0].T,
        jnp.concatenate(
            [conv_weight[0], decay_log[0].T, conv_bias, step_bias, skip_gain], axis=0
        ),
        jnp.concatenate([mixer_gain, expert_gain, router_weight[0].T], axis=0),
    )
    wide = input_weight.shape[2] // 2
    experts = expert_parts(up_weight[0, 0], down_weight[0, 0], first)
    early = gather_call(
        0,
        (
            packed.astype(jnp.bfloat16),
            input_weight[0, :, :wide].astype(jnp.bfloat16),
            input_weight[0, :, wide:].astype(jnp.bfloat16),
            output_weight[0].astype(jnp.bfloat16),
        ),
    )
    experts = tie(experts, early[:1])
    gathered = gather_call(1, (), early)
    gathered = (gathered[:4], gathered[4:])
    part = model_width // count

    def unpack(layer):
        select, step, rows = [
            gathered[layer][0][:, k].reshape(count * chan, lanes) for k in range(3)
        ]
        rows = rows.T[: thin + 2 + expert_count].astype(jnp.float32)
        model = rows[thin:].reshape(-1, count, chan)[:, :, :part].reshape(-1, model_width)
        return SimpleNamespace(
            select=select, step=step, conv=rows[:tap_count],
            rate=-jnp.exp(rows[tap_count : tap_count + states]),
            conv_bias=rows[thin - 3], step_bias=rows[thin - 2 : thin - 1],
            skip=rows[thin - 1 : thin], mixer_gain=model[0], expert_gain=model[1],
            router=model[2:].astype(jnp.bfloat16),
        )

    small = [unpack(0), unpack(1)]
    experts_two = [expert_spread(*experts[:2]), expert_spread(*experts[2:])]
    big = [
        (
            gathered[k][1].reshape(model_width, wide),
            gathered[k][2].reshape(model_width, wide),
            gathered[k][3].reshape(wide, model_width),
        )
        + experts_two[k]
        for k in range(2)
    ]

    own_routes, sent_routes = pick(first, routes[0, 0, :, 0], routes[0, 1, :, 0])
    routing = pick(first, own_routes, swap(sent_routes))
    lengths_row = lax.dynamic_index_in_dim(lengths[:, 0, :], section, 0, keepdims=False)
    positions = lax.axis_index("expert") * row_count + jnp.arange(
        1 - tap_count, row_count, dtype=jnp.int32
    )
    documents = doc_ids(lengths_row, positions)
    mark = doc_marks(documents, tap_count)

    residual = lax.dynamic_index_in_dim(inputs, section, 0, keepdims=False).astype(jnp.float32)
    outputs_seen = []
    kept = []
    for layer in range(2):
        out_residual, stored = layer_forward(
            residual, small[layer], big[layer], routing[layer], documents, mark, low_rank
        )
        outputs_seen.append(out_residual.astype(jnp.bfloat16))
        residual = outputs_seen[-1].astype(jnp.float32)
        kept.append(stored)

    grad_out = lax.dynamic_index_in_dim(cotangent, section, 0, keepdims=False).astype(jnp.float32)
    input_grads = [None, None]
    settled = [None, None]
    small_sums = [None, None]
    line, pending = None, ()
    for layer in (1, 0):
        earlier = line
        back_residual, grad_taps_in, late, line, small_grads = layer_backward(
            grad_out, kept[layer], small[layer], big[layer], section, earlier, pending, ranks
        )
        input_grads[layer] = back_residual
        grad_out = back_residual.astype(jnp.bfloat16).astype(jnp.float32)
        if layer == 1:
            pending = (settle(grad_taps_in),) + late
        else:
            settled[1] = pending + (earlier.total(),)
            final_late = late + (line.total(),)
        across, along = lax.axis_size("dp"), lax.axis_size("expert")
        grad_select, grad_step, rows, model = small_grads
        model = model.reshape(-1, count, part)
        model = jnp.pad(model, ((0, 0), (0, 0), (0, chan - part))).reshape(-1, count * chan)
        rows = widen(jnp.concatenate([rows, model], axis=0).T)
        whole = jnp.stack(
            [array.reshape(across, along, chan, lanes) for array in (grad_select, grad_step, rows)],
            axis=2,
        ).astype(jnp.bfloat16)
        small_sums[layer] = whole.transpose(1, 0, 2, 3, 4).reshape(count, -1, model_width)

    own_small, sent_small = pick(first, small_sums[0], small_sums[1])
    own_small = own_small.astype(jnp.float32) + swap(sent_small).astype(jnp.float32)
    last = jnp.concatenate(
        [grad_taps_in.reshape(count, part, -1), own_small.astype(jnp.bfloat16)], axis=1
    )
    last = settle_direct(last.reshape(-1, model_width))
    settled[0] = (last[:part],) + final_late
    total = last[part:].reshape(3, chan, lanes).astype(jnp.float32)
    rows = total[2].T
    model = rows[thin : thin + 2 + expert_count, :part]

    def whole_input():
        taps = hand_back((settled[0][0], settled[1][0]), first, 1)
        return jnp.concatenate([taps, hand_back((settled[0][1], settled[1][1]), first, 1)], axis=1)

    experts_back = hand_back((settled[0][3], settled[1][3]), first, 1)
    def both(array):
        mine, sent = pick(first, array[0], array[1])
        return jnp.stack(pick(first, mine, swap(sent)))[None]

    return (
        both(outputs_seen),
        both(input_grads),
        model[:1],
        whole_input()[None],
        rows[:tap_count][None],
        rows[thin - 3 : thin - 2],
        total[0, :, :ranks][None],
        total[1, :, :low_rank].T[None],
        rows[thin - 2 : thin - 1],
        rows[tap_count : tap_count + states].T[None],
        rows[thin - 1 : thin],
        hand_back((settled[0][2], settled[1][2]), first, 0)[None],
        model[1:2],
        model[2:].T[None],
        experts_back[0].T[None, None],
        experts_back[1][None, None],
    )


def solution(mesh):
    return jax.shard_map(
        shards,
        mesh=mesh,
        in_specs=(
            P(None, ("dp", "expert"), None),
            P(None, ("dp", "expert"), None),
            P("section", None, ("dp", "expert"), None),
            P(None, "dp", None),
            P("section", ("dp", "expert")),
            P("section", ("dp", "expert"), None),
            P("section", None, ("dp", "expert")),
            P("section", ("dp", "expert")),
            P("section", ("dp", "expert"), None),
            P("section", None, ("dp", "expert")),
            P("section", ("dp", "expert")),
            P("section", ("dp", "expert"), None),
            P("section", ("dp", "expert")),
            P("section", ("dp", "expert"), None),
            P("section", ("dp", "expert")),
            P("section", ("dp", "expert"), None),
            P("section", "expert", None, "dp"),
            P("section", "expert", "dp", None),
        ),
        out_specs=(
            P("section", None, ("dp", "expert"), None),
            P("section", None, ("dp", "expert"), None),
            P("section", ("dp", "expert")),
            P("section", ("dp", "expert"), None),
            P("section", None, ("dp", "expert")),
            P("section", ("dp", "expert")),
            P("section", ("dp", "expert"), None),
            P("section", None, ("dp", "expert")),
            P("section", ("dp", "expert")),
            P("section", ("dp", "expert"), None),
            P("section", ("dp", "expert")),
            P("section", ("dp", "expert"), None),
            P("section", ("dp", "expert")),
            P("section", ("dp", "expert"), None),
            P("section", "expert", None, "dp"),
            P("section", "expert", "dp", None),
        ),
        check_vma=False,
    )
```

```python
import functools
from types import SimpleNamespace

import jax
import jax.numpy as jnp
from jax import lax
from jax.experimental import pallas as pl
from jax.experimental.pallas import tpu as pltpu
from jax.sharding import PartitionSpec as P

epsilon = 1e-05
lanes = 128
group = 8
reset = 1e30
fold_order = (3, 7, 5, 1, 4, 0, 6, 2)


def row_of(tile, index, states):
    return jnp.broadcast_to(tile[index : index + 1, :], (states, tile.shape[1]))


def fold(parts, shift, rows):
    count = len(parts)
    if count == 1:
        return parts[0]
    span = group // count
    left = fold(parts[: count // 2], shift, rows)
    right = fold(parts[count // 2 :], shift + (span if count > 2 else 0), rows)
    mask = ((rows - shift) & span) != 0
    if count == 2:
        mask = jnp.logical_not(mask)
    return jnp.where(mask, left, right) + pltpu.roll(jnp.where(mask, right, left), span, 0)


def state_sums(parts):
    rows = lax.broadcasted_iota(jnp.int32, (group, lanes), 0)
    halved = [part[:group] + part[group:] for part in parts]
    return fold([halved[k] for k in fold_order], 0, rows)


def end_kernel(step_ref, act_ref, start_ref, in_ref, rate_ref, end_ref):
    rows, width = step_ref.shape
    states = rate_ref.shape[0]
    tiles = width // lanes
    cols = [slice(j * lanes, (j + 1) * lanes) for j in range(tiles)]

    def body(g, carry):
        state, total = carry
        at = pl.ds(pl.multiple_of(g * group, group), group)
        state = list(state)
        total = list(total)
        begin = start_ref[at, :]
        for j in range(tiles):
            step = step_ref[at, cols[j]]
            drive = step * act_ref[at, cols[j]].astype(jnp.float32)
            fall = step + begin
            total[j] = total[j] + fall
            rate = rate_ref[:, cols[j]]
            for i in range(group):
                decay = jnp.exp(row_of(fall, i, states) * rate)
                state[j] = decay * state[j] + row_of(drive, i, states) * in_ref[g * group + i]
        return tuple(state), tuple(total)

    zero = tuple(jnp.zeros((states, lanes), jnp.float32) for _ in range(tiles))
    none = tuple(jnp.zeros((group, lanes), jnp.float32) for _ in range(tiles))
    state, total = lax.fori_loop(0, rows // group, body, (zero, none))
    for j in range(tiles):
        end_ref[:states, cols[j]] = state[j]
        end_ref[states:, cols[j]] = total[j]


def scan_kernel(step_ref, act_ref, start_ref, in_ref, out_ref, rate_ref, entry_ref, skip_ref, y_ref):
    rows, width = step_ref.shape
    states = rate_ref.shape[0]
    tiles = width // lanes
    cols = [slice(j * lanes, (j + 1) * lanes) for j in range(tiles)]

    def body(g, state):
        at = pl.ds(pl.multiple_of(g * group, group), group)
        state = list(state)
        begin = start_ref[at, :]
        for j in range(tiles):
            step = step_ref[at, cols[j]]
            act = act_ref[at, cols[j]].astype(jnp.float32)
            drive = step * act
            fall = step + begin
            rate = rate_ref[:, cols[j]]
            parts = []
            for i in range(group):
                decay = jnp.exp(row_of(fall, i, states) * rate)
                state[j] = decay * state[j] + row_of(drive, i, states) * in_ref[g * group + i]
                parts.append(state[j] * out_ref[g * group + i])
            y_ref[at, cols[j]] = skip_ref[:, cols[j]] * act + state_sums(parts)
        return tuple(state)

    lax.fori_loop(
        0, rows // group, body, tuple(entry_ref[:, cols[j]] for j in range(tiles))
    )


def entry_kernel(step_ref, start_ref, out_ref, rate_ref, grad_ref, end_ref):
    rows, width = step_ref.shape
    states = rate_ref.shape[0]
    tiles = width // lanes
    cols = [slice(j * lanes, (j + 1) * lanes) for j in range(tiles)]
    groups = rows // group

    def body(k, state):
        g = groups - 1 - k
        at = pl.ds(pl.multiple_of(g * group, group), group)
        state = list(state)
        begin = start_ref[at, :]
        for j in range(tiles):
            fall = step_ref[at, cols[j]] + begin
            grad = grad_ref[at, cols[j]]
            rate = rate_ref[:, cols[j]]
            for i in reversed(range(group)):
                decay = jnp.exp(row_of(fall, i, states) * rate)
                state[j] = decay * (state[j] + row_of(grad, i, states) * out_ref[g * group + i])
        return tuple(state)

    zero = tuple(jnp.zeros((states, lanes), jnp.float32) for _ in range(tiles))
    state = lax.fori_loop(0, groups, body, zero)
    for j in range(tiles):
        end_ref[:, cols[j]] = state[j]


def back_kernel(
    step_ref, act_ref, start_ref, in_ref, out_ref, rate_ref, entry_ref, adj_ref, skip_ref, grad_ref,
    back_act_ref, back_step_ref, back_rate_ref, back_in_ref, back_out_ref, kept, decays,
):
    rows, width = step_ref.shape
    states = rate_ref.shape[0]
    tiles = width // lanes
    cols = [slice(j * lanes, (j + 1) * lanes) for j in range(tiles)]
    groups = rows // group

    @pl.when(pl.program_id(0) == 0)
    def _():
        back_in_ref[...] = jnp.zeros_like(back_in_ref)
        back_out_ref[...] = jnp.zeros_like(back_out_ref)

    for j in range(tiles):
        kept[0, :, cols[j]] = entry_ref[:, cols[j]]

    def ahead(g, state):
        at = pl.ds(pl.multiple_of(g * group, group), group)
        state = list(state)
        begin = start_ref[at, :]
        for j in range(tiles):
            step = step_ref[at, cols[j]]
            drive = step * act_ref[at, cols[j]].astype(jnp.float32)
            fall = step + begin
            rate = rate_ref[:, cols[j]]
            for i in range(group):
                decay = jnp.exp(row_of(fall, i, states) * rate)
                decays[g * group + i, :, cols[j]] = decay
                state[j] = decay * state[j] + row_of(drive, i, states) * in_ref[g * group + i]
                kept[g * group + i + 1, :, cols[j]] = state[j]
        return tuple(state)

    lax.fori_loop(0, groups, ahead, tuple(entry_ref[:, cols[j]] for j in range(tiles)))

    def behind(k, carry):
        flow, slope = carry
        g = groups - 1 - k
        at = pl.ds(pl.multiple_of(g * group, group), group)
        flow = list(flow)
        slope = list(slope)
        back_in = [back_in_ref[g * group + i] for i in range(group)]
        back_out = [back_out_ref[g * group + i] for i in range(group)]
        for j in range(tiles):
            step = step_ref[at, cols[j]]
            act = act_ref[at, cols[j]].astype(jnp.float32)
            drive = step * act
            grad = grad_ref[at, cols[j]]
            rate = rate_ref[:, cols[j]]
            drives, falls = [], []
            for i in reversed(range(group)):
                t = g * group + i
                grad_row = row_of(grad, i, states)
                adj = flow[j] + grad_row * out_ref[t]
                back_out[i] = back_out[i] + kept[t + 1, :, cols[j]] * grad_row
                back_in[i] = back_in[i] + adj * row_of(drive, i, states)
                drives.insert(0, adj * in_ref[t])
                flow[j] = adj * decays[t, :, cols[j]]
                turn = flow[j] * kept[t, :, cols[j]]
                falls.insert(0, turn * rate)
                slope[j] = slope[j] + row_of(step, i, states) * turn
            back_drive, back_fall = state_sums(drives), state_sums(falls)
            back_act_ref[at, cols[j]] = step * back_drive + skip_ref[:, cols[j]] * grad
            back_step_ref[at, cols[j]] = act * back_drive + back_fall
        for i in range(group):
            back_in_ref[g * group + i] = back_in[i]
            back_out_ref[g * group + i] = back_out[i]
        return tuple(flow), tuple(slope)

    zero = tuple(jnp.zeros((states, lanes), jnp.float32) for _ in range(tiles))
    _, slope = lax.fori_loop(
        0, groups, behind, (tuple(adj_ref[:, cols[j]] for j in range(tiles)), zero)
    )
    for j in range(tiles):
        back_rate_ref[:, cols[j]] = slope[j] * rate_ref[:, cols[j]]


def specs(rows, states, block):
    wide = pl.BlockSpec((rows, block), lambda c: (0, c))
    mark = pl.BlockSpec((rows, lanes), lambda c: (0, 0))
    maps = pl.BlockSpec((rows, states, lanes), lambda c: (0, 0, 0))
    held = pl.BlockSpec((states, block), lambda c: (0, c))
    line = pl.BlockSpec((1, block), lambda c: (0, c))
    total = pl.BlockSpec((states + group, block), lambda c: (0, c))
    return wide, mark, maps, held, line, total


def params(mib):
    return pltpu.CompilerParams(
        dimension_semantics=("arbitrary",), vmem_limit_bytes=mib * 1024 * 1024
    )


def block_of(width, most):
    best = lanes
    for tiles in range(1, most // lanes + 1):
        if width % (tiles * lanes) == 0:
            best = tiles * lanes
    return best


def f32(*shape):
    return jax.ShapeDtypeStruct(shape, jnp.float32)


def end_call(step, act, start, in_map, rate, block=None):
    rows, width = step.shape
    states = rate.shape[0]
    block = block or block_of(width, 768)
    wide, mark, maps, held, line, total = specs(rows, states, block)
    return pl.pallas_call(
        end_kernel,
        grid=(width // block,),
        in_specs=[wide, wide, mark, maps, held],
        out_specs=total,
        out_shape=f32(states + group, width),
        compiler_params=params(40),
        cost_estimate=pl.CostEstimate(flops=8 * rows * states * width, bytes_accessed=6 * rows * width, transcendentals=rows * states * width),
        name="state_end",
    )(step, act, start, in_map, rate)


def scan_call(step, act, start, in_map, out_map, rate, entry, skip, block=None):
    rows, width = step.shape
    states = rate.shape[0]
    block = block or block_of(width, 768)
    wide, mark, maps, held, line, total = specs(rows, states, block)
    return pl.pallas_call(
        scan_kernel,
        grid=(width // block,),
        in_specs=[wide, wide, mark, maps, maps, held, held, line],
        out_specs=wide,
        out_shape=f32(rows, width),
        compiler_params=params(40),
        cost_estimate=pl.CostEstimate(flops=12 * rows * states * width, bytes_accessed=10 * rows * width, transcendentals=rows * states * width),
        name="state_scan",
    )(step, act, start, in_map, out_map, rate, entry, skip)


def entry_call(step, start, out_map, rate, grad, block=None):
    rows, width = step.shape
    states = rate.shape[0]
    block = block or block_of(width, 768)
    wide, mark, maps, held, line, total = specs(rows, states, block)
    return pl.pallas_call(
        entry_kernel,
        grid=(width // block,),
        in_specs=[wide, mark, maps, held, wide],
        out_specs=held,
        out_shape=f32(states, width),
        compiler_params=params(40),
        cost_estimate=pl.CostEstimate(flops=8 * rows * states * width, bytes_accessed=8 * rows * width, transcendentals=rows * states * width),
        name="adjoint_entry",
    )(step, start, out_map, rate, grad)


def back_call(step, act, start, in_map, out_map, rate, entry, adj, skip, grad, block=None):
    rows, width = step.shape
    states = rate.shape[0]
    block = block or block_of(width, 768)
    wide, mark, maps, held, line, total = specs(rows, states, block)
    return pl.pallas_call(
        back_kernel,
        grid=(width // block,),
        in_specs=[wide, wide, mark, maps, maps, held, held, held, line, wide],
        out_specs=[wide, wide, held, maps, maps],
        out_shape=[
            f32(rows, width), f32(rows, width), f32(states, width),
            f32(rows, states, lanes), f32(rows, states, lanes),
        ],
        scratch_shapes=[
            pltpu.VMEM((rows + 1, states, block), jnp.float32),
            pltpu.VMEM((rows, states, block), jnp.float32),
        ],
        compiler_params=params(56),
        cost_estimate=pl.CostEstimate(flops=40 * rows * states * width, bytes_accessed=20 * rows * width, transcendentals=rows * states * width),
        name="scan_back",
    )(step, act, start, in_map, out_map, rate, entry, adj, skip, grad)


def from_behind(array, axis, by):
    length = lax.axis_size(axis)
    pairs = [(i, i + by) for i in range(length) if 0 <= i + by < length]
    return lax.ppermute(array, axis, pairs)


def norm_scale(residual, gain):
    return (
        residual * lax.rsqrt(jnp.mean(residual * residual, axis=-1, keepdims=True) + epsilon) * gain
    )


def product(left, right):
    return jnp.dot(left, right, preferred_element_type=jnp.float32)


def cross_rows(left, right):
    return lax.dot_general(
        left, right, (((0,), (0,)), ((), ())), preferred_element_type=jnp.float32
    )


def cross_cols(left, right):
    return lax.dot_general(
        left, right, (((1,), (1,)), ((), ())), preferred_element_type=jnp.float32
    )


def gate_product(values, gates):
    return values * jax.nn.silu(gates)


def doc_ids(lengths_row, positions):
    boundaries = jnp.cumsum(lengths_row, dtype=jnp.int32)
    counted = jnp.sum(
        (positions[:, None] >= boundaries[None, :]).astype(jnp.int32), axis=1, dtype=jnp.int32
    )
    return jnp.where(positions < 0, -1, counted)


def conv_act(wide_in, taps_weight, taps_bias, documents):
    tap_count = taps_weight.shape[0]
    row_count = wide_in.shape[0] - tap_count + 1
    own_docs = documents[tap_count - 1 :]
    summed = taps_bias + taps_weight[tap_count - 1] * wide_in[tap_count - 1 :]
    for offset in range(1, tap_count):
        start_row = tap_count - 1 - offset
        lagged = wide_in[start_row : start_row + row_count]
        same_doc = (documents[start_row : start_row + row_count] == own_docs)[:, None]
        summed = summed + taps_weight[start_row] * jnp.where(same_doc, lagged, 0.0)
    return jax.nn.silu(summed)


def dispatch_tables(chosen, capacity):
    indicator = chosen.astype(jnp.int32)
    row_count, expert_count = indicator.shape
    earlier_rows = jnp.cumsum(indicator, axis=0, dtype=jnp.int32) - indicator
    slot_rank = jnp.sum(earlier_rows * indicator, axis=1, dtype=jnp.int32)
    expert_of = jnp.sum(
        indicator * jnp.arange(expert_count, dtype=jnp.int32)[None, :], axis=1, dtype=jnp.int32
    )
    slot_index = expert_of * capacity + slot_rank
    all_slots = jnp.arange(expert_count * capacity, dtype=jnp.int32)
    matches = slot_index[None, :] == all_slots[:, None]
    token_index = jnp.sum(
        jnp.where(matches, jnp.arange(row_count, dtype=jnp.int32)[None, :], 0),
        axis=1,
        dtype=jnp.int32,
    )
    token_index = token_index + row_count * (1 - jnp.any(matches, axis=1).astype(jnp.int32))
    return (slot_index, token_index)


def gather_kernel(
    phase, along_dp, along_expert, own_refs, layer_refs,
    here_sem, z_send, z_recv, xy_send, xy_recv, c_send, c_recv,
):
    section = lax.axis_index("section")
    d = lax.axis_index("dp")
    e = lax.axis_index("expert")
    arrays = range(len(layer_refs[0]))
    mesh_id = pl.DeviceIdType.MESH
    ways = (1, -1)
    direct = [m for m in range(1, along_expert) if m != 3]

    def exists(index):
        return jnp.logical_and(index >= 0, index < along_dp)

    barrier = pltpu.get_barrier_semaphore()
    peers = [(section, d, e ^ m) for m in range(1, along_expert)] + [(1 - section, d, e)]
    for peer in peers:
        pl.semaphore_signal(barrier, inc=1, device_id=peer, device_id_type=mesh_id)
    expected = len(peers)
    if phase == 0:
        for way in ways:

            @pl.when(exists(d + way))
            def _():
                pl.semaphore_signal(
                    barrier, inc=1, device_id=(section, d + way, e), device_id_type=mesh_id
                )

        expected = expected + jnp.where(d > 0, 1, 0) + jnp.where(d < along_dp - 1, 1, 0)
    pl.semaphore_wait(barrier, expected)

    items = [(0, 0, 0)] + [
        (1 + 2 * step + (way < 0), way, step) for step in range(along_dp - 1) for way in ways
    ]

    def origin(item):
        index, way, step = item
        return d - way * (step + 1) if way else d

    def mine(item):
        if item[1] == 0:
            return phase == 0
        if item[2] > 0:
            return phase == 1
        return True if item[1] < 0 else phase == 0

    def here_now(item):
        if item[1] < 0 and item[2] == 0:
            return (d == 0) if phase == 0 else (d > 0)
        return d >= 0

    def when(item, *more):
        if item[1] == 0 and not more:
            return lambda work: work()
        alive = exists(origin(item))
        for other in more:
            alive = jnp.logical_and(alive, other)
        return pl.when(alive)

    def work(all_refs, other_refs):
        def place(item, m):
            return origin(item) * along_expert + (e ^ m)

        def copy(item, m, a, peer, send, recv):
            held = all_refs[a].at[place(item, m)]
            own = phase == 0 and item[1] == 0 and m == 0
            return pltpu.make_async_remote_copy(
                src_ref=own_refs[a] if own else held,
                dst_ref=held,
                send_sem=send,
                recv_sem=recv,
                device_id=peer,
                device_id_type=mesh_id,
            )

        def onward(item, way, a):
            step = item[2] + 1 if item[1] else 0
            k = 0 if way > 0 else 1
            peer = (section, d + way, e)
            return copy(item, 0, a, peer, z_send.at[k, step, a], z_recv.at[k, step, a])

        def to_expert(item, m, a):
            peer = (section, d, e ^ m)
            sems = (xy_send.at[item[0], m - 1, a], xy_recv.at[item[0], m - 1, a])
            return copy(item, 0, a, peer, *sems)

        def relayed(item, a):
            return 1 + (a + (item[2] + 1 if a == arrays[-1] else 0)) % 2

        def relay(item, m, a):
            peer = (section, d, e ^ 3 ^ m)
            sems = (xy_send.at[item[0], 2, a], xy_recv.at[item[0], 2, a])
            return copy(item, m, a, peer, *sems)

        def to_core(item, m, a):
            peer = (1 - section, d, e)
            return copy(item, m, a, peer, c_send.at[item[0], m, a], c_recv.at[item[0], m, a])

        def landed(ref, sem):
            pltpu.make_async_copy(ref, ref, sem).wait()

        def here(a):
            return pltpu.make_async_copy(
                own_refs[a], all_refs[a].at[place(items[0], 0)], here_sem.at[a]
            )

        def share(item):
            for a in arrays:
                for m in direct:
                    to_expert(item, m, a).start()

        def gather(item):
            for m in direct:
                for a in arrays:
                    landed(all_refs[a].at[place(item, m)], xy_recv.at[item[0], m - 1, a])
                    if m < 3 and relayed(item, a) == 3 - m:
                        relay(item, m, a).start()
                    to_core(item, m, a).start()

        def gather_last(item):
            for a in arrays:
                landed(all_refs[a].at[place(item, 3)], xy_recv.at[item[0], 2, a])
                to_core(item, 3, a).start()

        def finish_shared(item):
            for a in arrays:
                for m in direct:
                    to_expert(item, m, a).wait_send()
                relay(item, 3 - relayed(item, a), a).wait_send()
                for m in range(1, along_expert):
                    finish_core(item, m, a)

        def finish_core(item, m, a):
            to_core(item, m, a).wait_send()
            landed(other_refs[a].at[place(item, m)], c_recv.at[item[0], m, a])

        if phase == 0:
            for a in arrays:
                here(a).start()
                for way in ways:

                    @pl.when(exists(d + way))
                    def _():
                        onward(items[0], way, a).start()

                for m in direct:
                    to_expert(items[0], m, a).start()
                to_core(items[0], 0, a).start()
            queue = [items[0]]
            for step in range(along_dp - 1):
                for item in [item for item in items[1:] if item[2] == step]:
                    k = 0 if item[1] > 0 else 1

                    @when(item)
                    def _():
                        for a in arrays:
                            landed(all_refs[a].at[place(item, 0)], z_recv.at[k, step, a])

                    if step < along_dp - 2:

                        @when(item, exists(d + item[1]))
                        def _():
                            for a in arrays:
                                onward(item, item[1], a).start()

                    @when(item)
                    def _():
                        for a in arrays:
                            to_core(item, 0, a).start()

                    if mine(item):
                        when(item, here_now(item))(lambda: share(item))
                for item in queue:
                    when(item, here_now(item))(lambda: gather(item))
                queue = [item for item in items[1:] if item[2] == step and mine(item)]
            for item in queue:
                when(item, here_now(item))(lambda: gather(item))
            for item in items:
                if mine(item):
                    when(item, here_now(item))(lambda: gather_last(item))
            for a in arrays:
                here(a).wait()
            for item in items:
                if mine(item):
                    when(item, here_now(item))(lambda: finish_shared(item))

                @when(item)
                def _():
                    for a in arrays:
                        finish_core(item, 0, a)

                for way in ways if item[1] == 0 else (item[1],):
                    if item[1] == 0 or item[2] < along_dp - 2:

                        @when(item, exists(d + way))
                        def _():
                            for a in arrays:
                                onward(item, way, a).wait_send()
        else:
            rest = [item for item in items if mine(item)]
            for step in (share, gather, gather_last, finish_shared):
                for item in rest:
                    when(item, here_now(item))(lambda: step(item))

    @pl.when(section == 0)
    def _():
        work(layer_refs[0], layer_refs[1])

    @pl.when(section == 1)
    def _():
        work(layer_refs[1], layer_refs[0])


def gather_call(phase, parts, held=()):
    along_dp, along_expert = lax.axis_size("dp"), lax.axis_size("expert")
    total = len(parts) if phase == 0 else len(held) // 2
    given = parts if phase == 0 else held
    items = 2 * along_dp - 1

    def body(*refs):
        outs = refs[len(given) : len(given) + 2 * total]
        gather_kernel(
            phase, along_dp, along_expert, refs[: len(given)], (outs[:total], outs[total:]),
            *refs[len(given) + 2 * total :],
        )

    dma = pltpu.SemaphoreType.DMA
    shapes = [
        jax.ShapeDtypeStruct((along_dp * along_expert,) + part.shape, part.dtype)
        for part in parts
    ]
    return pl.pallas_call(
        body,
        in_specs=[pl.BlockSpec(memory_space=pltpu.HBM)] * len(given),
        out_specs=[pl.BlockSpec(memory_space=pltpu.HBM)] * (2 * total),
        out_shape=shapes * 2
        if phase == 0
        else [jax.ShapeDtypeStruct(part.shape, part.dtype) for part in held],
        input_output_aliases={} if phase == 0 else {k: k for k in range(2 * total)},
        scratch_shapes=[
            dma((total,)),
            dma((2, along_dp - 1, total)),
            dma((2, along_dp - 1, total)),
            dma((items, along_expert - 1, total)),
            dma((items, along_expert - 1, total)),
            dma((items, along_expert, total)),
            dma((items, along_expert, total)),
        ],
        compiler_params=pltpu.CompilerParams(collective_id=phase, has_side_effects=True),
        cost_estimate=pl.CostEstimate(flops=0, bytes_accessed=250 * 2**20, transcendentals=0),
        name="weights_along_dp" if phase == 0 else "weights_across",
    )(*given)


def carry_kernel(count, backward, *refs):
    if backward:
        end_ref, totals_ref, rate_ref, entry_ref, ends_ref, send_sem, recv_sem = refs
        shared = [ends_ref]
    else:
        end_ref, rate_ref, entry_ref, totals_ref, ends_ref, send_sem, recv_sem = refs
        shared = [ends_ref, totals_ref]
    states = rate_ref.shape[0]
    e = lax.axis_index("expert")
    mesh_id = pl.DeviceIdType.MESH

    def peer(m):
        return (lax.axis_index("section"), lax.axis_index("dp"), e ^ m)

    barrier = pltpu.get_barrier_semaphore()
    for m in range(1, count):
        pl.semaphore_signal(barrier, inc=1, device_id=peer(m), device_id_type=mesh_id)
    pl.semaphore_wait(barrier, count - 1)
    ends_ref[e] = end_ref[:states].astype(jnp.bfloat16)
    if not backward:
        totals_ref[e] = jnp.sum(end_ref[states:], axis=0, keepdims=True)

    def copy(m, a):
        return pltpu.make_async_remote_copy(
            src_ref=shared[a].at[e],
            dst_ref=shared[a].at[e],
            send_sem=send_sem.at[m - 1, a],
            recv_sem=recv_sem.at[m - 1, a],
            device_id=peer(m),
            device_id_type=mesh_id,
        )

    for m in range(1, count):
        for a in range(len(shared)):
            copy(m, a).start()
    for m in range(1, count):
        for a in range(len(shared)):
            there = shared[a].at[e ^ m]
            pltpu.make_async_copy(there, there, recv_sem.at[m - 1, a]).wait()
    width = rate_ref.shape[1]
    for start in range(0, width, lanes):
        cols = slice(start, start + lanes)
        state = jnp.zeros((states, lanes), jnp.float32)
        for k in range(count - 1, -1, -1) if backward else range(count):
            reached = jnp.where(k > e if backward else k < e, 1.0, 0.0)
            kept = jnp.exp(rate_ref[:, cols] * totals_ref[k, :, cols])
            new = kept * state + ends_ref[k, :, cols].astype(jnp.float32)
            state = state + reached * (new - state)
        entry_ref[:, cols] = state
    for m in range(1, count):
        for a in range(len(shared)):
            copy(m, a).wait_send()


def carry_call(end, rate, totals=None):
    count = lax.axis_size("expert")
    states, width = rate.shape
    backward = totals is not None
    dma = pltpu.SemaphoreType.DMA
    vmem = pl.BlockSpec(memory_space=pltpu.VMEM)
    operands = (end, totals, rate) if backward else (end, rate)
    total_shape = jax.ShapeDtypeStruct((count, 1, width), jnp.float32)
    out = pl.pallas_call(
        functools.partial(carry_kernel, count, backward),
        in_specs=[vmem] * len(operands),
        out_specs=[vmem] if backward else [vmem, vmem],
        out_shape=[f32(states, width)] + ([] if backward else [total_shape]),
        scratch_shapes=[
            pltpu.VMEM((count, states, width), jnp.bfloat16),
            dma((count - 1, 2)),
            dma((count - 1, 2)),
        ],
        compiler_params=pltpu.CompilerParams(
            collective_id=3 if backward else 2, has_side_effects=True
        ),
        name="adjoint_carry" if backward else "state_carry",
    )(*operands)
    return out


def swap(array):
    return lax.ppermute(array, "section", [(0, 1), (1, 0)])


def pick(first, left, right):
    return jnp.where(first, left, right), jnp.where(first, right, left)


def halves(array, first, axis):
    width = array.shape[axis] // 2
    low = lax.slice_in_dim(array, 0, width, axis=axis)
    high = lax.slice_in_dim(array, width, 2 * width, axis=axis)
    return pick(first, low, high)


def turned(array, axis, hop):
    length = lax.axis_size(axis)
    return lax.ppermute(array, axis, [(i, (i + hop) % length) for i in range(length)])


def crossed(array, axis, mask):
    length = lax.axis_size(axis)
    return lax.ppermute(array, axis, [(i, i ^ mask) for i in range(length)])


def expert_parts(up, down, first):
    pairs = [
        halves(master.astype(jnp.bfloat16), first, axis)
        for axis, master in enumerate((down, up))
    ]
    others = [swap(sent) for _, sent in pairs]
    down, up = [pick(first, own, got) for (own, _), got in zip(pairs, others)]
    return [up[0], down[0], up[1], down[1]]


def expert_spread(up, down):
    return tuple(
        lax.all_gather(part, ("section", "dp"), axis=axis, tiled=True)
        for axis, part in ((1, up), (0, down))
    )


def tie(values, after):
    count = len(values)

    def body(*refs):
        del refs

    return pl.pallas_call(
        body,
        in_specs=[pl.BlockSpec(memory_space=pl.ANY)] * (count + len(after)),
        out_specs=[pl.BlockSpec(memory_space=pl.ANY)] * count,
        out_shape=[jax.ShapeDtypeStruct(value.shape, value.dtype) for value in values],
        input_output_aliases={k: k for k in range(count)},
        name="order",
    )(*values, *after)


class LineSum:
    def __init__(self, up, down):
        self.parts = (up, down)
        self.here, self.count = lax.axis_index("dp"), lax.axis_size("dp")
        self.width = up.shape[0] // self.count
        self.step, self.moving = 0, (None, None)

    def chunk(self, index):
        start = jnp.clip(index, 0, self.count - 1) * self.width
        cuts = [lax.dynamic_slice_in_dim(part, start, self.width, 0) for part in self.parts]
        return jnp.stack(cuts).astype(jnp.float32)

    def advance(self, steps=1):
        for _ in range(steps):
            ahead = self.count - 1 - self.step
            if ahead == 0:
                break
            moved = []
            for way, moving in zip((1, -1), self.moving):
                held = self.chunk(self.here + way * ahead)
                if moving is not None:
                    held = held + moving.astype(jnp.float32)
                pairs = [
                    (i, i + way) for i in range(self.count) if 0 <= i + way * ahead < self.count
                ]
                moved.append(lax.ppermute(held.astype(jnp.bfloat16), "dp", pairs))
            self.moving = tuple(moved)
            self.step += 1
        return self.moving

    def total(self):
        up, down = self.advance(self.count)
        summed = self.chunk(self.here) + up.astype(jnp.float32) + down.astype(jnp.float32)
        return summed.astype(jnp.bfloat16)


def joined(pair, product_of):
    sent = swap(product_of(pair[1]).astype(jnp.bfloat16))
    return (product_of(pair[0]) + sent.astype(jnp.float32)).astype(jnp.bfloat16)


def by_expert(array, split):
    rows, width = array.shape
    across, along = lax.axis_size("dp"), lax.axis_size("expert")
    parts = array.reshape(rows, across, along, split, width // (across * along * split))
    return parts.transpose(0, 3, 2, 1, 4).reshape(rows, width)


def settle_expert(total):
    return lax.psum_scatter(total, "expert", scatter_dimension=0, tiled=True)


def settle_dp(total):
    return lax.psum_scatter(total, "dp", scatter_dimension=0, tiled=True)


def settle_direct(total):
    here, along = lax.axis_index("expert"), lax.axis_size("expert")
    width = total.shape[0] // along

    def chunk(array, index, size):
        return lax.dynamic_slice_in_dim(array, index * size, size, 0)

    summed = chunk(total, here, width).astype(jnp.float32)
    for mask in range(1, along):
        summed = summed + crossed(chunk(total, here ^ mask, width), "expert", mask).astype(
            jnp.float32
        )
    total = summed.astype(jnp.bfloat16)
    here, across = lax.axis_index("dp"), lax.axis_size("dp")
    width = width // across
    summed = chunk(total, here, width).astype(jnp.float32)
    for hop in range(1, across):
        there = lax.rem(here + hop, across)
        summed = summed + turned(chunk(total, there, width), "dp", hop).astype(jnp.float32)
    return summed.astype(jnp.bfloat16)


def hand_back(parts, first, cut):
    own, sent = pick(first, parts[0], parts[1])
    low, high = pick(first, own, swap(sent))
    return jnp.concatenate([low, high], axis=cut).astype(jnp.float32)


def widen(array):
    return jnp.pad(array, ((0, 0), (0, lanes - array.shape[1])))


def piled(parts):
    total, at = None, 0
    rows = sum(part.shape[0] for part in parts)
    for part in parts:
        padded = jnp.pad(part, ((at, rows - at - part.shape[0]), (0, 0)))
        total = padded if total is None else total + padded
        at += part.shape[0]
    return total


def pack(select, step, rows, model):
    model = jnp.pad(model, ((0, 0), (0, rows[0].shape[1] - model.shape[1])))
    thin = piled(rows + [model]).T
    return jnp.concatenate([widen(select), widen(step), widen(thin)], axis=1)


def layer_forward(residual, small, big, routing, documents, mark, low_rank):
    conv_part, gate_part, output_weight, up_weight, down_weight = big
    row_count, model_width = residual.shape
    tap_count = small.conv.shape[0]
    states = small.rate.shape[0]
    expert_count = small.router.shape[0]
    capacity = 2 * row_count // expert_count
    normed = norm_scale(residual, small.mixer_gain).astype(jnp.bfloat16)
    conv_in = product(normed, conv_part).astype(jnp.bfloat16)
    gate_in = product(normed, gate_part).astype(jnp.bfloat16)
    rim_rows = from_behind(conv_in[row_count - tap_count + 1 :], "expert", 1)
    wide_in = jnp.concatenate([rim_rows, conv_in], axis=0)
    activated = conv_act(
        wide_in.astype(jnp.float32), small.conv, small.conv_bias, documents
    ).astype(jnp.bfloat16)
    projected = product(activated, small.select)
    step_low = jnp.where(jnp.arange(lanes) < low_rank, projected, 0.0).astype(jnp.bfloat16)
    in_wide = jnp.broadcast_to(
        projected[:, low_rank : low_rank + states, None], (row_count, states, lanes)
    )
    out_wide = jnp.broadcast_to(
        projected[:, low_rank + states : low_rank + 2 * states, None], (row_count, states, lanes)
    )
    step_pre = cross_cols(step_low, small.step) + small.step_bias
    step_size = jax.nn.softplus(step_pre)
    ends = end_call(step_size, activated, mark, in_wide, small.rate)
    entry_state, totals = carry_call(ends, small.rate)
    scanned = scan_call(
        step_size, activated, mark, in_wide, out_wide, small.rate, entry_state, small.skip
    )
    gated_out = gate_product(scanned, gate_in.astype(jnp.float32)).astype(jnp.bfloat16)
    middle = residual + product(gated_out, output_weight)
    normed_two = norm_scale(middle, small.expert_gain).astype(jnp.bfloat16)
    logits = cross_cols(normed_two, small.router)
    probability = jax.nn.softmax(logits, axis=-1)
    chosen = routing[:, None] == jnp.arange(expert_count, dtype=jnp.int32)[None, :]
    gate_value = jnp.sum(jnp.where(chosen, probability, 0.0), axis=1)
    slot_index, token_index = dispatch_tables(chosen, capacity)
    padded = jnp.concatenate([normed_two, jnp.zeros((1, model_width), jnp.bfloat16)], axis=0)
    outgoing = padded[token_index].reshape(expert_count, capacity, model_width)
    arrived = lax.all_to_all(outgoing, "expert", split_axis=0, concat_axis=0, tiled=True)
    flat_rows = arrived.reshape(-1, model_width)
    pre_act = product(flat_rows, up_weight)
    hidden = jax.nn.gelu(pre_act).astype(jnp.bfloat16)
    result = product(hidden, down_weight).astype(jnp.bfloat16).reshape(arrived.shape)
    returned = lax.all_to_all(result, "expert", split_axis=0, concat_axis=0, tiled=True)
    mixture = returned.reshape(-1, model_width)[slot_index].astype(jnp.float32)
    out_residual = middle + gate_value[:, None] * mixture
    stored = SimpleNamespace(
        residual=residual, normed=normed, wide_in=wide_in, gate_in=gate_in, activated=activated,
        step_low=step_low, step_pre=step_pre, step_size=step_size, in_wide=in_wide,
        out_wide=out_wide, totals=totals, entry_state=entry_state, scanned=scanned,
        gated_out=gated_out, middle=middle, normed_two=normed_two, probability=probability,
        chosen=chosen, gate_value=gate_value, slot_index=slot_index, token_index=token_index,
        pre_act=pre_act, hidden=hidden, flat_rows=flat_rows, mixture=mixture,
        documents=documents, mark=mark,
    )
    return out_residual, stored


def layer_backward(grad_out, kept, small, big, section, earlier, pending, ranks):
    conv_part, gate_part, output_weight, up_weight, down_weight = big
    first = section == 0
    row_count, model_width = grad_out.shape
    tap_count = small.conv.shape[0]
    expert_count = small.router.shape[0]
    capacity = 2 * row_count // expert_count
    back_gate = jnp.sum(grad_out * kept.mixture, axis=1)
    back_result = (kept.gate_value[:, None] * grad_out).astype(jnp.bfloat16)
    padded = jnp.concatenate([back_result, jnp.zeros((1, model_width), jnp.bfloat16)], axis=0)
    back_outgoing = padded[kept.token_index].reshape(expert_count, capacity, model_width)
    back_arrived = lax.all_to_all(back_outgoing, "expert", split_axis=0, concat_axis=0, tiled=True)
    back_flat = back_arrived.reshape(-1, model_width)
    back_hidden = cross_cols(back_flat, down_weight)
    back_pre = jax.vjp(jax.nn.gelu, kept.pre_act)[1](back_hidden)[0].astype(jnp.bfloat16)
    back_expert = cross_cols(back_pre, up_weight).astype(jnp.bfloat16).reshape(back_arrived.shape)
    if earlier is not None:
        back_expert, *earlier.moving = tie([back_expert, *earlier.moving], ())
        earlier.advance()
    back_returned = lax.all_to_all(back_expert, "expert", split_axis=0, concat_axis=0, tiled=True)
    grad_down = joined(halves(kept.hidden, first, 1), lambda half: cross_rows(half, back_flat))
    grad_up = joined(halves(back_pre, first, 1), lambda half: cross_rows(half, kept.flat_rows))
    line = LineSum(grad_up, grad_down)
    line.advance()
    back_tokens = back_returned.reshape(-1, model_width)[kept.slot_index].astype(jnp.float32)
    back_logits = (
        (back_gate * kept.gate_value)[:, None]
        * (kept.chosen.astype(jnp.float32) - kept.probability)
    ).astype(jnp.bfloat16)
    grad_router = cross_rows(back_logits, kept.normed_two)
    back_normed_two = back_tokens + product(back_logits, small.router)
    back_mid_norm, grad_expert_gain = jax.vjp(norm_scale, kept.middle, small.expert_gain)[1](
        back_normed_two
    )
    back_middle = grad_out + back_mid_norm
    back_branch = back_middle.astype(jnp.bfloat16)
    gated_pair = halves(by_expert(kept.gated_out, 2), first, 1)
    grad_output = joined(gated_pair, lambda half: cross_rows(half, back_branch))
    back_gated = cross_cols(back_branch, output_weight)
    back_scanned, back_gate_in = jax.vjp(
        gate_product, kept.scanned, kept.gate_in.astype(jnp.float32)
    )[1](back_gated)
    normed_rows = by_expert(kept.normed, 1)
    part_rows = model_width // (lax.axis_size("dp") * lax.axis_size("expert"))
    back_gate_in = back_gate_in.astype(jnp.bfloat16)
    grad_gate = joined(halves(back_gate_in, first, 1), lambda half: cross_rows(normed_rows, half))
    together = [part.reshape(-1, part_rows, model_width) for part in (grad_gate, grad_output)]
    together = jnp.stack(together, axis=1).reshape(-1, model_width)
    late = settle_expert(together)
    ready = (grad_up, grad_down, together)
    if earlier is None:
        (back_scanned,) = tie([back_scanned], ready)
    else:
        back_scanned, *earlier.moving = tie([back_scanned, *earlier.moving], ready)
    rate = small.rate
    back_ends = entry_call(kept.step_size, kept.mark, kept.out_wide, rate, back_scanned)
    (adjoint,) = carry_call(back_ends, rate, kept.totals)
    back_act, back_step, grad_decay, back_in, back_out = back_call(
        kept.step_size, kept.activated, kept.mark, kept.in_wide, kept.out_wide,
        rate, kept.entry_state, adjoint, small.skip, back_scanned,
    )
    back_step, *line.moving = tie([back_step, *line.moving], pending)
    line.advance()
    act_float = kept.activated.astype(jnp.float32)
    grad_skip = jnp.sum(back_scanned * act_float, axis=0, keepdims=True)
    back_step_pre = back_step * jax.nn.sigmoid(kept.step_pre)
    grad_step_bias = jnp.sum(back_step_pre, axis=0, keepdims=True)
    back_step_low = back_step_pre.astype(jnp.bfloat16)
    grad_step = cross_rows(back_step_low, kept.step_low)
    back_rank = product(back_step_low, small.step)
    low_rank = ranks - 2 * rate.shape[0]
    maps = jnp.concatenate([jnp.sum(back_in, axis=2), jnp.sum(back_out, axis=2)], axis=1)
    back_projected = back_rank + jnp.pad(maps, ((0, 0), (low_rank, lanes - ranks)))
    back_projected = back_projected.astype(jnp.bfloat16)
    grad_select = cross_rows(kept.activated, back_projected)
    back_activated = back_act + cross_cols(back_projected, small.select)

    def conv_piece(wide_float, taps_in, bias_in):
        return conv_act(wide_float, taps_in, bias_in, kept.documents)

    back_wide, grad_conv, grad_conv_bias = jax.vjp(
        conv_piece, kept.wide_in.astype(jnp.float32), small.conv, small.conv_bias
    )[1](back_activated)
    rim_back = from_behind(back_wide[: tap_count - 1], "expert", -1)
    back_conv_in = back_wide[tap_count - 1 :] + jnp.pad(
        rim_back, ((row_count - tap_count + 1, 0), (0, 0))
    )
    back_conv_in = back_conv_in.astype(jnp.bfloat16)
    grad_taps_in = joined(halves(back_conv_in, first, 1), lambda half: cross_rows(normed_rows, half))
    back_normed = cross_cols(back_conv_in, conv_part) + cross_cols(back_gate_in, gate_part)
    back_residual_norm, grad_mixer_gain = jax.vjp(
        norm_scale, kept.residual, small.mixer_gain
    )[1](back_normed)
    back_residual = back_middle + back_residual_norm
    lines = piled([grad_conv, grad_decay, grad_conv_bias[None], grad_step_bias, grad_skip])
    model = piled([grad_mixer_gain[None], grad_expert_gain[None], grad_router])
    small_grads = (grad_select, grad_step, lines, model)
    if earlier is not None:
        small_grads = tie(list(small_grads), (grad_taps_in,))
    return back_residual, grad_taps_in, late, line, small_grads


def small_outputs(total, taps, states, ranks, low_rank, expert_count, part):
    chan = total.shape[1]
    thin = taps + states + 3

    def body(total_ref, *outs):
        mixer, conv, conv_bias, select, step, step_bias, decay, skip, expert, router = outs
        down = lax.broadcasted_iota(jnp.int32, (lanes, lanes), 0)
        right = lax.broadcasted_iota(jnp.int32, (lanes, lanes), 1)
        same = jnp.where(down == right, 1.0, 0.0).astype(jnp.bfloat16)
        rows = cross_cols(same, total_ref[2])
        select[0] = total_ref[0].astype(jnp.float32)[:, :ranks]
        step[0] = cross_cols(same, total_ref[1])[:low_rank]
        conv[0] = rows[:taps]
        decay[0] = total_ref[2].astype(jnp.float32)[:, taps : taps + states]
        for ref, at in ((conv_bias, thin - 3), (step_bias, thin - 2), (skip, thin - 1)):
            ref[...] = rows[at : at + 1]
        mixer[...] = rows[thin : thin + 1, :part]
        expert[...] = rows[thin + 1 : thin + 2, :part]
        whole = total_ref[2].astype(jnp.float32)
        router[0] = whole[:part, thin + 2 : thin + 2 + expert_count]

    line = f32(1, chan)
    return pl.pallas_call(
        body,
        out_shape=[
            f32(1, part), f32(1, taps, chan), line, f32(1, chan, ranks), f32(1, low_rank, chan),
            line, f32(1, chan, states), line, f32(1, part), f32(1, part, expert_count),
        ],
        name="small_outputs",
    )(total)


def doc_marks(documents, tap_count):
    own = documents[tap_count - 1 :]
    begins = own != documents[tap_count - 2 : -1]
    return jnp.broadcast_to(jnp.where(begins, reset, 0.0)[:, None], (own.shape[0], lanes))


def shards(
    inputs,
    cotangent,
    routes,
    lengths,
    mixer_gain,
    input_weight,
    conv_weight,
    conv_bias,
    select_weight,
    step_weight,
    step_bias,
    decay_log,
    skip_gain,
    output_weight,
    expert_gain,
    router_weight,
    up_weight,
    down_weight,
):
    section = lax.axis_index("section")
    first = section == 0
    count = lax.axis_size("dp") * lax.axis_size("expert")
    row_count, model_width = inputs.shape[1:]
    tap_count = conv_weight.shape[1]
    chan = conv_bias.shape[1]
    low_rank = step_weight.shape[1]
    states = decay_log.shape[2]
    ranks = select_weight.shape[2]
    expert_count = router_weight.shape[2]

    thin = tap_count + states + 3
    packed = pack(
        select_weight[0],
        step_weight[0].T,
        [conv_weight[0], decay_log[0].T, conv_bias, step_bias, skip_gain],
        piled([mixer_gain, expert_gain, router_weight[0].T]),
    )
    wide = input_weight.shape[2] // 2
    experts = expert_parts(up_weight[0, 0], down_weight[0, 0], first)
    early = gather_call(
        0,
        (
            packed.astype(jnp.bfloat16),
            input_weight[0, :, :wide].astype(jnp.bfloat16),
            input_weight[0, :, wide:].astype(jnp.bfloat16),
            output_weight[0].astype(jnp.bfloat16),
        ),
    )
    experts = tie(experts, early[:1])
    gathered = gather_call(1, (), early)
    gathered = (gathered[:4], gathered[4:])
    part = model_width // count

    def unpack(layer):
        whole = gathered[layer][0].reshape(count * chan, 3 * lanes)
        select, step, rows = [whole[:, k * lanes : (k + 1) * lanes] for k in range(3)]
        rows = rows.T[: thin + 2 + expert_count].astype(jnp.float32)
        model = rows[thin:].reshape(-1, count, chan)[:, :, :part].reshape(-1, model_width)
        return SimpleNamespace(
            select=select, step=step, conv=rows[:tap_count],
            rate=-jnp.exp(rows[tap_count : tap_count + states]),
            conv_bias=rows[thin - 3], step_bias=rows[thin - 2 : thin - 1],
            skip=rows[thin - 1 : thin], mixer_gain=model[0], expert_gain=model[1],
            router=model[2:].astype(jnp.bfloat16),
        )

    small = [unpack(0), unpack(1)]
    experts_two = [expert_spread(*experts[:2]), expert_spread(*experts[2:])]
    big = [
        (
            gathered[k][1].reshape(model_width, wide),
            gathered[k][2].reshape(model_width, wide),
            gathered[k][3].reshape(wide, model_width),
        )
        + experts_two[k]
        for k in range(2)
    ]

    own_routes, sent_routes = pick(first, routes[0, 0, :, 0], routes[0, 1, :, 0])
    routing = pick(first, own_routes, swap(sent_routes))
    lengths_row = lax.dynamic_index_in_dim(lengths[:, 0, :], section, 0, keepdims=False)
    positions = lax.axis_index("expert") * row_count + jnp.arange(
        1 - tap_count, row_count, dtype=jnp.int32
    )
    documents = doc_ids(lengths_row, positions)
    mark = doc_marks(documents, tap_count)

    residual = lax.dynamic_index_in_dim(inputs, section, 0, keepdims=False).astype(jnp.float32)
    outputs_seen = []
    kept = []
    for layer in range(2):
        out_residual, stored = layer_forward(
            residual, small[layer], big[layer], routing[layer], documents, mark, low_rank
        )
        outputs_seen.append(out_residual.astype(jnp.bfloat16))
        residual = outputs_seen[-1].astype(jnp.float32)
        kept.append(stored)

    grad_out = lax.dynamic_index_in_dim(cotangent, section, 0, keepdims=False).astype(jnp.float32)
    input_grads = [None, None]
    settled = [None, None]
    small_sums = [None, None]
    line, pending = None, ()
    for layer in (1, 0):
        earlier = line
        back_residual, grad_taps_in, late, line, small_grads = layer_backward(
            grad_out, kept[layer], small[layer], big[layer], section, earlier, pending, ranks
        )
        input_grads[layer] = back_residual
        grad_out = back_residual.astype(jnp.bfloat16).astype(jnp.float32)
        if layer == 1:
            pending = (settle_dp(settle_expert(grad_taps_in)), settle_dp(late))
        else:
            settled[1] = pending + (earlier.total(),)
            final_late = (settle_dp(late), line.total())
        across, along = lax.axis_size("dp"), lax.axis_size("expert")
        grad_select, grad_step, rows, model = small_grads
        model = model.reshape(-1, count, part)
        model = jnp.pad(model, ((0, 0), (0, 0), (0, chan - part))).reshape(-1, count * chan)
        rows = widen(piled([rows, model]).T)
        whole = jnp.stack(
            [
                array.astype(jnp.bfloat16).reshape(across, along, chan, lanes)
                for array in (grad_select, grad_step, rows)
            ],
            axis=2,
        )
        small_sums[layer] = whole.transpose(1, 0, 2, 3, 4).reshape(-1, lanes)

    own_small, sent_small = pick(first, small_sums[0], small_sums[1])
    own_small = own_small.astype(jnp.float32) + swap(sent_small).astype(jnp.float32)
    total = settle_direct(own_small.astype(jnp.bfloat16))
    small_out = small_outputs(
        total.reshape(3, chan, lanes), tap_count, states, ranks, low_rank, expert_count, part
    )
    settled[0] = (settle_direct(grad_taps_in),) + final_late
    both_late = [(late_one[1][:part], late_one[1][part:]) for late_one in settled]

    def whole_input():
        taps = hand_back((settled[0][0], settled[1][0]), first, 1)
        return jnp.concatenate([taps, hand_back([pair[0] for pair in both_late], first, 1)], axis=1)

    experts_back = hand_back((settled[0][2], settled[1][2]), first, 1)
    def both(array):
        mine, sent = pick(first, array[0], array[1])
        return jnp.stack(pick(first, mine, swap(sent)))[None]

    return (
        both(outputs_seen),
        both(input_grads),
        small_out[0],
        whole_input()[None],
        *small_out[1:8],
        hand_back([pair[1] for pair in both_late], first, 0)[None],
        *small_out[8:],
        experts_back[0].T[None, None],
        experts_back[1][None, None],
    )


def solution(mesh):
    return jax.shard_map(
        shards,
        mesh=mesh,
        in_specs=(
            P(None, ("dp", "expert"), None),
            P(None, ("dp", "expert"), None),
            P("section", None, ("dp", "expert"), None),
            P(None, "dp", None),
            P("section", ("dp", "expert")),
            P("section", ("dp", "expert"), None),
            P("section", None, ("dp", "expert")),
            P("section", ("dp", "expert")),
            P("section", ("dp", "expert"), None),
            P("section", None, ("dp", "expert")),
            P("section", ("dp", "expert")),
            P("section", ("dp", "expert"), None),
            P("section", ("dp", "expert")),
            P("section", ("dp", "expert"), None),
            P("section", ("dp", "expert")),
            P("section", ("dp", "expert"), None),
            P("section", "expert", None, "dp"),
            P("section", "expert", "dp", None),
        ),
        out_specs=(
            P("section", None, ("dp", "expert"), None),
            P("section", None, ("dp", "expert"), None),
            P("section", ("dp", "expert")),
            P("section", ("dp", "expert"), None),
            P("section", None, ("dp", "expert")),
            P("section", ("dp", "expert")),
            P("section", ("dp", "expert"), None),
            P("section", None, ("dp", "expert")),
            P("section", ("dp", "expert")),
            P("section", ("dp", "expert"), None),
            P("section", ("dp", "expert")),
            P("section", ("dp", "expert"), None),
            P("section", ("dp", "expert")),
            P("section", ("dp", "expert"), None),
            P("section", "expert", None, "dp"),
            P("section", "expert", "dp", None),
        ),
        check_vma=False,
    )
```

```python
import functools
from types import SimpleNamespace

import jax
import jax.numpy as jnp
from jax import lax
from jax.experimental import pallas as pl
from jax.experimental.pallas import tpu as pltpu
from jax.sharding import PartitionSpec as P

epsilon = 1e-05
lanes = 128
group = 8
reset = 1e30
fold_order = (3, 7, 5, 1, 4, 0, 6, 2)


def row_of(tile, index, states):
    return jnp.broadcast_to(tile[index : index + 1, :], (states, tile.shape[1]))


def fold(parts, shift, rows):
    count = len(parts)
    if count == 1:
        return parts[0]
    span = group // count
    left = fold(parts[: count // 2], shift, rows)
    right = fold(parts[count // 2 :], shift + (span if count > 2 else 0), rows)
    mask = ((rows - shift) & span) != 0
    if count == 2:
        mask = jnp.logical_not(mask)
    return jnp.where(mask, left, right) + pltpu.roll(jnp.where(mask, right, left), span, 0)


def state_sums(parts):
    rows = lax.broadcasted_iota(jnp.int32, (group, lanes), 0)
    halved = [part[:group] + part[group:] for part in parts]
    return fold([halved[k] for k in fold_order], 0, rows)


def end_kernel(step_ref, act_ref, start_ref, in_ref, rate_ref, end_ref):
    rows, width = step_ref.shape
    states = rate_ref.shape[0]
    tiles = width // lanes
    cols = [slice(j * lanes, (j + 1) * lanes) for j in range(tiles)]

    def body(g, carry):
        state, total = carry
        at = pl.ds(pl.multiple_of(g * group, group), group)
        state = list(state)
        total = list(total)
        begin = start_ref[at, :]
        for j in range(tiles):
            step = step_ref[at, cols[j]]
            drive = step * act_ref[at, cols[j]].astype(jnp.float32)
            fall = step + begin
            total[j] = total[j] + fall
            rate = rate_ref[:, cols[j]]
            for i in range(group):
                decay = jnp.exp(row_of(fall, i, states) * rate)
                state[j] = decay * state[j] + row_of(drive, i, states) * in_ref[g * group + i]
        return tuple(state), tuple(total)

    zero = tuple(jnp.zeros((states, lanes), jnp.float32) for _ in range(tiles))
    none = tuple(jnp.zeros((group, lanes), jnp.float32) for _ in range(tiles))
    state, total = lax.fori_loop(0, rows // group, body, (zero, none))
    for j in range(tiles):
        end_ref[:states, cols[j]] = state[j]
        end_ref[states:, cols[j]] = total[j]


def scan_kernel(step_ref, act_ref, start_ref, in_ref, out_ref, rate_ref, entry_ref, skip_ref, y_ref):
    rows, width = step_ref.shape
    states = rate_ref.shape[0]
    tiles = width // lanes
    cols = [slice(j * lanes, (j + 1) * lanes) for j in range(tiles)]

    def body(g, state):
        at = pl.ds(pl.multiple_of(g * group, group), group)
        state = list(state)
        begin = start_ref[at, :]
        for j in range(tiles):
            step = step_ref[at, cols[j]]
            act = act_ref[at, cols[j]].astype(jnp.float32)
            drive = step * act
            fall = step + begin
            rate = rate_ref[:, cols[j]]
            parts = []
            for i in range(group):
                decay = jnp.exp(row_of(fall, i, states) * rate)
                state[j] = decay * state[j] + row_of(drive, i, states) * in_ref[g * group + i]
                parts.append(state[j] * out_ref[g * group + i])
            y_ref[at, cols[j]] = skip_ref[:, cols[j]] * act + state_sums(parts)
        return tuple(state)

    lax.fori_loop(
        0, rows // group, body, tuple(entry_ref[:, cols[j]] for j in range(tiles))
    )


def entry_kernel(step_ref, start_ref, out_ref, rate_ref, grad_ref, end_ref):
    rows, width = step_ref.shape
    states = rate_ref.shape[0]
    tiles = width // lanes
    cols = [slice(j * lanes, (j + 1) * lanes) for j in range(tiles)]
    groups = rows // group

    def body(k, state):
        g = groups - 1 - k
        at = pl.ds(pl.multiple_of(g * group, group), group)
        state = list(state)
        begin = start_ref[at, :]
        for j in range(tiles):
            fall = step_ref[at, cols[j]] + begin
            grad = grad_ref[at, cols[j]]
            rate = rate_ref[:, cols[j]]
            for i in reversed(range(group)):
                decay = jnp.exp(row_of(fall, i, states) * rate)
                state[j] = decay * (state[j] + row_of(grad, i, states) * out_ref[g * group + i])
        return tuple(state)

    zero = tuple(jnp.zeros((states, lanes), jnp.float32) for _ in range(tiles))
    state = lax.fori_loop(0, groups, body, zero)
    for j in range(tiles):
        end_ref[:, cols[j]] = state[j]


def back_kernel(
    step_ref, act_ref, start_ref, in_ref, out_ref, rate_ref, entry_ref, adj_ref, skip_ref, grad_ref,
    back_act_ref, back_step_ref, back_rate_ref, back_in_ref, back_out_ref, kept, decays,
):
    rows, width = step_ref.shape
    states = rate_ref.shape[0]
    tiles = width // lanes
    cols = [slice(j * lanes, (j + 1) * lanes) for j in range(tiles)]
    groups = rows // group

    @pl.when(pl.program_id(0) == 0)
    def _():
        back_in_ref[...] = jnp.zeros_like(back_in_ref)
        back_out_ref[...] = jnp.zeros_like(back_out_ref)

    for j in range(tiles):
        kept[0, :, cols[j]] = entry_ref[:, cols[j]]

    def ahead(g, state):
        at = pl.ds(pl.multiple_of(g * group, group), group)
        state = list(state)
        begin = start_ref[at, :]
        for j in range(tiles):
            step = step_ref[at, cols[j]]
            drive = step * act_ref[at, cols[j]].astype(jnp.float32)
            fall = step + begin
            rate = rate_ref[:, cols[j]]
            for i in range(group):
                decay = jnp.exp(row_of(fall, i, states) * rate)
                decays[g * group + i, :, cols[j]] = decay
                state[j] = decay * state[j] + row_of(drive, i, states) * in_ref[g * group + i]
                kept[g * group + i + 1, :, cols[j]] = state[j]
        return tuple(state)

    lax.fori_loop(0, groups, ahead, tuple(entry_ref[:, cols[j]] for j in range(tiles)))

    def behind(k, carry):
        flow, slope = carry
        g = groups - 1 - k
        at = pl.ds(pl.multiple_of(g * group, group), group)
        flow = list(flow)
        slope = list(slope)
        back_in = [back_in_ref[g * group + i] for i in range(group)]
        back_out = [back_out_ref[g * group + i] for i in range(group)]
        for j in range(tiles):
            step = step_ref[at, cols[j]]
            act = act_ref[at, cols[j]].astype(jnp.float32)
            drive = step * act
            grad = grad_ref[at, cols[j]]
            rate = rate_ref[:, cols[j]]
            drives, falls = [], []
            for i in reversed(range(group)):
                t = g * group + i
                grad_row = row_of(grad, i, states)
                adj = flow[j] + grad_row * out_ref[t]
                back_out[i] = back_out[i] + kept[t + 1, :, cols[j]] * grad_row
                back_in[i] = back_in[i] + adj * row_of(drive, i, states)
                drives.insert(0, adj * in_ref[t])
                flow[j] = adj * decays[t, :, cols[j]]
                turn = flow[j] * kept[t, :, cols[j]]
                falls.insert(0, turn * rate)
                slope[j] = slope[j] + row_of(step, i, states) * turn
            back_drive, back_fall = state_sums(drives), state_sums(falls)
            back_act_ref[at, cols[j]] = step * back_drive + skip_ref[:, cols[j]] * grad
            back_step_ref[at, cols[j]] = act * back_drive + back_fall
        for i in range(group):
            back_in_ref[g * group + i] = back_in[i]
            back_out_ref[g * group + i] = back_out[i]
        return tuple(flow), tuple(slope)

    zero = tuple(jnp.zeros((states, lanes), jnp.float32) for _ in range(tiles))
    _, slope = lax.fori_loop(
        0, groups, behind, (tuple(adj_ref[:, cols[j]] for j in range(tiles)), zero)
    )
    for j in range(tiles):
        back_rate_ref[:, cols[j]] = slope[j] * rate_ref[:, cols[j]]


def specs(rows, states, block):
    wide = pl.BlockSpec((rows, block), lambda c: (0, c))
    mark = pl.BlockSpec((rows, lanes), lambda c: (0, 0))
    maps = pl.BlockSpec((rows, states, lanes), lambda c: (0, 0, 0))
    held = pl.BlockSpec((states, block), lambda c: (0, c))
    line = pl.BlockSpec((1, block), lambda c: (0, c))
    total = pl.BlockSpec((states + group, block), lambda c: (0, c))
    return wide, mark, maps, held, line, total


def params(mib):
    return pltpu.CompilerParams(
        dimension_semantics=("arbitrary",), vmem_limit_bytes=mib * 1024 * 1024
    )


def block_of(width, most):
    best = lanes
    for tiles in range(1, most // lanes + 1):
        if width % (tiles * lanes) == 0:
            best = tiles * lanes
    return best


def f32(*shape):
    return jax.ShapeDtypeStruct(shape, jnp.float32)


def end_call(step, act, start, in_map, rate, block=None):
    rows, width = step.shape
    states = rate.shape[0]
    block = block or block_of(width, 768)
    wide, mark, maps, held, line, total = specs(rows, states, block)
    return pl.pallas_call(
        end_kernel,
        grid=(width // block,),
        in_specs=[wide, wide, mark, maps, held],
        out_specs=total,
        out_shape=f32(states + group, width),
        compiler_params=params(40),
        cost_estimate=pl.CostEstimate(flops=8 * rows * states * width, bytes_accessed=6 * rows * width, transcendentals=rows * states * width),
        name="state_end",
    )(step, act, start, in_map, rate)


def scan_call(step, act, start, in_map, out_map, rate, entry, skip, block=None):
    rows, width = step.shape
    states = rate.shape[0]
    block = block or block_of(width, 768)
    wide, mark, maps, held, line, total = specs(rows, states, block)
    return pl.pallas_call(
        scan_kernel,
        grid=(width // block,),
        in_specs=[wide, wide, mark, maps, maps, held, held, line],
        out_specs=wide,
        out_shape=f32(rows, width),
        compiler_params=params(40),
        cost_estimate=pl.CostEstimate(flops=12 * rows * states * width, bytes_accessed=10 * rows * width, transcendentals=rows * states * width),
        name="state_scan",
    )(step, act, start, in_map, out_map, rate, entry, skip)


def entry_call(step, start, out_map, rate, grad, block=None):
    rows, width = step.shape
    states = rate.shape[0]
    block = block or block_of(width, 768)
    wide, mark, maps, held, line, total = specs(rows, states, block)
    return pl.pallas_call(
        entry_kernel,
        grid=(width // block,),
        in_specs=[wide, mark, maps, held, wide],
        out_specs=held,
        out_shape=f32(states, width),
        compiler_params=params(40),
        cost_estimate=pl.CostEstimate(flops=8 * rows * states * width, bytes_accessed=8 * rows * width, transcendentals=rows * states * width),
        name="adjoint_entry",
    )(step, start, out_map, rate, grad)


def back_call(step, act, start, in_map, out_map, rate, entry, adj, skip, grad, block=None):
    rows, width = step.shape
    states = rate.shape[0]
    block = block or block_of(width, 768)
    wide, mark, maps, held, line, total = specs(rows, states, block)
    return pl.pallas_call(
        back_kernel,
        grid=(width // block,),
        in_specs=[wide, wide, mark, maps, maps, held, held, held, line, wide],
        out_specs=[wide, wide, held, maps, maps],
        out_shape=[
            f32(rows, width), f32(rows, width), f32(states, width),
            f32(rows, states, lanes), f32(rows, states, lanes),
        ],
        scratch_shapes=[
            pltpu.VMEM((rows + 1, states, block), jnp.float32),
            pltpu.VMEM((rows, states, block), jnp.float32),
        ],
        compiler_params=params(56),
        cost_estimate=pl.CostEstimate(flops=40 * rows * states * width, bytes_accessed=20 * rows * width, transcendentals=rows * states * width),
        name="scan_back",
    )(step, act, start, in_map, out_map, rate, entry, adj, skip, grad)


def from_behind(array, axis, by):
    length = lax.axis_size(axis)
    pairs = [(i, i + by) for i in range(length) if 0 <= i + by < length]
    return lax.ppermute(array, axis, pairs)


def norm_scale(residual, gain):
    return (
        residual * lax.rsqrt(jnp.mean(residual * residual, axis=-1, keepdims=True) + epsilon) * gain
    )


def product(left, right):
    return jnp.dot(left, right, preferred_element_type=jnp.float32)


def cross_rows(left, right):
    return lax.dot_general(
        left, right, (((0,), (0,)), ((), ())), preferred_element_type=jnp.float32
    )


def cross_cols(left, right):
    return lax.dot_general(
        left, right, (((1,), (1,)), ((), ())), preferred_element_type=jnp.float32
    )


def gate_product(values, gates):
    return values * jax.nn.silu(gates)


def doc_ids(lengths_row, positions):
    boundaries = jnp.cumsum(lengths_row, dtype=jnp.int32)
    counted = jnp.sum(
        (positions[:, None] >= boundaries[None, :]).astype(jnp.int32), axis=1, dtype=jnp.int32
    )
    return jnp.where(positions < 0, -1, counted)


def conv_act(wide_in, taps_weight, taps_bias, documents):
    tap_count = taps_weight.shape[0]
    row_count = wide_in.shape[0] - tap_count + 1
    own_docs = documents[tap_count - 1 :]
    summed = taps_bias + taps_weight[tap_count - 1] * wide_in[tap_count - 1 :]
    for offset in range(1, tap_count):
        start_row = tap_count - 1 - offset
        lagged = wide_in[start_row : start_row + row_count]
        same_doc = (documents[start_row : start_row + row_count] == own_docs)[:, None]
        summed = summed + taps_weight[start_row] * jnp.where(same_doc, lagged, 0.0)
    return jax.nn.silu(summed)


def dispatch_tables(chosen, capacity):
    indicator = chosen.astype(jnp.int32)
    row_count, expert_count = indicator.shape
    earlier_rows = jnp.cumsum(indicator, axis=0, dtype=jnp.int32) - indicator
    slot_rank = jnp.sum(earlier_rows * indicator, axis=1, dtype=jnp.int32)
    expert_of = jnp.sum(
        indicator * jnp.arange(expert_count, dtype=jnp.int32)[None, :], axis=1, dtype=jnp.int32
    )
    slot_index = expert_of * capacity + slot_rank
    all_slots = jnp.arange(expert_count * capacity, dtype=jnp.int32)
    matches = slot_index[None, :] == all_slots[:, None]
    token_index = jnp.sum(
        jnp.where(matches, jnp.arange(row_count, dtype=jnp.int32)[None, :], 0),
        axis=1,
        dtype=jnp.int32,
    )
    token_index = token_index + row_count * (1 - jnp.any(matches, axis=1).astype(jnp.int32))
    return (slot_index, token_index)


def rows_rows(left, right):
    return lax.dot_general(
        left, right, (((0,), (0,)), ((), ())), preferred_element_type=jnp.float32
    )


def expert_kernel(x_ref, up_ref, down_ref, pre_ref, hidden_ref, out_ref, total):
    step = pl.program_id(0)
    pre = product(x_ref[...], up_ref[...])
    pre_ref[...] = pre
    hidden = jax.nn.gelu(pre).astype(jnp.bfloat16)
    hidden_ref[...] = hidden
    part = product(hidden, down_ref[...])

    @pl.when(step == 0)
    def _():
        total[...] = part

    @pl.when(step > 0)
    def _():
        total[...] += part

    @pl.when(step == pl.num_programs(0) - 1)
    def _():
        out_ref[...] = total[...].astype(jnp.bfloat16)


def expert_back_kernel(back_ref, up_ref, down_ref, pre_ref, back_pre_ref, out_ref, total):
    step = pl.program_id(0)
    back_hidden = cross_cols(back_ref[...], down_ref[...])
    back_pre = jax.vjp(jax.nn.gelu, pre_ref[...])[1](back_hidden)[0].astype(jnp.bfloat16)
    back_pre_ref[...] = back_pre
    part = cross_cols(back_pre, up_ref[...])

    @pl.when(step == 0)
    def _():
        total[...] = part

    @pl.when(step > 0)
    def _():
        total[...] += part

    @pl.when(step == pl.num_programs(0) - 1)
    def _():
        out_ref[...] = total[...].astype(jnp.bfloat16)


def expert_call(rows_in, up, down, pre=None):
    rows, width = rows_in.shape
    hidden_width = up.shape[1]
    block = 512
    fixed = pl.BlockSpec((rows, width), lambda i: (0, 0))
    wide = pl.BlockSpec((rows, block), lambda i: (0, i))
    first = pl.BlockSpec((width, block), lambda i: (0, i))
    second = pl.BlockSpec((block, width), lambda i: (i, 0))
    low = jax.ShapeDtypeStruct((rows, hidden_width), jnp.bfloat16)
    out = jax.ShapeDtypeStruct((rows, width), jnp.bfloat16)
    forward = pre is None
    return pl.pallas_call(
        expert_kernel if forward else expert_back_kernel,
        grid=(hidden_width // block,),
        in_specs=[fixed, first, second] + ([] if forward else [wide]),
        out_specs=[wide, wide, fixed] if forward else [wide, fixed],
        out_shape=[f32(rows, hidden_width), low, out] if forward else [low, out],
        scratch_shapes=[pltpu.VMEM((rows, width), jnp.float32)],
        compiler_params=params(40),
        cost_estimate=pl.CostEstimate(
            flops=4 * rows * width * hidden_width,
            bytes_accessed=4 * width * hidden_width + 6 * rows * hidden_width,
            transcendentals=rows * hidden_width,
        ),
        name="expert_rows" if forward else "expert_rows_back",
    )(rows_in, up, down, *(() if forward else (pre,)))


def expert_grads(part, hidden, back_pre, back_flat, flat_rows, received=()):
    rows, width = back_flat.shape
    half = hidden.shape[1] // 2
    block = 384
    steps = half // block

    def body(part_ref, hidden_ref, back_ref, flat_ref, x_ref, *refs):
        del part_ref
        outs = refs[len(received) :]
        for k, (left, right) in enumerate(((back_ref, x_ref), (hidden_ref, flat_ref))):
            total = rows_rows(left[...], right[...])
            if received:
                total = total + refs[k][...].astype(jnp.float32)
            outs[k][...] = total.astype(jnp.bfloat16)

    wide = pl.BlockSpec((rows, block), lambda i, part_ref: (0, part_ref[0] * steps + i))
    fixed = pl.BlockSpec((rows, width), lambda i, part_ref: (0, 0))
    tall = pl.BlockSpec((block, width), lambda i, part_ref: (i, 0))
    out = jax.ShapeDtypeStruct((half, width), jnp.bfloat16)
    return pl.pallas_call(
        body,
        grid_spec=pltpu.PrefetchScalarGridSpec(
            num_scalar_prefetch=1,
            grid=(steps,),
            in_specs=[wide, wide, fixed, fixed] + [tall] * len(received),
            out_specs=[tall, tall],
        ),
        out_shape=[out, out],
        compiler_params=params(40),
        cost_estimate=pl.CostEstimate(
            flops=4 * rows * width * half, bytes_accessed=8 * half * width, transcendentals=0
        ),
        name="expert_grads",
    )(part, hidden, back_pre, back_flat, flat_rows, *received)


def pack_small(masters):
    mixer, conv, conv_bias, select, step, step_bias, decay, skip, expert, router = masters
    chan, states = decay.shape[1:]
    taps, ranks, low_rank = conv.shape[1], select.shape[2], step.shape[1]
    part, expert_count = router.shape[1:]
    thin = taps + states + 3

    def body(mixer_ref, conv_ref, conv_bias_ref, select_ref, step_ref, step_bias_ref, decay_ref,
             skip_ref, expert_ref, router_ref, out_ref, rows, columns):
        def shift(by):
            down = lax.broadcasted_iota(jnp.int32, (lanes, lanes), 0)
            right = lax.broadcasted_iota(jnp.int32, (lanes, lanes), 1)
            return jnp.where(right == down + by, 1.0, 0.0).astype(jnp.bfloat16)

        across = lax.broadcasted_iota(jnp.int32, (chan, chan), 0)
        along = lax.broadcasted_iota(jnp.int32, (chan, chan), 1)
        same = jnp.where(across == along, 1.0, 0.0).astype(jnp.bfloat16)
        rows[...] = jnp.zeros_like(rows)
        rows[:taps] = conv_ref[0]
        rows[thin - 3 : thin - 2] = conv_bias_ref[...]
        rows[thin - 2 : thin - 1] = step_bias_ref[...]
        rows[thin - 1 : thin] = skip_ref[...]
        rows[thin : thin + 1, :part] = mixer_ref[...]
        rows[thin + 1 : thin + 2, :part] = expert_ref[...]
        total = cross_cols(same, rows[...].astype(jnp.bfloat16))
        columns[...] = jnp.zeros_like(columns)
        columns[:, :states] = decay_ref[0]
        total = total + product(columns[...].astype(jnp.bfloat16), shift(taps))
        columns[...] = jnp.zeros_like(columns)
        columns[:part, :expert_count] = router_ref[0]
        total = total + product(columns[...].astype(jnp.bfloat16), shift(thin + 2))
        out_ref[:, 2 * lanes :] = total.astype(jnp.bfloat16)
        columns[...] = jnp.zeros_like(columns)
        columns[:, :ranks] = select_ref[0]
        out_ref[:, :lanes] = columns[...].astype(jnp.bfloat16)
        rows[...] = jnp.zeros_like(rows)
        rows[:low_rank] = step_ref[0]
        total = cross_cols(same, rows[...].astype(jnp.bfloat16))
        out_ref[:, lanes : 2 * lanes] = total.astype(jnp.bfloat16)

    return pl.pallas_call(
        body,
        out_shape=jax.ShapeDtypeStruct((chan, 3 * lanes), jnp.bfloat16),
        scratch_shapes=[
            pltpu.VMEM((lanes, chan), jnp.float32),
            pltpu.VMEM((chan, lanes), jnp.float32),
        ],
        name="pack_small",
    )(*masters)


def gather_kernel(
    phase, along_dp, along_expert, own_refs, layer_refs,
    here_sem, z_send, z_recv, xy_send, xy_recv, c_send, c_recv,
):
    section = lax.axis_index("section")
    d = lax.axis_index("dp")
    e = lax.axis_index("expert")
    arrays = range(len(layer_refs[0]))
    mesh_id = pl.DeviceIdType.MESH
    ways = (1, -1)
    direct = [m for m in range(1, along_expert) if m != 3]

    def exists(index):
        return jnp.logical_and(index >= 0, index < along_dp)

    barrier = pltpu.get_barrier_semaphore()
    peers = [(section, d, e ^ m) for m in range(1, along_expert)] + [(1 - section, d, e)]
    for peer in peers:
        pl.semaphore_signal(barrier, inc=1, device_id=peer, device_id_type=mesh_id)
    expected = len(peers)
    if phase == 0:
        for way in ways:

            @pl.when(exists(d + way))
            def _():
                pl.semaphore_signal(
                    barrier, inc=1, device_id=(section, d + way, e), device_id_type=mesh_id
                )

        expected = expected + jnp.where(d > 0, 1, 0) + jnp.where(d < along_dp - 1, 1, 0)
    pl.semaphore_wait(barrier, expected)

    items = [(0, 0, 0)] + [
        (1 + 2 * step + (way < 0), way, step) for step in range(along_dp - 1) for way in ways
    ]

    def origin(item):
        index, way, step = item
        return d - way * (step + 1) if way else d

    def mine(item):
        if item[1] == 0:
            return phase == 0
        if item[2] > 0:
            return phase == 1
        return True if item[1] < 0 else phase == 0

    def here_now(item):
        if item[1] < 0 and item[2] == 0:
            return (d == 0) if phase == 0 else (d > 0)
        return d >= 0

    def when(item, *more):
        if item[1] == 0 and not more:
            return lambda work: work()
        alive = exists(origin(item))
        for other in more:
            alive = jnp.logical_and(alive, other)
        return pl.when(alive)

    def work(all_refs, other_refs):
        def place(item, m):
            return origin(item) * along_expert + (e ^ m)

        def copy(item, m, a, peer, send, recv):
            held = all_refs[a].at[place(item, m)]
            own = phase == 0 and item[1] == 0 and m == 0
            return pltpu.make_async_remote_copy(
                src_ref=own_refs[a] if own else held,
                dst_ref=held,
                send_sem=send,
                recv_sem=recv,
                device_id=peer,
                device_id_type=mesh_id,
            )

        def onward(item, way, a):
            step = item[2] + 1 if item[1] else 0
            k = 0 if way > 0 else 1
            peer = (section, d + way, e)
            return copy(item, 0, a, peer, z_send.at[k, step, a], z_recv.at[k, step, a])

        def to_expert(item, m, a):
            peer = (section, d, e ^ m)
            sems = (xy_send.at[item[0], m - 1, a], xy_recv.at[item[0], m - 1, a])
            return copy(item, 0, a, peer, *sems)

        def relayed(item, a):
            return 1 + (a + (item[2] + 1 if a == arrays[-1] else 0)) % 2

        def relay(item, m, a):
            peer = (section, d, e ^ 3 ^ m)
            sems = (xy_send.at[item[0], 2, a], xy_recv.at[item[0], 2, a])
            return copy(item, m, a, peer, *sems)

        def to_core(item, m, a):
            peer = (1 - section, d, e)
            return copy(item, m, a, peer, c_send.at[item[0], m, a], c_recv.at[item[0], m, a])

        def landed(ref, sem):
            pltpu.make_async_copy(ref, ref, sem).wait()

        def here(a):
            return pltpu.make_async_copy(
                own_refs[a], all_refs[a].at[place(items[0], 0)], here_sem.at[a]
            )

        def share(item):
            for a in arrays:
                for m in direct:
                    to_expert(item, m, a).start()

        def gather(item):
            for m in direct:
                for a in arrays:
                    landed(all_refs[a].at[place(item, m)], xy_recv.at[item[0], m - 1, a])
                    if m < 3 and relayed(item, a) == 3 - m:
                        relay(item, m, a).start()
                    to_core(item, m, a).start()

        def gather_last(item):
            for a in arrays:
                landed(all_refs[a].at[place(item, 3)], xy_recv.at[item[0], 2, a])
                to_core(item, 3, a).start()

        def finish_shared(item):
            for a in arrays:
                for m in direct:
                    to_expert(item, m, a).wait_send()
                relay(item, 3 - relayed(item, a), a).wait_send()
                for m in range(1, along_expert):
                    finish_core(item, m, a)

        def finish_core(item, m, a):
            to_core(item, m, a).wait_send()
            landed(other_refs[a].at[place(item, m)], c_recv.at[item[0], m, a])

        if phase == 0:
            for a in arrays:
                here(a).start()
                for way in ways:

                    @pl.when(exists(d + way))
                    def _():
                        onward(items[0], way, a).start()

                for m in direct:
                    to_expert(items[0], m, a).start()
                to_core(items[0], 0, a).start()
            queue = [items[0]]
            for step in range(along_dp - 1):
                for item in [item for item in items[1:] if item[2] == step]:
                    k = 0 if item[1] > 0 else 1

                    @when(item)
                    def _():
                        for a in arrays:
                            landed(all_refs[a].at[place(item, 0)], z_recv.at[k, step, a])

                    if step < along_dp - 2:

                        @when(item, exists(d + item[1]))
                        def _():
                            for a in arrays:
                                onward(item, item[1], a).start()

                    @when(item)
                    def _():
                        for a in arrays:
                            to_core(item, 0, a).start()

                    if mine(item):
                        when(item, here_now(item))(lambda: share(item))
                for item in queue:
                    when(item, here_now(item))(lambda: gather(item))
                queue = [item for item in items[1:] if item[2] == step and mine(item)]
            for item in queue:
                when(item, here_now(item))(lambda: gather(item))
            for item in items:
                if mine(item):
                    when(item, here_now(item))(lambda: gather_last(item))
            for a in arrays:
                here(a).wait()
            for item in items:
                if mine(item):
                    when(item, here_now(item))(lambda: finish_shared(item))

                @when(item)
                def _():
                    for a in arrays:
                        finish_core(item, 0, a)

                for way in ways if item[1] == 0 else (item[1],):
                    if item[1] == 0 or item[2] < along_dp - 2:

                        @when(item, exists(d + way))
                        def _():
                            for a in arrays:
                                onward(item, way, a).wait_send()
        else:
            rest = [item for item in items if mine(item)]
            for step in (share, gather, gather_last, finish_shared):
                for item in rest:
                    when(item, here_now(item))(lambda: step(item))

    @pl.when(section == 0)
    def _():
        work(layer_refs[0], layer_refs[1])

    @pl.when(section == 1)
    def _():
        work(layer_refs[1], layer_refs[0])


def gather_call(phase, parts, held=()):
    along_dp, along_expert = lax.axis_size("dp"), lax.axis_size("expert")
    total = len(parts) if phase == 0 else len(held) // 2
    given = parts if phase == 0 else held
    items = 2 * along_dp - 1

    def body(*refs):
        outs = refs[len(given) : len(given) + 2 * total]
        gather_kernel(
            phase, along_dp, along_expert, refs[: len(given)], (outs[:total], outs[total:]),
            *refs[len(given) + 2 * total :],
        )

    dma = pltpu.SemaphoreType.DMA
    shapes = [
        jax.ShapeDtypeStruct((along_dp * along_expert,) + part.shape, part.dtype)
        for part in parts
    ]
    return pl.pallas_call(
        body,
        in_specs=[pl.BlockSpec(memory_space=pltpu.HBM)] * len(given),
        out_specs=[pl.BlockSpec(memory_space=pltpu.HBM)] * (2 * total),
        out_shape=shapes * 2
        if phase == 0
        else [jax.ShapeDtypeStruct(part.shape, part.dtype) for part in held],
        input_output_aliases={} if phase == 0 else {k: k for k in range(2 * total)},
        scratch_shapes=[
            dma((total,)),
            dma((2, along_dp - 1, total)),
            dma((2, along_dp - 1, total)),
            dma((items, along_expert - 1, total)),
            dma((items, along_expert - 1, total)),
            dma((items, along_expert, total)),
            dma((items, along_expert, total)),
        ],
        compiler_params=pltpu.CompilerParams(collective_id=phase, has_side_effects=True),
        cost_estimate=pl.CostEstimate(flops=0, bytes_accessed=250 * 2**20, transcendentals=0),
        name="weights_along_dp" if phase == 0 else "weights_across",
    )(*given)


def carry_kernel(count, backward, *refs):
    if backward:
        end_ref, totals_ref, rate_ref, entry_ref, ends_ref, send_sem, recv_sem = refs
        shared = [ends_ref]
    else:
        end_ref, rate_ref, entry_ref, totals_ref, ends_ref, send_sem, recv_sem = refs
        shared = [ends_ref, totals_ref]
    states = rate_ref.shape[0]
    e = lax.axis_index("expert")
    mesh_id = pl.DeviceIdType.MESH

    def peer(m):
        return (lax.axis_index("section"), lax.axis_index("dp"), e ^ m)

    barrier = pltpu.get_barrier_semaphore()
    for m in range(1, count):
        pl.semaphore_signal(barrier, inc=1, device_id=peer(m), device_id_type=mesh_id)
    pl.semaphore_wait(barrier, count - 1)
    ends_ref[e] = end_ref[:states].astype(jnp.bfloat16)
    if not backward:
        totals_ref[e] = jnp.sum(end_ref[states:], axis=0, keepdims=True)

    def copy(m, a):
        return pltpu.make_async_remote_copy(
            src_ref=shared[a].at[e],
            dst_ref=shared[a].at[e],
            send_sem=send_sem.at[m - 1, a],
            recv_sem=recv_sem.at[m - 1, a],
            device_id=peer(m),
            device_id_type=mesh_id,
        )

    for m in range(1, count):
        for a in range(len(shared)):
            copy(m, a).start()
    for m in range(1, count):
        for a in range(len(shared)):
            there = shared[a].at[e ^ m]
            pltpu.make_async_copy(there, there, recv_sem.at[m - 1, a]).wait()
    width = rate_ref.shape[1]
    for start in range(0, width, lanes):
        cols = slice(start, start + lanes)
        state = jnp.zeros((states, lanes), jnp.float32)
        for k in range(count - 1, -1, -1) if backward else range(count):
            reached = jnp.where(k > e if backward else k < e, 1.0, 0.0)
            kept = jnp.exp(rate_ref[:, cols] * totals_ref[k, :, cols])
            new = kept * state + ends_ref[k, :, cols].astype(jnp.float32)
            state = state + reached * (new - state)
        entry_ref[:, cols] = state
    for m in range(1, count):
        for a in range(len(shared)):
            copy(m, a).wait_send()


def carry_call(end, rate, totals=None):
    count = lax.axis_size("expert")
    states, width = rate.shape
    backward = totals is not None
    dma = pltpu.SemaphoreType.DMA
    vmem = pl.BlockSpec(memory_space=pltpu.VMEM)
    operands = (end, totals, rate) if backward else (end, rate)
    total_shape = jax.ShapeDtypeStruct((count, 1, width), jnp.float32)
    out = pl.pallas_call(
        functools.partial(carry_kernel, count, backward),
        in_specs=[vmem] * len(operands),
        out_specs=[vmem] if backward else [vmem, vmem],
        out_shape=[f32(states, width)] + ([] if backward else [total_shape]),
        scratch_shapes=[
            pltpu.VMEM((count, states, width), jnp.bfloat16),
            dma((count - 1, 2)),
            dma((count - 1, 2)),
        ],
        compiler_params=pltpu.CompilerParams(
            collective_id=3 if backward else 2, has_side_effects=True
        ),
        name="adjoint_carry" if backward else "state_carry",
    )(*operands)
    return out


def settle_kernel(along_dp, along_expert, taps_ref, small_ref, taps_out, small_out,
                  taps_held, small_held, taps_part, small_part, taps_last, small_last,
                  xy_send, xy_recv, z_send, z_recv):
    section = lax.axis_index("section")
    d = lax.axis_index("dp")
    e = lax.axis_index("expert")
    mesh_id = pl.DeviceIdType.MESH
    pairs = ((taps_ref, taps_held, taps_part, taps_last, taps_out),
             (small_ref, small_held, small_part, small_last, small_out))

    barrier = pltpu.get_barrier_semaphore()
    peers = [(section, d, e ^ m) for m in range(1, along_expert)]
    peers += [(section, lax.rem(d + k, along_dp), e) for k in range(1, along_dp)]
    for peer in peers:
        pl.semaphore_signal(barrier, inc=1, device_id=peer, device_id_type=mesh_id)
    pl.semaphore_wait(barrier, len(peers))

    def across(m, a):
        return pltpu.make_async_remote_copy(
            src_ref=pairs[a][0].at[e ^ m], dst_ref=pairs[a][1].at[m - 1],
            send_sem=xy_send.at[m - 1, a], recv_sem=xy_recv.at[m - 1, a],
            device_id=(section, d, e ^ m), device_id_type=mesh_id,
        )

    def along(k, a):
        there = lax.rem(d + k, along_dp)
        return pltpu.make_async_remote_copy(
            src_ref=pairs[a][2].at[there], dst_ref=pairs[a][3].at[k - 1],
            send_sem=z_send.at[k - 1, a], recv_sem=z_recv.at[k - 1, a],
            device_id=(section, there, e), device_id_type=mesh_id,
        )

    def landed(ref, sem):
        pltpu.make_async_copy(ref, ref, sem).wait()

    for a in range(2):
        for m in range(1, along_expert):
            across(m, a).start()
    for a, (own, held, part, last, out) in enumerate(pairs):
        for m in range(1, along_expert):
            landed(held.at[m - 1], xy_recv.at[m - 1, a])
        for k in range(along_dp):
            total = own[e, k].astype(jnp.float32)
            for m in range(1, along_expert):
                total = total + held[m - 1, k].astype(jnp.float32)
            part[k] = total.astype(jnp.bfloat16)
        for k in range(1, along_dp):
            along(k, a).start()
    for a, (own, held, part, last, out) in enumerate(pairs):
        total = part[d].astype(jnp.float32)
        for k in range(1, along_dp):
            landed(last.at[k - 1], z_recv.at[k - 1, a])
            total = total + last[k - 1].astype(jnp.float32)
        out[...] = total.astype(jnp.bfloat16)
    for a in range(2):
        for m in range(1, along_expert):
            across(m, a).wait_send()
        for k in range(1, along_dp):
            along(k, a).wait_send()


def settle_call(taps, small):
    along_dp, along_expert = lax.axis_size("dp"), lax.axis_size("expert")
    vmem = pl.BlockSpec(memory_space=pltpu.VMEM)
    dma = pltpu.SemaphoreType.DMA
    arrays = (taps, small)

    def room(*lead):
        return [pltpu.VMEM(lead + array.shape[2:], jnp.bfloat16) for array in arrays]

    return pl.pallas_call(
        functools.partial(settle_kernel, along_dp, along_expert),
        in_specs=[vmem] * 2,
        out_specs=[vmem] * 2,
        out_shape=[jax.ShapeDtypeStruct(array.shape[2:], jnp.bfloat16) for array in arrays],
        scratch_shapes=room(along_expert - 1, along_dp)
        + room(along_dp)
        + room(along_dp - 1)
        + [dma((along_expert - 1, 2))] * 2
        + [dma((along_dp - 1, 2))] * 2,
        compiler_params=pltpu.CompilerParams(
            collective_id=4, has_side_effects=True, vmem_limit_bytes=40 * 2**20
        ),
        cost_estimate=pl.CostEstimate(flops=0, bytes_accessed=200 * 2**20, transcendentals=0),
        name="last_settle",
    )(*arrays)


def small_grads_call(select, step, conv, decay, lines, models, router, ranks, low_rank):
    across, along = lax.axis_size("dp"), lax.axis_size("expert")
    count = across * along
    chan = select.shape[0] // count
    part = router.shape[1] // count
    taps, states = conv.shape[0], decay.shape[0]

    def body(select_ref, step_ref, conv_ref, decay_ref, a_ref, b_ref, c_ref, mixer_ref, expert_ref,
             router_ref, out_ref, rows, models_rows):
        down = lax.broadcasted_iota(jnp.int32, (lanes, lanes), 0)
        right = lax.broadcasted_iota(jnp.int32, (lanes, lanes), 1)
        same = jnp.where(down == right, 1.0, 0.0).astype(jnp.bfloat16)
        rows[...] = jnp.zeros_like(rows)
        rows[ranks : ranks + taps] = conv_ref[...]
        rows[ranks + taps : ranks + taps + states] = decay_ref[...]
        at = ranks + taps + states
        for k, ref in enumerate((a_ref, b_ref, c_ref)):
            rows[at + k : at + k + 1] = ref[...]
        models_rows[...] = jnp.zeros_like(models_rows)
        models_rows[low_rank : low_rank + 1] = mixer_ref[...]
        models_rows[low_rank + 1 : low_rank + 2] = expert_ref[...]
        models_rows[low_rank + 2 : low_rank + 2 + router_ref.shape[0]] = router_ref[...]
        first = rows_rows(rows[...].astype(jnp.bfloat16), same) + select_ref[...]
        second = step_ref[...]
        model = rows_rows(models_rows[...].astype(jnp.bfloat16), same)
        for j in range(count):
            spot = (j % along) * across + j // along
            out_ref[spot, 0] = first[j * chan : (j + 1) * chan].astype(jnp.bfloat16)
            block = second[j * chan : (j + 1) * chan]
            top = block[:part] + model[j * part : (j + 1) * part]
            out_ref[spot, 1] = jnp.concatenate([top, block[part:]], axis=0).astype(jnp.bfloat16)

    return pl.pallas_call(
        body,
        out_shape=jax.ShapeDtypeStruct((count, 2, chan, lanes), jnp.bfloat16),
        scratch_shapes=[
            pltpu.VMEM((lanes, count * chan), jnp.float32),
            pltpu.VMEM((lanes, router.shape[1]), jnp.float32),
        ],
        compiler_params=pltpu.CompilerParams(vmem_limit_bytes=40 * 2**20),
        name="small_gradients",
    )(select, step, conv, decay, *lines, *models, router)


def swap(array):
    return lax.ppermute(array, "section", [(0, 1), (1, 0)])


def pick(first, left, right):
    return jnp.where(first, left, right), jnp.where(first, right, left)


def halves(array, first, axis):
    width = array.shape[axis] // 2
    low = lax.slice_in_dim(array, 0, width, axis=axis)
    high = lax.slice_in_dim(array, width, 2 * width, axis=axis)
    return pick(first, low, high)


def turned(array, axis, hop):
    length = lax.axis_size(axis)
    return lax.ppermute(array, axis, [(i, (i + hop) % length) for i in range(length)])


def crossed(array, axis, mask):
    length = lax.axis_size(axis)
    return lax.ppermute(array, axis, [(i, i ^ mask) for i in range(length)])


def expert_parts(up, down, first):
    pairs = [
        halves(master.astype(jnp.bfloat16), first, axis)
        for axis, master in enumerate((down, up))
    ]
    others = [swap(sent) for _, sent in pairs]
    down, up = [pick(first, own, got) for (own, _), got in zip(pairs, others)]
    return [up[0], down[0], up[1], down[1]]


def expert_spread(up, down):
    return tuple(
        lax.all_gather(part, ("section", "dp"), axis=axis, tiled=True)
        for axis, part in ((1, up), (0, down))
    )


def tie(values, after):
    count = len(values)

    def body(*refs):
        del refs

    return pl.pallas_call(
        body,
        in_specs=[pl.BlockSpec(memory_space=pl.ANY)] * (count + len(after)),
        out_specs=[pl.BlockSpec(memory_space=pl.ANY)] * count,
        out_shape=[jax.ShapeDtypeStruct(value.shape, value.dtype) for value in values],
        input_output_aliases={k: k for k in range(count)},
        name="order",
    )(*values, *after)


class LineSum:
    def __init__(self, up, down):
        self.parts = (up, down)
        self.here, self.count = lax.axis_index("dp"), lax.axis_size("dp")
        self.width = up.shape[0] // self.count
        self.step, self.moving = 0, (None, None)

    def chunk(self, index):
        start = jnp.clip(index, 0, self.count - 1) * self.width
        cuts = [lax.dynamic_slice_in_dim(part, start, self.width, 0) for part in self.parts]
        return jnp.stack(cuts).astype(jnp.float32)

    def advance(self, steps=1):
        for _ in range(steps):
            ahead = self.count - 1 - self.step
            if ahead == 0:
                break
            moved = []
            for way, moving in zip((1, -1), self.moving):
                held = self.chunk(self.here + way * ahead)
                if moving is not None:
                    held = held + moving.astype(jnp.float32)
                pairs = [
                    (i, i + way) for i in range(self.count) if 0 <= i + way * ahead < self.count
                ]
                moved.append(lax.ppermute(held.astype(jnp.bfloat16), "dp", pairs))
            self.moving = tuple(moved)
            self.step += 1
        return self.moving

    def total(self):
        up, down = self.advance(self.count)
        summed = self.chunk(self.here) + up.astype(jnp.float32) + down.astype(jnp.float32)
        return summed.astype(jnp.bfloat16)


def joined(pair, product_of):
    sent = swap(product_of(pair[1]).astype(jnp.bfloat16))
    return (product_of(pair[0]) + sent.astype(jnp.float32)).astype(jnp.bfloat16)


def by_expert(array, split):
    rows, width = array.shape
    across, along = lax.axis_size("dp"), lax.axis_size("expert")
    parts = array.reshape(rows, across, along, split, width // (across * along * split))
    return parts.transpose(0, 3, 2, 1, 4).reshape(rows, width)


def settle_expert(total):
    return lax.psum_scatter(total, "expert", scatter_dimension=0, tiled=True)


def settle_dp(total):
    return lax.psum_scatter(total, "dp", scatter_dimension=0, tiled=True)


def settle_direct(total):
    here, along = lax.axis_index("expert"), lax.axis_size("expert")
    width = total.shape[0] // along

    def chunk(array, index, size):
        return lax.dynamic_slice_in_dim(array, index * size, size, 0)

    summed = chunk(total, here, width).astype(jnp.float32)
    for mask in range(1, along):
        summed = summed + crossed(chunk(total, here ^ mask, width), "expert", mask).astype(
            jnp.float32
        )
    total = summed.astype(jnp.bfloat16)
    here, across = lax.axis_index("dp"), lax.axis_size("dp")
    width = width // across
    summed = chunk(total, here, width).astype(jnp.float32)
    for hop in range(1, across):
        there = lax.rem(here + hop, across)
        summed = summed + turned(chunk(total, there, width), "dp", hop).astype(jnp.float32)
    return summed.astype(jnp.bfloat16)


def hand_back(parts, first, cut):
    own, sent = pick(first, parts[0], parts[1])
    low, high = pick(first, own, swap(sent))
    return jnp.concatenate([low, high], axis=cut).astype(jnp.float32)


def widen(array):
    return jnp.pad(array, ((0, 0), (0, lanes - array.shape[1])))


def piled(parts):
    total, at = None, 0
    rows = sum(part.shape[0] for part in parts)
    for part in parts:
        padded = jnp.pad(part, ((at, rows - at - part.shape[0]), (0, 0)))
        total = padded if total is None else total + padded
        at += part.shape[0]
    return total


def dispatch_back(grad_out, gate_value, token_index, expert_count, capacity):
    back_result = (gate_value[:, None] * grad_out).astype(jnp.bfloat16)
    none = jnp.zeros((1, grad_out.shape[1]), jnp.bfloat16)
    padded = jnp.concatenate([back_result, none], axis=0)
    outgoing = padded[token_index].reshape(expert_count, capacity, -1)
    return lax.all_to_all(outgoing, "expert", split_axis=0, concat_axis=0, tiled=True)


def layer_forward(residual, small, big, routing, documents, mark, low_rank, grad_out):
    conv_part, gate_part, output_weight, up_weight, down_weight = big
    row_count, model_width = residual.shape
    tap_count = small.conv.shape[0]
    states = small.rate.shape[0]
    expert_count = small.router.shape[0]
    capacity = 2 * row_count // expert_count
    normed = norm_scale(residual, small.mixer_gain).astype(jnp.bfloat16)
    conv_in = product(normed, conv_part).astype(jnp.bfloat16)
    gate_in = product(normed, gate_part).astype(jnp.bfloat16)
    rim_rows = from_behind(conv_in[row_count - tap_count + 1 :], "expert", 1)
    wide_in = jnp.concatenate([rim_rows, conv_in], axis=0)
    activated = conv_act(
        wide_in.astype(jnp.float32), small.conv, small.conv_bias, documents
    ).astype(jnp.bfloat16)
    projected = product(activated, small.select)
    step_low = jnp.where(jnp.arange(lanes) < low_rank, projected, 0.0).astype(jnp.bfloat16)
    in_wide = jnp.broadcast_to(
        projected[:, low_rank : low_rank + states, None], (row_count, states, lanes)
    )
    out_wide = jnp.broadcast_to(
        projected[:, low_rank + states : low_rank + 2 * states, None], (row_count, states, lanes)
    )
    step_pre = cross_cols(step_low, small.step) + small.step_bias
    step_size = jax.nn.softplus(step_pre)
    ends = end_call(step_size, activated, mark, in_wide, small.rate)
    entry_state, totals = carry_call(ends, small.rate)
    scanned = scan_call(
        step_size, activated, mark, in_wide, out_wide, small.rate, entry_state, small.skip
    )
    gated_out = gate_product(scanned, gate_in.astype(jnp.float32)).astype(jnp.bfloat16)
    middle = residual + product(gated_out, output_weight)
    normed_two = norm_scale(middle, small.expert_gain).astype(jnp.bfloat16)
    logits = cross_cols(normed_two, small.router)
    probability = jax.nn.softmax(logits, axis=-1)
    chosen = routing[:, None] == jnp.arange(expert_count, dtype=jnp.int32)[None, :]
    gate_value = jnp.sum(jnp.where(chosen, probability, 0.0), axis=1)
    slot_index, token_index = dispatch_tables(chosen, capacity)
    padded = jnp.concatenate([normed_two, jnp.zeros((1, model_width), jnp.bfloat16)], axis=0)
    outgoing = padded[token_index].reshape(expert_count, capacity, model_width)
    arrived = lax.all_to_all(outgoing, "expert", split_axis=0, concat_axis=0, tiled=True)
    flat_rows = arrived.reshape(-1, model_width)
    back_arrived = None
    if grad_out is not None:
        back_arrived = dispatch_back(grad_out, gate_value, token_index, expert_count, capacity)
        (flat_rows,) = tie([flat_rows], (back_arrived,))
    pre_act, hidden, result = expert_call(flat_rows, up_weight, down_weight)
    result = result.reshape(arrived.shape)
    returned = lax.all_to_all(result, "expert", split_axis=0, concat_axis=0, tiled=True)
    mixture = returned.reshape(-1, model_width)[slot_index].astype(jnp.float32)
    out_residual = middle + gate_value[:, None] * mixture
    stored = SimpleNamespace(
        residual=residual, normed=normed, wide_in=wide_in, gate_in=gate_in, activated=activated,
        step_low=step_low, step_pre=step_pre, step_size=step_size, in_wide=in_wide,
        out_wide=out_wide, totals=totals, entry_state=entry_state, scanned=scanned,
        gated_out=gated_out, middle=middle, normed_two=normed_two, probability=probability,
        chosen=chosen, gate_value=gate_value, slot_index=slot_index, token_index=token_index,
        pre_act=pre_act, hidden=hidden, flat_rows=flat_rows, mixture=mixture,
        documents=documents, mark=mark, back_arrived=back_arrived,
    )
    return out_residual, stored


def layer_backward(grad_out, kept, small, big, section, earlier, pending, ranks):
    conv_part, gate_part, output_weight, up_weight, down_weight = big
    first = section == 0
    row_count, model_width = grad_out.shape
    tap_count = small.conv.shape[0]
    expert_count = small.router.shape[0]
    capacity = 2 * row_count // expert_count
    back_gate = jnp.sum(grad_out * kept.mixture, axis=1)
    back_arrived = kept.back_arrived
    if back_arrived is None:
        back_arrived = dispatch_back(
            grad_out, kept.gate_value, kept.token_index, expert_count, capacity
        )
    back_flat = back_arrived.reshape(-1, model_width)
    back_pre, back_expert = expert_call(back_flat, up_weight, down_weight, kept.pre_act)
    back_expert = back_expert.reshape(back_arrived.shape)
    if earlier is not None:
        back_expert, *earlier.moving = tie([back_expert, *earlier.moving], ())
        earlier.advance()
    back_returned = lax.all_to_all(back_expert, "expert", split_axis=0, concat_axis=0, tiled=True)
    sources = (kept.hidden, back_pre, back_flat, kept.flat_rows)
    own_part, sent_part = jnp.reshape(section, (1,)), jnp.reshape(1 - section, (1,))
    received = [swap(part) for part in expert_grads(sent_part, *sources)]
    grad_up, grad_down = expert_grads(own_part, *sources, received)
    line = LineSum(grad_up, grad_down)
    line.advance()
    back_tokens = back_returned.reshape(-1, model_width)[kept.slot_index].astype(jnp.float32)
    back_logits = (
        (back_gate * kept.gate_value)[:, None]
        * (kept.chosen.astype(jnp.float32) - kept.probability)
    ).astype(jnp.bfloat16)
    grad_router = cross_rows(back_logits, kept.normed_two)
    back_normed_two = back_tokens + product(back_logits, small.router)
    back_mid_norm, grad_expert_gain = jax.vjp(norm_scale, kept.middle, small.expert_gain)[1](
        back_normed_two
    )
    back_middle = grad_out + back_mid_norm
    back_branch = back_middle.astype(jnp.bfloat16)
    gated_pair = halves(by_expert(kept.gated_out, 2), first, 1)
    grad_output = joined(gated_pair, lambda half: cross_rows(half, back_branch))
    back_gated = cross_cols(back_branch, output_weight)
    back_scanned, back_gate_in = jax.vjp(
        gate_product, kept.scanned, kept.gate_in.astype(jnp.float32)
    )[1](back_gated)
    normed_rows = by_expert(kept.normed, 1)
    part_rows = model_width // (lax.axis_size("dp") * lax.axis_size("expert"))
    back_gate_in = back_gate_in.astype(jnp.bfloat16)
    grad_gate = joined(halves(back_gate_in, first, 1), lambda half: cross_rows(normed_rows, half))
    together = [part.reshape(-1, part_rows, model_width) for part in (grad_gate, grad_output)]
    together = jnp.stack(together, axis=1).reshape(-1, model_width)
    late = settle_expert(together)
    (back_scanned,) = tie([back_scanned], (grad_up, grad_down, together))
    rate = small.rate
    back_ends = entry_call(kept.step_size, kept.mark, kept.out_wide, rate, back_scanned)
    (adjoint,) = carry_call(back_ends, rate, kept.totals)
    back_act, back_step, grad_decay, back_in, back_out = back_call(
        kept.step_size, kept.activated, kept.mark, kept.in_wide, kept.out_wide,
        rate, kept.entry_state, adjoint, small.skip, back_scanned,
    )
    moving = list(line.moving) + ([] if earlier is None else list(earlier.moving))
    back_step, *moving = tie([back_step, *moving], pending)
    line.moving = tuple(moving[:2])
    if earlier is not None:
        earlier.moving = tuple(moving[2:])
    line.advance()
    act_float = kept.activated.astype(jnp.float32)
    grad_skip = jnp.sum(back_scanned * act_float, axis=0, keepdims=True)
    back_step_pre = back_step * jax.nn.sigmoid(kept.step_pre)
    grad_step_bias = jnp.sum(back_step_pre, axis=0, keepdims=True)
    back_step_low = back_step_pre.astype(jnp.bfloat16)
    grad_step = cross_rows(back_step_low, kept.step_low)
    back_rank = product(back_step_low, small.step)
    low_rank = ranks - 2 * rate.shape[0]
    maps = jnp.concatenate([jnp.sum(back_in, axis=2), jnp.sum(back_out, axis=2)], axis=1)
    back_projected = back_rank + jnp.pad(maps, ((0, 0), (low_rank, lanes - ranks)))
    back_projected = back_projected.astype(jnp.bfloat16)
    grad_select = cross_rows(kept.activated, back_projected)
    back_activated = back_act + cross_cols(back_projected, small.select)

    def conv_piece(wide_float, taps_in, bias_in):
        return conv_act(wide_float, taps_in, bias_in, kept.documents)

    back_wide, grad_conv, grad_conv_bias = jax.vjp(
        conv_piece, kept.wide_in.astype(jnp.float32), small.conv, small.conv_bias
    )[1](back_activated)
    rim_back = from_behind(back_wide[: tap_count - 1], "expert", -1)
    back_conv_in = back_wide[tap_count - 1 :] + jnp.pad(
        rim_back, ((row_count - tap_count + 1, 0), (0, 0))
    )
    back_conv_in = back_conv_in.astype(jnp.bfloat16)
    grad_taps_in = joined(halves(back_conv_in, first, 1), lambda half: cross_rows(normed_rows, half))
    back_normed = cross_cols(back_conv_in, conv_part) + cross_cols(back_gate_in, gate_part)
    back_residual_norm, grad_mixer_gain = jax.vjp(
        norm_scale, kept.residual, small.mixer_gain
    )[1](back_normed)
    back_residual = back_middle + back_residual_norm
    if earlier is not None:
        grad_select, grad_step = tie([grad_select, grad_step], (grad_taps_in,))
    small_grads = small_grads_call(
        grad_select, grad_step, grad_conv, grad_decay,
        (grad_conv_bias[None], grad_step_bias, grad_skip),
        (grad_mixer_gain[None], grad_expert_gain[None]), grad_router, ranks, ranks - 2 * rate.shape[0],
    )
    return back_residual, grad_taps_in, late, line, small_grads


def small_outputs(total, taps, states, ranks, low_rank, expert_count, part):
    chan = total.shape[1]
    thin = taps + states + 3

    def body(total_ref, *outs):
        mixer, conv, conv_bias, select, step, step_bias, decay, skip, expert, router = outs
        down = lax.broadcasted_iota(jnp.int32, (lanes, lanes), 0)
        right = lax.broadcasted_iota(jnp.int32, (lanes, lanes), 1)
        same = jnp.where(down == right, 1.0, 0.0).astype(jnp.bfloat16)
        rows = cross_cols(same, total_ref[0])
        others = cross_cols(same, total_ref[1])
        select[0] = total_ref[0].astype(jnp.float32)[:, :ranks]
        step[0] = others[:low_rank]
        conv[0] = rows[ranks : ranks + taps]
        decay[0] = total_ref[0].astype(jnp.float32)[:, ranks + taps : ranks + taps + states]
        for ref, at in ((conv_bias, thin - 3), (step_bias, thin - 2), (skip, thin - 1)):
            ref[...] = rows[ranks + at : ranks + at + 1]
        mixer[...] = others[low_rank : low_rank + 1, :part]
        expert[...] = others[low_rank + 1 : low_rank + 2, :part]
        whole = total_ref[1].astype(jnp.float32)
        router[0] = whole[:part, low_rank + 2 : low_rank + 2 + expert_count]

    line = f32(1, chan)
    return pl.pallas_call(
        body,
        out_shape=[
            f32(1, part), f32(1, taps, chan), line, f32(1, chan, ranks), f32(1, low_rank, chan),
            line, f32(1, chan, states), line, f32(1, part), f32(1, part, expert_count),
        ],
        name="small_outputs",
    )(total)


def doc_marks(documents, tap_count):
    own = documents[tap_count - 1 :]
    begins = own != documents[tap_count - 2 : -1]
    return jnp.broadcast_to(jnp.where(begins, reset, 0.0)[:, None], (own.shape[0], lanes))


def shards(
    inputs,
    cotangent,
    routes,
    lengths,
    mixer_gain,
    input_weight,
    conv_weight,
    conv_bias,
    select_weight,
    step_weight,
    step_bias,
    decay_log,
    skip_gain,
    output_weight,
    expert_gain,
    router_weight,
    up_weight,
    down_weight,
):
    section = lax.axis_index("section")
    first = section == 0
    count = lax.axis_size("dp") * lax.axis_size("expert")
    row_count, model_width = inputs.shape[1:]
    tap_count = conv_weight.shape[1]
    chan = conv_bias.shape[1]
    low_rank = step_weight.shape[1]
    states = decay_log.shape[2]
    ranks = select_weight.shape[2]
    expert_count = router_weight.shape[2]

    thin = tap_count + states + 3
    packed = pack_small(
        (
            mixer_gain, conv_weight, conv_bias, select_weight, step_weight, step_bias, decay_log,
            skip_gain, expert_gain, router_weight,
        )
    )
    wide = input_weight.shape[2] // 2
    experts = expert_parts(up_weight[0, 0], down_weight[0, 0], first)
    early = gather_call(
        0,
        (
            packed,
            input_weight[0, :, :wide].astype(jnp.bfloat16),
            input_weight[0, :, wide:].astype(jnp.bfloat16),
            output_weight[0].astype(jnp.bfloat16),
        ),
    )
    experts = tie(experts, early[:1])
    gathered = gather_call(1, (), early)
    gathered = (gathered[:4], gathered[4:])
    part = model_width // count

    def unpack(layer):
        whole = gathered[layer][0].reshape(count * chan, 3 * lanes)
        select, step, rows = [whole[:, k * lanes : (k + 1) * lanes] for k in range(3)]
        rows = rows.T[: thin + 2 + expert_count].astype(jnp.float32)
        model = rows[thin:].reshape(-1, count, chan)[:, :, :part].reshape(-1, model_width)
        return SimpleNamespace(
            select=select, step=step, conv=rows[:tap_count],
            rate=-jnp.exp(rows[tap_count : tap_count + states]),
            conv_bias=rows[thin - 3], step_bias=rows[thin - 2 : thin - 1],
            skip=rows[thin - 1 : thin], mixer_gain=model[0], expert_gain=model[1],
            router=model[2:].astype(jnp.bfloat16),
        )

    small = [unpack(0), unpack(1)]
    experts_two = [expert_spread(*experts[:2]), expert_spread(*experts[2:])]
    big = [
        (
            gathered[k][1].reshape(model_width, wide),
            gathered[k][2].reshape(model_width, wide),
            gathered[k][3].reshape(wide, model_width),
        )
        + experts_two[k]
        for k in range(2)
    ]

    own_routes, sent_routes = pick(first, routes[0, 0, :, 0], routes[0, 1, :, 0])
    routing = pick(first, own_routes, swap(sent_routes))
    lengths_row = lax.dynamic_index_in_dim(lengths[:, 0, :], section, 0, keepdims=False)
    positions = lax.axis_index("expert") * row_count + jnp.arange(
        1 - tap_count, row_count, dtype=jnp.int32
    )
    documents = doc_ids(lengths_row, positions)
    mark = doc_marks(documents, tap_count)

    residual = lax.dynamic_index_in_dim(inputs, section, 0, keepdims=False).astype(jnp.float32)
    grad_last = lax.dynamic_index_in_dim(cotangent, section, 0, keepdims=False)
    grad_last = grad_last.astype(jnp.float32)
    outputs_seen = []
    kept = []
    for layer in range(2):
        out_residual, stored = layer_forward(
            residual, small[layer], big[layer], routing[layer], documents, mark, low_rank, grad_last if layer else None
        )
        outputs_seen.append(out_residual.astype(jnp.bfloat16))
        residual = outputs_seen[-1].astype(jnp.float32)
        kept.append(stored)

    grad_out = grad_last
    input_grads = [None, None]
    settled = [None, None]
    small_sums = [None, None]
    line, pending = None, ()
    for layer in (1, 0):
        earlier = line
        back_residual, grad_taps_in, late, line, small_grads = layer_backward(
            grad_out, kept[layer], small[layer], big[layer], section, earlier, pending, ranks
        )
        input_grads[layer] = back_residual
        grad_out = back_residual.astype(jnp.bfloat16).astype(jnp.float32)
        if layer == 1:
            pending = (settle_dp(settle_expert(grad_taps_in)), settle_dp(late))
        else:
            settled[1] = pending + (earlier.total(),)
            final_late = settle_dp(late)
        small_sums[layer] = small_grads

    across, along = lax.axis_size("dp"), lax.axis_size("expert")
    own_small, sent_small = pick(first, small_sums[0], small_sums[1])
    own_small = own_small.astype(jnp.float32) + swap(sent_small).astype(jnp.float32)
    last, small_last = settle_call(
        grad_taps_in.reshape(along, across, part, model_width),
        own_small.astype(jnp.bfloat16).reshape(along, across, 2, chan, lanes),
    )
    settled[0] = (last, final_late, line.total())
    small_out = small_outputs(
        small_last, tap_count, states, ranks, low_rank, expert_count, part
    )
    experts_back = hand_back((settled[0][2], settled[1][2]), first, 1)
    up_back, down_back = experts_back[0].T, experts_back[1]
    both_late = [(late_one[1][:part], late_one[1][part:]) for late_one in settled]

    def whole_input():
        taps = hand_back((settled[0][0], settled[1][0]), first, 1)
        return jnp.concatenate([taps, hand_back([pair[0] for pair in both_late], first, 1)], axis=1)

    def both(array):
        mine, sent = pick(first, array[0], array[1])
        return jnp.stack(pick(first, mine, swap(sent)))[None]

    return (
        both(outputs_seen),
        both(input_grads),
        small_out[0],
        whole_input()[None],
        *small_out[1:8],
        hand_back([pair[1] for pair in both_late], first, 0)[None],
        *small_out[8:],
        up_back[None, None],
        down_back[None, None],
    )


def solution(mesh):
    return jax.shard_map(
        shards,
        mesh=mesh,
        in_specs=(
            P(None, ("dp", "expert"), None),
            P(None, ("dp", "expert"), None),
            P("section", None, ("dp", "expert"), None),
            P(None, "dp", None),
            P("section", ("dp", "expert")),
            P("section", ("dp", "expert"), None),
            P("section", None, ("dp", "expert")),
            P("section", ("dp", "expert")),
            P("section", ("dp", "expert"), None),
            P("section", None, ("dp", "expert")),
            P("section", ("dp", "expert")),
            P("section", ("dp", "expert"), None),
            P("section", ("dp", "expert")),
            P("section", ("dp", "expert"), None),
            P("section", ("dp", "expert")),
            P("section", ("dp", "expert"), None),
            P("section", "expert", None, "dp"),
            P("section", "expert", "dp", None),
        ),
        out_specs=(
            P("section", None, ("dp", "expert"), None),
            P("section", None, ("dp", "expert"), None),
            P("section", ("dp", "expert")),
            P("section", ("dp", "expert"), None),
            P("section", None, ("dp", "expert")),
            P("section", ("dp", "expert")),
            P("section", ("dp", "expert"), None),
            P("section", None, ("dp", "expert")),
            P("section", ("dp", "expert")),
            P("section", ("dp", "expert"), None),
            P("section", ("dp", "expert")),
            P("section", ("dp", "expert"), None),
            P("section", ("dp", "expert")),
            P("section", ("dp", "expert"), None),
            P("section", "expert", None, "dp"),
            P("section", "expert", "dp", None),
        ),
        check_vma=False,
    )
```

```python
import functools
from types import SimpleNamespace

import jax
import jax.numpy as jnp
from jax import lax
from jax.experimental import pallas as pl
from jax.experimental.pallas import tpu as pltpu
from jax.sharding import PartitionSpec as P

epsilon = 1e-05
lanes = 128
group = 8
reset = 1e30
fold_order = (3, 7, 5, 1, 4, 0, 6, 2)


def row_of(tile, index, states):
    return jnp.broadcast_to(tile[index : index + 1, :], (states, tile.shape[1]))


def fold(parts, shift, rows):
    count = len(parts)
    if count == 1:
        return parts[0]
    span = group // count
    left = fold(parts[: count // 2], shift, rows)
    right = fold(parts[count // 2 :], shift + (span if count > 2 else 0), rows)
    mask = ((rows - shift) & span) != 0
    if count == 2:
        mask = jnp.logical_not(mask)
    return jnp.where(mask, left, right) + pltpu.roll(jnp.where(mask, right, left), span, 0)


def state_sums(parts):
    rows = lax.broadcasted_iota(jnp.int32, (group, lanes), 0)
    halved = [part[:group] + part[group:] for part in parts]
    return fold([halved[k] for k in fold_order], 0, rows)


def end_kernel(step_ref, act_ref, start_ref, in_ref, rate_ref, end_ref):
    rows, width = step_ref.shape
    states = rate_ref.shape[0]
    tiles = width // lanes
    cols = [slice(j * lanes, (j + 1) * lanes) for j in range(tiles)]

    def body(g, carry):
        state, total = carry
        at = pl.ds(pl.multiple_of(g * group, group), group)
        state = list(state)
        total = list(total)
        begin = start_ref[at, :]
        for j in range(tiles):
            step = step_ref[at, cols[j]]
            drive = step * act_ref[at, cols[j]].astype(jnp.float32)
            fall = step + begin
            total[j] = total[j] + fall
            rate = rate_ref[:, cols[j]]
            for i in range(group):
                decay = jnp.exp(row_of(fall, i, states) * rate)
                state[j] = decay * state[j] + row_of(drive, i, states) * in_ref[g * group + i]
        return tuple(state), tuple(total)

    zero = tuple(jnp.zeros((states, lanes), jnp.float32) for _ in range(tiles))
    none = tuple(jnp.zeros((group, lanes), jnp.float32) for _ in range(tiles))
    state, total = lax.fori_loop(0, rows // group, body, (zero, none))
    for j in range(tiles):
        end_ref[:states, cols[j]] = state[j]
        end_ref[states:, cols[j]] = total[j]


def scan_kernel(step_ref, act_ref, start_ref, in_ref, out_ref, rate_ref, entry_ref, skip_ref, y_ref):
    rows, width = step_ref.shape
    states = rate_ref.shape[0]
    tiles = width // lanes
    cols = [slice(j * lanes, (j + 1) * lanes) for j in range(tiles)]

    def body(g, state):
        at = pl.ds(pl.multiple_of(g * group, group), group)
        state = list(state)
        begin = start_ref[at, :]
        for j in range(tiles):
            step = step_ref[at, cols[j]]
            act = act_ref[at, cols[j]].astype(jnp.float32)
            drive = step * act
            fall = step + begin
            rate = rate_ref[:, cols[j]]
            parts = []
            for i in range(group):
                decay = jnp.exp(row_of(fall, i, states) * rate)
                state[j] = decay * state[j] + row_of(drive, i, states) * in_ref[g * group + i]
                parts.append(state[j] * out_ref[g * group + i])
            y_ref[at, cols[j]] = skip_ref[:, cols[j]] * act + state_sums(parts)
        return tuple(state)

    lax.fori_loop(
        0, rows // group, body, tuple(entry_ref[:, cols[j]] for j in range(tiles))
    )


def entry_kernel(step_ref, start_ref, out_ref, rate_ref, grad_ref, end_ref):
    rows, width = step_ref.shape
    states = rate_ref.shape[0]
    tiles = width // lanes
    cols = [slice(j * lanes, (j + 1) * lanes) for j in range(tiles)]
    groups = rows // group

    def body(k, state):
        g = groups - 1 - k
        at = pl.ds(pl.multiple_of(g * group, group), group)
        state = list(state)
        begin = start_ref[at, :]
        for j in range(tiles):
            fall = step_ref[at, cols[j]] + begin
            grad = grad_ref[at, cols[j]]
            rate = rate_ref[:, cols[j]]
            for i in reversed(range(group)):
                decay = jnp.exp(row_of(fall, i, states) * rate)
                state[j] = decay * (state[j] + row_of(grad, i, states) * out_ref[g * group + i])
        return tuple(state)

    zero = tuple(jnp.zeros((states, lanes), jnp.float32) for _ in range(tiles))
    state = lax.fori_loop(0, groups, body, zero)
    for j in range(tiles):
        end_ref[:, cols[j]] = state[j]


def back_kernel(
    step_ref, act_ref, start_ref, in_ref, out_ref, rate_ref, entry_ref, adj_ref, skip_ref, grad_ref,
    back_act_ref, back_step_ref, back_rate_ref, back_in_ref, back_out_ref, kept, decays,
):
    rows, width = step_ref.shape
    states = rate_ref.shape[0]
    tiles = width // lanes
    cols = [slice(j * lanes, (j + 1) * lanes) for j in range(tiles)]
    groups = rows // group

    @pl.when(pl.program_id(0) == 0)
    def _():
        back_in_ref[...] = jnp.zeros_like(back_in_ref)
        back_out_ref[...] = jnp.zeros_like(back_out_ref)

    for j in range(tiles):
        kept[0, :, cols[j]] = entry_ref[:, cols[j]]

    def ahead(g, state):
        at = pl.ds(pl.multiple_of(g * group, group), group)
        state = list(state)
        begin = start_ref[at, :]
        for j in range(tiles):
            step = step_ref[at, cols[j]]
            drive = step * act_ref[at, cols[j]].astype(jnp.float32)
            fall = step + begin
            rate = rate_ref[:, cols[j]]
            for i in range(group):
                decay = jnp.exp(row_of(fall, i, states) * rate)
                decays[g * group + i, :, cols[j]] = decay
                state[j] = decay * state[j] + row_of(drive, i, states) * in_ref[g * group + i]
                kept[g * group + i + 1, :, cols[j]] = state[j]
        return tuple(state)

    lax.fori_loop(0, groups, ahead, tuple(entry_ref[:, cols[j]] for j in range(tiles)))

    def behind(k, carry):
        flow, slope = carry
        g = groups - 1 - k
        at = pl.ds(pl.multiple_of(g * group, group), group)
        flow = list(flow)
        slope = list(slope)
        back_in = [back_in_ref[g * group + i] for i in range(group)]
        back_out = [back_out_ref[g * group + i] for i in range(group)]
        for j in range(tiles):
            step = step_ref[at, cols[j]]
            act = act_ref[at, cols[j]].astype(jnp.float32)
            drive = step * act
            grad = grad_ref[at, cols[j]]
            rate = rate_ref[:, cols[j]]
            drives, falls = [], []
            for i in reversed(range(group)):
                t = g * group + i
                grad_row = row_of(grad, i, states)
                adj = flow[j] + grad_row * out_ref[t]
                back_out[i] = back_out[i] + kept[t + 1, :, cols[j]] * grad_row
                back_in[i] = back_in[i] + adj * row_of(drive, i, states)
                drives.insert(0, adj * in_ref[t])
                flow[j] = adj * decays[t, :, cols[j]]
                turn = flow[j] * kept[t, :, cols[j]]
                falls.insert(0, turn * rate)
                slope[j] = slope[j] + row_of(step, i, states) * turn
            back_drive, back_fall = state_sums(drives), state_sums(falls)
            back_act_ref[at, cols[j]] = step * back_drive + skip_ref[:, cols[j]] * grad
            back_step_ref[at, cols[j]] = act * back_drive + back_fall
        for i in range(group):
            back_in_ref[g * group + i] = back_in[i]
            back_out_ref[g * group + i] = back_out[i]
        return tuple(flow), tuple(slope)

    zero = tuple(jnp.zeros((states, lanes), jnp.float32) for _ in range(tiles))
    _, slope = lax.fori_loop(
        0, groups, behind, (tuple(adj_ref[:, cols[j]] for j in range(tiles)), zero)
    )
    for j in range(tiles):
        back_rate_ref[:, cols[j]] = slope[j] * rate_ref[:, cols[j]]


def specs(rows, states, block):
    wide = pl.BlockSpec((rows, block), lambda c: (0, c))
    mark = pl.BlockSpec((rows, lanes), lambda c: (0, 0))
    maps = pl.BlockSpec((rows, states, lanes), lambda c: (0, 0, 0))
    held = pl.BlockSpec((states, block), lambda c: (0, c))
    line = pl.BlockSpec((1, block), lambda c: (0, c))
    total = pl.BlockSpec((states + group, block), lambda c: (0, c))
    return wide, mark, maps, held, line, total


def params(mib):
    return pltpu.CompilerParams(
        dimension_semantics=("arbitrary",), vmem_limit_bytes=mib * 1024 * 1024
    )


def block_of(width, most):
    best = lanes
    for tiles in range(1, most // lanes + 1):
        if width % (tiles * lanes) == 0:
            best = tiles * lanes
    return best


def f32(*shape):
    return jax.ShapeDtypeStruct(shape, jnp.float32)


def end_call(step, act, start, in_map, rate, block=None):
    rows, width = step.shape
    states = rate.shape[0]
    block = block or block_of(width, 768)
    wide, mark, maps, held, line, total = specs(rows, states, block)
    return pl.pallas_call(
        end_kernel,
        grid=(width // block,),
        in_specs=[wide, wide, mark, maps, held],
        out_specs=total,
        out_shape=f32(states + group, width),
        compiler_params=params(40),
        cost_estimate=pl.CostEstimate(flops=8 * rows * states * width, bytes_accessed=6 * rows * width, transcendentals=rows * states * width),
        name="state_end",
    )(step, act, start, in_map, rate)


def scan_call(step, act, start, in_map, out_map, rate, entry, skip, block=None):
    rows, width = step.shape
    states = rate.shape[0]
    block = block or block_of(width, 768)
    wide, mark, maps, held, line, total = specs(rows, states, block)
    return pl.pallas_call(
        scan_kernel,
        grid=(width // block,),
        in_specs=[wide, wide, mark, maps, maps, held, held, line],
        out_specs=wide,
        out_shape=f32(rows, width),
        compiler_params=params(40),
        cost_estimate=pl.CostEstimate(flops=12 * rows * states * width, bytes_accessed=10 * rows * width, transcendentals=rows * states * width),
        name="state_scan",
    )(step, act, start, in_map, out_map, rate, entry, skip)


def entry_call(step, start, out_map, rate, grad, block=None):
    rows, width = step.shape
    states = rate.shape[0]
    block = block or block_of(width, 768)
    wide, mark, maps, held, line, total = specs(rows, states, block)
    return pl.pallas_call(
        entry_kernel,
        grid=(width // block,),
        in_specs=[wide, mark, maps, held, wide],
        out_specs=held,
        out_shape=f32(states, width),
        compiler_params=params(40),
        cost_estimate=pl.CostEstimate(flops=8 * rows * states * width, bytes_accessed=8 * rows * width, transcendentals=rows * states * width),
        name="adjoint_entry",
    )(step, start, out_map, rate, grad)


def back_call(step, act, start, in_map, out_map, rate, entry, adj, skip, grad, block=None):
    rows, width = step.shape
    states = rate.shape[0]
    block = block or block_of(width, 768)
    wide, mark, maps, held, line, total = specs(rows, states, block)
    return pl.pallas_call(
        back_kernel,
        grid=(width // block,),
        in_specs=[wide, wide, mark, maps, maps, held, held, held, line, wide],
        out_specs=[wide, wide, held, maps, maps],
        out_shape=[
            f32(rows, width), f32(rows, width), f32(states, width),
            f32(rows, states, lanes), f32(rows, states, lanes),
        ],
        scratch_shapes=[
            pltpu.VMEM((rows + 1, states, block), jnp.float32),
            pltpu.VMEM((rows, states, block), jnp.float32),
        ],
        compiler_params=params(56),
        cost_estimate=pl.CostEstimate(flops=40 * rows * states * width, bytes_accessed=20 * rows * width, transcendentals=rows * states * width),
        name="scan_back",
    )(step, act, start, in_map, out_map, rate, entry, adj, skip, grad)


def from_behind(array, axis, by):
    length = lax.axis_size(axis)
    pairs = [(i, i + by) for i in range(length) if 0 <= i + by < length]
    return lax.ppermute(array, axis, pairs)


def norm_scale(residual, gain):
    return (
        residual * lax.rsqrt(jnp.mean(residual * residual, axis=-1, keepdims=True) + epsilon) * gain
    )


def product(left, right):
    return jnp.dot(left, right, preferred_element_type=jnp.float32)


def cross_rows(left, right):
    return lax.dot_general(
        left, right, (((0,), (0,)), ((), ())), preferred_element_type=jnp.float32
    )


def cross_cols(left, right):
    return lax.dot_general(
        left, right, (((1,), (1,)), ((), ())), preferred_element_type=jnp.float32
    )


def gate_product(values, gates):
    return values * jax.nn.silu(gates)


def doc_ids(lengths_row, positions):
    boundaries = jnp.cumsum(lengths_row, dtype=jnp.int32)
    counted = jnp.sum(
        (positions[:, None] >= boundaries[None, :]).astype(jnp.int32), axis=1, dtype=jnp.int32
    )
    return jnp.where(positions < 0, -1, counted)


def conv_act(wide_in, taps_weight, taps_bias, documents):
    tap_count = taps_weight.shape[0]
    row_count = wide_in.shape[0] - tap_count + 1
    own_docs = documents[tap_count - 1 :]
    summed = taps_bias + taps_weight[tap_count - 1] * wide_in[tap_count - 1 :]
    for offset in range(1, tap_count):
        start_row = tap_count - 1 - offset
        lagged = wide_in[start_row : start_row + row_count]
        same_doc = (documents[start_row : start_row + row_count] == own_docs)[:, None]
        summed = summed + taps_weight[start_row] * jnp.where(same_doc, lagged, 0.0)
    return jax.nn.silu(summed)


def dispatch_tables(chosen, capacity):
    indicator = chosen.astype(jnp.int32)
    row_count, expert_count = indicator.shape
    earlier_rows = jnp.cumsum(indicator, axis=0, dtype=jnp.int32) - indicator
    slot_rank = jnp.sum(earlier_rows * indicator, axis=1, dtype=jnp.int32)
    expert_of = jnp.sum(
        indicator * jnp.arange(expert_count, dtype=jnp.int32)[None, :], axis=1, dtype=jnp.int32
    )
    slot_index = expert_of * capacity + slot_rank
    all_slots = jnp.arange(expert_count * capacity, dtype=jnp.int32)
    matches = slot_index[None, :] == all_slots[:, None]
    token_index = jnp.sum(
        jnp.where(matches, jnp.arange(row_count, dtype=jnp.int32)[None, :], 0),
        axis=1,
        dtype=jnp.int32,
    )
    token_index = token_index + row_count * (1 - jnp.any(matches, axis=1).astype(jnp.int32))
    return (slot_index, token_index)


def rows_rows(left, right):
    return lax.dot_general(
        left, right, (((0,), (0,)), ((), ())), preferred_element_type=jnp.float32
    )


def expert_kernel(x_ref, up_ref, down_ref, pre_ref, hidden_ref, out_ref, total):
    step = pl.program_id(0)
    pre = product(x_ref[...], up_ref[...])
    pre_ref[...] = pre
    hidden = jax.nn.gelu(pre).astype(jnp.bfloat16)
    hidden_ref[...] = hidden
    part = product(hidden, down_ref[...])

    @pl.when(step == 0)
    def _():
        total[...] = part

    @pl.when(step > 0)
    def _():
        total[...] += part

    @pl.when(step == pl.num_programs(0) - 1)
    def _():
        out_ref[...] = total[...].astype(jnp.bfloat16)


def expert_back_kernel(back_ref, up_ref, down_ref, pre_ref, back_pre_ref, out_ref, total):
    step = pl.program_id(0)
    back_hidden = cross_cols(back_ref[...], down_ref[...])
    back_pre = jax.vjp(jax.nn.gelu, pre_ref[...])[1](back_hidden)[0].astype(jnp.bfloat16)
    back_pre_ref[...] = back_pre
    part = cross_cols(back_pre, up_ref[...])

    @pl.when(step == 0)
    def _():
        total[...] = part

    @pl.when(step > 0)
    def _():
        total[...] += part

    @pl.when(step == pl.num_programs(0) - 1)
    def _():
        out_ref[...] = total[...].astype(jnp.bfloat16)


def expert_call(rows_in, up, down, pre=None):
    rows, width = rows_in.shape
    hidden_width = up.shape[1]
    block = 512
    fixed = pl.BlockSpec((rows, width), lambda i: (0, 0))
    wide = pl.BlockSpec((rows, block), lambda i: (0, i))
    first = pl.BlockSpec((width, block), lambda i: (0, i))
    second = pl.BlockSpec((block, width), lambda i: (i, 0))
    low = jax.ShapeDtypeStruct((rows, hidden_width), jnp.bfloat16)
    out = jax.ShapeDtypeStruct((rows, width), jnp.bfloat16)
    forward = pre is None
    return pl.pallas_call(
        expert_kernel if forward else expert_back_kernel,
        grid=(hidden_width // block,),
        in_specs=[fixed, first, second] + ([] if forward else [wide]),
        out_specs=[wide, wide, fixed] if forward else [wide, fixed],
        out_shape=[f32(rows, hidden_width), low, out] if forward else [low, out],
        scratch_shapes=[pltpu.VMEM((rows, width), jnp.float32)],
        compiler_params=params(40),
        cost_estimate=pl.CostEstimate(
            flops=4 * rows * width * hidden_width,
            bytes_accessed=4 * width * hidden_width + 6 * rows * hidden_width,
            transcendentals=rows * hidden_width,
        ),
        name="expert_rows" if forward else "expert_rows_back",
    )(rows_in, up, down, *(() if forward else (pre,)))


def expert_grads(part, hidden, back_pre, back_flat, flat_rows, received=()):
    rows, width = back_flat.shape
    half = hidden.shape[1] // 2
    block = 384
    steps = half // block

    def body(part_ref, hidden_ref, back_ref, flat_ref, x_ref, *refs):
        del part_ref
        outs = refs[len(received) :]
        for k, (left, right) in enumerate(((back_ref, x_ref), (hidden_ref, flat_ref))):
            total = rows_rows(left[...], right[...])
            if received:
                total = total + refs[k][...].astype(jnp.float32)
            outs[k][...] = total.astype(jnp.bfloat16)

    wide = pl.BlockSpec((rows, block), lambda i, part_ref: (0, part_ref[0] * steps + i))
    fixed = pl.BlockSpec((rows, width), lambda i, part_ref: (0, 0))
    tall = pl.BlockSpec((block, width), lambda i, part_ref: (i, 0))
    out = jax.ShapeDtypeStruct((half, width), jnp.bfloat16)
    return pl.pallas_call(
        body,
        grid_spec=pltpu.PrefetchScalarGridSpec(
            num_scalar_prefetch=1,
            grid=(steps,),
            in_specs=[wide, wide, fixed, fixed] + [tall] * len(received),
            out_specs=[tall, tall],
        ),
        out_shape=[out, out],
        compiler_params=params(40),
        cost_estimate=pl.CostEstimate(
            flops=4 * rows * width * half, bytes_accessed=8 * half * width, transcendentals=0
        ),
        name="expert_grads",
    )(part, hidden, back_pre, back_flat, flat_rows, *received)


def pack_small(masters):
    mixer, conv, conv_bias, select, step, step_bias, decay, skip, expert, router = masters
    chan, states = decay.shape[1:]
    taps, ranks, low_rank = conv.shape[1], select.shape[2], step.shape[1]
    part, expert_count = router.shape[1:]
    thin = taps + states + 3

    def body(mixer_ref, conv_ref, conv_bias_ref, select_ref, step_ref, step_bias_ref, decay_ref,
             skip_ref, expert_ref, router_ref, out_ref, rows, columns):
        def shift(by):
            down = lax.broadcasted_iota(jnp.int32, (lanes, lanes), 0)
            right = lax.broadcasted_iota(jnp.int32, (lanes, lanes), 1)
            return jnp.where(right == down + by, 1.0, 0.0).astype(jnp.bfloat16)

        across = lax.broadcasted_iota(jnp.int32, (chan, chan), 0)
        along = lax.broadcasted_iota(jnp.int32, (chan, chan), 1)
        same = jnp.where(across == along, 1.0, 0.0).astype(jnp.bfloat16)
        rows[...] = jnp.zeros_like(rows)
        rows[:taps] = conv_ref[0]
        rows[thin - 3 : thin - 2] = conv_bias_ref[...]
        rows[thin - 2 : thin - 1] = step_bias_ref[...]
        rows[thin - 1 : thin] = skip_ref[...]
        rows[thin : thin + 1, :part] = mixer_ref[...]
        rows[thin + 1 : thin + 2, :part] = expert_ref[...]
        total = cross_cols(same, rows[...].astype(jnp.bfloat16))
        columns[...] = jnp.zeros_like(columns)
        columns[:, :states] = decay_ref[0]
        total = total + product(columns[...].astype(jnp.bfloat16), shift(taps))
        columns[...] = jnp.zeros_like(columns)
        columns[:part, :expert_count] = router_ref[0]
        total = total + product(columns[...].astype(jnp.bfloat16), shift(thin + 2))
        out_ref[:, 2 * lanes :] = total.astype(jnp.bfloat16)
        columns[...] = jnp.zeros_like(columns)
        columns[:, :ranks] = select_ref[0]
        out_ref[:, :lanes] = columns[...].astype(jnp.bfloat16)
        rows[...] = jnp.zeros_like(rows)
        rows[:low_rank] = step_ref[0]
        total = cross_cols(same, rows[...].astype(jnp.bfloat16))
        out_ref[:, lanes : 2 * lanes] = total.astype(jnp.bfloat16)

    return pl.pallas_call(
        body,
        out_shape=jax.ShapeDtypeStruct((chan, 3 * lanes), jnp.bfloat16),
        scratch_shapes=[
            pltpu.VMEM((lanes, chan), jnp.float32),
            pltpu.VMEM((chan, lanes), jnp.float32),
        ],
        name="pack_small",
    )(*masters)


def gather_kernel(
    phase, along_dp, along_expert, own_refs, layer_refs,
    here_sem, z_send, z_recv, xy_send, xy_recv, c_send, c_recv,
):
    section = lax.axis_index("section")
    d = lax.axis_index("dp")
    e = lax.axis_index("expert")
    arrays = range(len(layer_refs[0]))
    mesh_id = pl.DeviceIdType.MESH
    ways = (1, -1)
    direct = [m for m in range(1, along_expert) if m != 3]

    def exists(index):
        return jnp.logical_and(index >= 0, index < along_dp)

    barrier = pltpu.get_barrier_semaphore()
    peers = [(section, d, e ^ m) for m in range(1, along_expert)] + [(1 - section, d, e)]
    for peer in peers:
        pl.semaphore_signal(barrier, inc=1, device_id=peer, device_id_type=mesh_id)
    expected = len(peers)
    if phase == 0:
        for way in ways:

            @pl.when(exists(d + way))
            def _():
                pl.semaphore_signal(
                    barrier, inc=1, device_id=(section, d + way, e), device_id_type=mesh_id
                )

        expected = expected + jnp.where(d > 0, 1, 0) + jnp.where(d < along_dp - 1, 1, 0)
    pl.semaphore_wait(barrier, expected)

    items = [(0, 0, 0)] + [
        (1 + 2 * step + (way < 0), way, step) for step in range(along_dp - 1) for way in ways
    ]

    def origin(item):
        index, way, step = item
        return d - way * (step + 1) if way else d

    def mine(item):
        if item[1] == 0:
            return phase == 0
        if item[2] > 0:
            return phase == 1
        return True if item[1] < 0 else phase == 0

    def here_now(item):
        if item[1] < 0 and item[2] == 0:
            return (d == 0) if phase == 0 else (d > 0)
        return d >= 0

    def when(item, *more):
        if item[1] == 0 and not more:
            return lambda work: work()
        alive = exists(origin(item))
        for other in more:
            alive = jnp.logical_and(alive, other)
        return pl.when(alive)

    def work(all_refs, other_refs):
        def place(item, m):
            return origin(item) * along_expert + (e ^ m)

        def copy(item, m, a, peer, send, recv):
            held = all_refs[a].at[place(item, m)]
            own = phase == 0 and item[1] == 0 and m == 0
            return pltpu.make_async_remote_copy(
                src_ref=own_refs[a] if own else held,
                dst_ref=held,
                send_sem=send,
                recv_sem=recv,
                device_id=peer,
                device_id_type=mesh_id,
            )

        def onward(item, way, a):
            step = item[2] + 1 if item[1] else 0
            k = 0 if way > 0 else 1
            peer = (section, d + way, e)
            return copy(item, 0, a, peer, z_send.at[k, step, a], z_recv.at[k, step, a])

        def to_expert(item, m, a):
            peer = (section, d, e ^ m)
            sems = (xy_send.at[item[0], m - 1, a], xy_recv.at[item[0], m - 1, a])
            return copy(item, 0, a, peer, *sems)

        def relayed(item, a):
            return 1 + (a + (item[2] + 1 if a == arrays[-1] else 0)) % 2

        def relay(item, m, a):
            peer = (section, d, e ^ 3 ^ m)
            sems = (xy_send.at[item[0], 2, a], xy_recv.at[item[0], 2, a])
            return copy(item, m, a, peer, *sems)

        def to_core(item, m, a):
            peer = (1 - section, d, e)
            return copy(item, m, a, peer, c_send.at[item[0], m, a], c_recv.at[item[0], m, a])

        def landed(ref, sem):
            pltpu.make_async_copy(ref, ref, sem).wait()

        def here(a):
            return pltpu.make_async_copy(
                own_refs[a], all_refs[a].at[place(items[0], 0)], here_sem.at[a]
            )

        def share(item):
            for a in arrays:
                for m in direct:
                    to_expert(item, m, a).start()

        def gather(item):
            for m in direct:
                for a in arrays:
                    landed(all_refs[a].at[place(item, m)], xy_recv.at[item[0], m - 1, a])
                    if m < 3 and relayed(item, a) == 3 - m:
                        relay(item, m, a).start()
                    to_core(item, m, a).start()

        def gather_last(item):
            for a in arrays:
                landed(all_refs[a].at[place(item, 3)], xy_recv.at[item[0], 2, a])
                to_core(item, 3, a).start()

        def finish_shared(item):
            for a in arrays:
                for m in direct:
                    to_expert(item, m, a).wait_send()
                relay(item, 3 - relayed(item, a), a).wait_send()
                for m in range(1, along_expert):
                    finish_core(item, m, a)

        def finish_core(item, m, a):
            to_core(item, m, a).wait_send()
            landed(other_refs[a].at[place(item, m)], c_recv.at[item[0], m, a])

        if phase == 0:
            for a in arrays:
                here(a).start()
                for way in ways:

                    @pl.when(exists(d + way))
                    def _():
                        onward(items[0], way, a).start()

                for m in direct:
                    to_expert(items[0], m, a).start()
                to_core(items[0], 0, a).start()
            queue = [items[0]]
            for step in range(along_dp - 1):
                for item in [item for item in items[1:] if item[2] == step]:
                    k = 0 if item[1] > 0 else 1

                    @when(item)
                    def _():
                        for a in arrays:
                            landed(all_refs[a].at[place(item, 0)], z_recv.at[k, step, a])

                    if step < along_dp - 2:

                        @when(item, exists(d + item[1]))
                        def _():
                            for a in arrays:
                                onward(item, item[1], a).start()

                    @when(item)
                    def _():
                        for a in arrays:
                            to_core(item, 0, a).start()

                    if mine(item):
                        when(item, here_now(item))(lambda: share(item))
                for item in queue:
                    when(item, here_now(item))(lambda: gather(item))
                queue = [item for item in items[1:] if item[2] == step and mine(item)]
            for item in queue:
                when(item, here_now(item))(lambda: gather(item))
            for item in items:
                if mine(item):
                    when(item, here_now(item))(lambda: gather_last(item))
            for a in arrays:
                here(a).wait()
            for item in items:
                if mine(item):
                    when(item, here_now(item))(lambda: finish_shared(item))

                @when(item)
                def _():
                    for a in arrays:
                        finish_core(item, 0, a)

                for way in ways if item[1] == 0 else (item[1],):
                    if item[1] == 0 or item[2] < along_dp - 2:

                        @when(item, exists(d + way))
                        def _():
                            for a in arrays:
                                onward(item, way, a).wait_send()
        else:
            rest = [item for item in items if mine(item)]
            for step in (share, gather, gather_last, finish_shared):
                for item in rest:
                    when(item, here_now(item))(lambda: step(item))

    @pl.when(section == 0)
    def _():
        work(layer_refs[0], layer_refs[1])

    @pl.when(section == 1)
    def _():
        work(layer_refs[1], layer_refs[0])


def gather_call(phase, parts, held=()):
    along_dp, along_expert = lax.axis_size("dp"), lax.axis_size("expert")
    total = len(parts) if phase == 0 else len(held) // 2
    given = parts if phase == 0 else held
    items = 2 * along_dp - 1

    def body(*refs):
        outs = refs[len(given) : len(given) + 2 * total]
        gather_kernel(
            phase, along_dp, along_expert, refs[: len(given)], (outs[:total], outs[total:]),
            *refs[len(given) + 2 * total :],
        )

    dma = pltpu.SemaphoreType.DMA
    shapes = [
        jax.ShapeDtypeStruct((along_dp * along_expert,) + part.shape, part.dtype)
        for part in parts
    ]
    return pl.pallas_call(
        body,
        in_specs=[pl.BlockSpec(memory_space=pltpu.HBM)] * len(given),
        out_specs=[pl.BlockSpec(memory_space=pltpu.HBM)] * (2 * total),
        out_shape=shapes * 2
        if phase == 0
        else [jax.ShapeDtypeStruct(part.shape, part.dtype) for part in held],
        input_output_aliases={} if phase == 0 else {k: k for k in range(2 * total)},
        scratch_shapes=[
            dma((total,)),
            dma((2, along_dp - 1, total)),
            dma((2, along_dp - 1, total)),
            dma((items, along_expert - 1, total)),
            dma((items, along_expert - 1, total)),
            dma((items, along_expert, total)),
            dma((items, along_expert, total)),
        ],
        compiler_params=pltpu.CompilerParams(collective_id=phase, has_side_effects=True),
        cost_estimate=pl.CostEstimate(flops=0, bytes_accessed=250 * 2**20, transcendentals=0),
        name="weights_along_dp" if phase == 0 else "weights_across",
    )(*given)


def carry_kernel(count, backward, *refs):
    if backward:
        end_ref, totals_ref, rate_ref, entry_ref, ends_ref, send_sem, recv_sem = refs
        shared = [ends_ref]
    else:
        end_ref, rate_ref, entry_ref, totals_ref, ends_ref, send_sem, recv_sem = refs
        shared = [ends_ref, totals_ref]
    states = rate_ref.shape[0]
    e = lax.axis_index("expert")
    mesh_id = pl.DeviceIdType.MESH

    def peer(m):
        return (lax.axis_index("section"), lax.axis_index("dp"), e ^ m)

    barrier = pltpu.get_barrier_semaphore()
    for m in range(1, count):
        pl.semaphore_signal(barrier, inc=1, device_id=peer(m), device_id_type=mesh_id)
    pl.semaphore_wait(barrier, count - 1)
    ends_ref[e] = end_ref[:states].astype(jnp.bfloat16)
    if not backward:
        totals_ref[e] = jnp.sum(end_ref[states:], axis=0, keepdims=True)

    def copy(m, a):
        return pltpu.make_async_remote_copy(
            src_ref=shared[a].at[e],
            dst_ref=shared[a].at[e],
            send_sem=send_sem.at[m - 1, a],
            recv_sem=recv_sem.at[m - 1, a],
            device_id=peer(m),
            device_id_type=mesh_id,
        )

    for m in range(1, count):
        for a in range(len(shared)):
            copy(m, a).start()
    for m in range(1, count):
        for a in range(len(shared)):
            there = shared[a].at[e ^ m]
            pltpu.make_async_copy(there, there, recv_sem.at[m - 1, a]).wait()
    width = rate_ref.shape[1]
    for start in range(0, width, lanes):
        cols = slice(start, start + lanes)
        state = jnp.zeros((states, lanes), jnp.float32)
        for k in range(count - 1, -1, -1) if backward else range(count):
            reached = jnp.where(k > e if backward else k < e, 1.0, 0.0)
            kept = jnp.exp(rate_ref[:, cols] * totals_ref[k, :, cols])
            new = kept * state + ends_ref[k, :, cols].astype(jnp.float32)
            state = state + reached * (new - state)
        entry_ref[:, cols] = state
    for m in range(1, count):
        for a in range(len(shared)):
            copy(m, a).wait_send()


def carry_call(end, rate, totals=None):
    count = lax.axis_size("expert")
    states, width = rate.shape
    backward = totals is not None
    dma = pltpu.SemaphoreType.DMA
    vmem = pl.BlockSpec(memory_space=pltpu.VMEM)
    operands = (end, totals, rate) if backward else (end, rate)
    total_shape = jax.ShapeDtypeStruct((count, 1, width), jnp.float32)
    out = pl.pallas_call(
        functools.partial(carry_kernel, count, backward),
        in_specs=[vmem] * len(operands),
        out_specs=[vmem] if backward else [vmem, vmem],
        out_shape=[f32(states, width)] + ([] if backward else [total_shape]),
        scratch_shapes=[
            pltpu.VMEM((count, states, width), jnp.bfloat16),
            dma((count - 1, 2)),
            dma((count - 1, 2)),
        ],
        compiler_params=pltpu.CompilerParams(
            collective_id=3 if backward else 2, has_side_effects=True
        ),
        name="adjoint_carry" if backward else "state_carry",
    )(*operands)
    return out


def settle_kernel(along_dp, along_expert, taps_ref, small_ref, taps_out, small_out,
                  taps_held, small_held, taps_part, small_part, taps_last, small_last,
                  xy_send, xy_recv, z_send, z_recv):
    section = lax.axis_index("section")
    d = lax.axis_index("dp")
    e = lax.axis_index("expert")
    mesh_id = pl.DeviceIdType.MESH
    pairs = ((taps_ref, taps_held, taps_part, taps_last, taps_out),
             (small_ref, small_held, small_part, small_last, small_out))

    barrier = pltpu.get_barrier_semaphore()
    peers = [(section, d, e ^ m) for m in range(1, along_expert)]
    peers += [(section, lax.rem(d + k, along_dp), e) for k in range(1, along_dp)]
    for peer in peers:
        pl.semaphore_signal(barrier, inc=1, device_id=peer, device_id_type=mesh_id)
    pl.semaphore_wait(barrier, len(peers))

    def across(m, a):
        return pltpu.make_async_remote_copy(
            src_ref=pairs[a][0].at[e ^ m], dst_ref=pairs[a][1].at[m - 1],
            send_sem=xy_send.at[m - 1, a], recv_sem=xy_recv.at[m - 1, a],
            device_id=(section, d, e ^ m), device_id_type=mesh_id,
        )

    def along(k, a):
        there = lax.rem(d + k, along_dp)
        return pltpu.make_async_remote_copy(
            src_ref=pairs[a][2].at[there], dst_ref=pairs[a][3].at[k - 1],
            send_sem=z_send.at[k - 1, a], recv_sem=z_recv.at[k - 1, a],
            device_id=(section, there, e), device_id_type=mesh_id,
        )

    def landed(ref, sem):
        pltpu.make_async_copy(ref, ref, sem).wait()

    for a in range(2):
        for m in range(1, along_expert):
            across(m, a).start()
    for a, (own, held, part, last, out) in enumerate(pairs):
        for m in range(1, along_expert):
            landed(held.at[m - 1], xy_recv.at[m - 1, a])
        for k in range(along_dp):
            total = own[e, k].astype(jnp.float32)
            for m in range(1, along_expert):
                total = total + held[m - 1, k].astype(jnp.float32)
            part[k] = total.astype(jnp.bfloat16)
        for k in range(1, along_dp):
            along(k, a).start()
    for a, (own, held, part, last, out) in enumerate(pairs):
        total = part[d].astype(jnp.float32)
        for k in range(1, along_dp):
            landed(last.at[k - 1], z_recv.at[k - 1, a])
            total = total + last[k - 1].astype(jnp.float32)
        out[...] = total.astype(jnp.bfloat16)
    for a in range(2):
        for m in range(1, along_expert):
            across(m, a).wait_send()
        for k in range(1, along_dp):
            along(k, a).wait_send()


def settle_call(taps, small):
    along_dp, along_expert = lax.axis_size("dp"), lax.axis_size("expert")
    vmem = pl.BlockSpec(memory_space=pltpu.VMEM)
    dma = pltpu.SemaphoreType.DMA
    arrays = (taps, small)

    def room(*lead):
        return [pltpu.VMEM(lead + array.shape[2:], jnp.bfloat16) for array in arrays]

    return pl.pallas_call(
        functools.partial(settle_kernel, along_dp, along_expert),
        in_specs=[vmem] * 2,
        out_specs=[vmem] * 2,
        out_shape=[jax.ShapeDtypeStruct(array.shape[2:], jnp.bfloat16) for array in arrays],
        scratch_shapes=room(along_expert - 1, along_dp)
        + room(along_dp)
        + room(along_dp - 1)
        + [dma((along_expert - 1, 2))] * 2
        + [dma((along_dp - 1, 2))] * 2,
        compiler_params=pltpu.CompilerParams(
            collective_id=4, has_side_effects=True, vmem_limit_bytes=40 * 2**20
        ),
        cost_estimate=pl.CostEstimate(flops=0, bytes_accessed=200 * 2**20, transcendentals=0),
        name="last_settle",
    )(*arrays)


def small_grads_call(select, step, conv, decay, lines, models, router, ranks, low_rank):
    across, along = lax.axis_size("dp"), lax.axis_size("expert")
    count = across * along
    chan = select.shape[0] // count
    part = router.shape[1] // count
    taps, states = conv.shape[0], decay.shape[0]

    def body(select_ref, step_ref, conv_ref, decay_ref, a_ref, b_ref, c_ref, mixer_ref, expert_ref,
             router_ref, out_ref, rows, models_rows):
        down = lax.broadcasted_iota(jnp.int32, (lanes, lanes), 0)
        right = lax.broadcasted_iota(jnp.int32, (lanes, lanes), 1)
        same = jnp.where(down == right, 1.0, 0.0).astype(jnp.bfloat16)
        rows[...] = jnp.zeros_like(rows)
        rows[ranks : ranks + taps] = conv_ref[...]
        rows[ranks + taps : ranks + taps + states] = decay_ref[...]
        at = ranks + taps + states
        for k, ref in enumerate((a_ref, b_ref, c_ref)):
            rows[at + k : at + k + 1] = ref[...]
        models_rows[...] = jnp.zeros_like(models_rows)
        models_rows[low_rank : low_rank + 1] = mixer_ref[...]
        models_rows[low_rank + 1 : low_rank + 2] = expert_ref[...]
        models_rows[low_rank + 2 : low_rank + 2 + router_ref.shape[0]] = router_ref[...]
        first = rows_rows(rows[...].astype(jnp.bfloat16), same) + select_ref[...]
        second = step_ref[...]
        model = rows_rows(models_rows[...].astype(jnp.bfloat16), same)
        for j in range(count):
            spot = (j % along) * across + j // along
            out_ref[spot, 0] = first[j * chan : (j + 1) * chan].astype(jnp.bfloat16)
            block = second[j * chan : (j + 1) * chan]
            top = block[:part] + model[j * part : (j + 1) * part]
            out_ref[spot, 1] = jnp.concatenate([top, block[part:]], axis=0).astype(jnp.bfloat16)

    return pl.pallas_call(
        body,
        out_shape=jax.ShapeDtypeStruct((count, 2, chan, lanes), jnp.bfloat16),
        scratch_shapes=[
            pltpu.VMEM((lanes, count * chan), jnp.float32),
            pltpu.VMEM((lanes, router.shape[1]), jnp.float32),
        ],
        compiler_params=pltpu.CompilerParams(vmem_limit_bytes=40 * 2**20),
        name="small_gradients",
    )(select, step, conv, decay, *lines, *models, router)


def swap(array):
    return lax.ppermute(array, "section", [(0, 1), (1, 0)])


def pick(first, left, right):
    return jnp.where(first, left, right), jnp.where(first, right, left)


def halves(array, first, axis):
    width = array.shape[axis] // 2
    low = lax.slice_in_dim(array, 0, width, axis=axis)
    high = lax.slice_in_dim(array, width, 2 * width, axis=axis)
    return pick(first, low, high)


def turned(array, axis, hop):
    length = lax.axis_size(axis)
    return lax.ppermute(array, axis, [(i, (i + hop) % length) for i in range(length)])


def crossed(array, axis, mask):
    length = lax.axis_size(axis)
    return lax.ppermute(array, axis, [(i, i ^ mask) for i in range(length)])


def expert_parts(up, down, first):
    pairs = [
        halves(master.astype(jnp.bfloat16), first, axis)
        for axis, master in enumerate((down, up))
    ]
    others = [swap(sent) for _, sent in pairs]
    down, up = [pick(first, own, got) for (own, _), got in zip(pairs, others)]
    return [up[0], down[0], up[1], down[1]]


def expert_spread(up, down):
    return tuple(
        lax.all_gather(part, ("section", "dp"), axis=axis, tiled=True)
        for axis, part in ((1, up), (0, down))
    )


def tie(values, after):
    count = len(values)

    def body(*refs):
        del refs

    return pl.pallas_call(
        body,
        in_specs=[pl.BlockSpec(memory_space=pl.ANY)] * (count + len(after)),
        out_specs=[pl.BlockSpec(memory_space=pl.ANY)] * count,
        out_shape=[jax.ShapeDtypeStruct(value.shape, value.dtype) for value in values],
        input_output_aliases={k: k for k in range(count)},
        name="order",
    )(*values, *after)


class LineSum:
    def __init__(self, up, down):
        self.parts = (up, down)
        self.here, self.count = lax.axis_index("dp"), lax.axis_size("dp")
        self.width = up.shape[0] // self.count
        self.step, self.moving = 0, (None, None)

    def chunk(self, index):
        start = jnp.clip(index, 0, self.count - 1) * self.width
        cuts = [lax.dynamic_slice_in_dim(part, start, self.width, 0) for part in self.parts]
        return jnp.stack(cuts).astype(jnp.float32)

    def advance(self, steps=1):
        for _ in range(steps):
            ahead = self.count - 1 - self.step
            if ahead == 0:
                break
            moved = []
            for way, moving in zip((1, -1), self.moving):
                held = self.chunk(self.here + way * ahead)
                if moving is not None:
                    held = held + moving.astype(jnp.float32)
                pairs = [
                    (i, i + way) for i in range(self.count) if 0 <= i + way * ahead < self.count
                ]
                moved.append(lax.ppermute(held.astype(jnp.bfloat16), "dp", pairs))
            self.moving = tuple(moved)
            self.step += 1
        return self.moving

    def total(self):
        up, down = self.advance(self.count)
        summed = self.chunk(self.here) + up.astype(jnp.float32) + down.astype(jnp.float32)
        return summed.astype(jnp.bfloat16)


def joined(pair, product_of):
    sent = swap(product_of(pair[1]).astype(jnp.bfloat16))
    return (product_of(pair[0]) + sent.astype(jnp.float32)).astype(jnp.bfloat16)


def by_expert(array, split):
    rows, width = array.shape
    across, along = lax.axis_size("dp"), lax.axis_size("expert")
    parts = array.reshape(rows, across, along, split, width // (across * along * split))
    return parts.transpose(0, 3, 2, 1, 4).reshape(rows, width)


def settle_expert(total):
    return lax.psum_scatter(total, "expert", scatter_dimension=0, tiled=True)


def settle_dp(total):
    return lax.psum_scatter(total, "dp", scatter_dimension=0, tiled=True)


def settle_direct(total):
    here, along = lax.axis_index("expert"), lax.axis_size("expert")
    width = total.shape[0] // along

    def chunk(array, index, size):
        return lax.dynamic_slice_in_dim(array, index * size, size, 0)

    summed = chunk(total, here, width).astype(jnp.float32)
    for mask in range(1, along):
        summed = summed + crossed(chunk(total, here ^ mask, width), "expert", mask).astype(
            jnp.float32
        )
    total = summed.astype(jnp.bfloat16)
    here, across = lax.axis_index("dp"), lax.axis_size("dp")
    width = width // across
    summed = chunk(total, here, width).astype(jnp.float32)
    for hop in range(1, across):
        there = lax.rem(here + hop, across)
        summed = summed + turned(chunk(total, there, width), "dp", hop).astype(jnp.float32)
    return summed.astype(jnp.bfloat16)


def hand_back(parts, first, cut):
    own, sent = pick(first, parts[0], parts[1])
    low, high = pick(first, own, swap(sent))
    return jnp.concatenate([low, high], axis=cut).astype(jnp.float32)


def widen(array):
    return jnp.pad(array, ((0, 0), (0, lanes - array.shape[1])))


def piled(parts):
    total, at = None, 0
    rows = sum(part.shape[0] for part in parts)
    for part in parts:
        padded = jnp.pad(part, ((at, rows - at - part.shape[0]), (0, 0)))
        total = padded if total is None else total + padded
        at += part.shape[0]
    return total


def dispatch_back(grad_out, gate_value, token_index, expert_count, capacity):
    back_result = (gate_value[:, None] * grad_out).astype(jnp.bfloat16)
    none = jnp.zeros((1, grad_out.shape[1]), jnp.bfloat16)
    padded = jnp.concatenate([back_result, none], axis=0)
    outgoing = padded[token_index].reshape(expert_count, capacity, -1)
    return lax.all_to_all(outgoing, "expert", split_axis=0, concat_axis=0, tiled=True)


def layer_forward(residual, small, big, routing, documents, mark, low_rank, grad_out):
    conv_part, gate_part, output_weight, up_weight, down_weight = big
    row_count, model_width = residual.shape
    tap_count = small.conv.shape[0]
    states = small.rate.shape[0]
    expert_count = small.router.shape[0]
    capacity = 2 * row_count // expert_count
    normed = norm_scale(residual, small.mixer_gain).astype(jnp.bfloat16)
    conv_in = product(normed, conv_part).astype(jnp.bfloat16)
    gate_in = product(normed, gate_part).astype(jnp.bfloat16)
    rim_rows = from_behind(conv_in[row_count - tap_count + 1 :], "expert", 1)
    wide_in = jnp.concatenate([rim_rows, conv_in], axis=0)
    activated = conv_act(
        wide_in.astype(jnp.float32), small.conv, small.conv_bias, documents
    ).astype(jnp.bfloat16)
    projected = product(activated, small.select)
    step_low = jnp.where(jnp.arange(lanes) < low_rank, projected, 0.0).astype(jnp.bfloat16)
    in_wide = jnp.broadcast_to(
        projected[:, low_rank : low_rank + states, None], (row_count, states, lanes)
    )
    out_wide = jnp.broadcast_to(
        projected[:, low_rank + states : low_rank + 2 * states, None], (row_count, states, lanes)
    )
    step_pre = cross_cols(step_low, small.step) + small.step_bias
    step_size = jax.nn.softplus(step_pre)
    ends = end_call(step_size, activated, mark, in_wide, small.rate)
    entry_state, totals = carry_call(ends, small.rate)
    scanned = scan_call(
        step_size, activated, mark, in_wide, out_wide, small.rate, entry_state, small.skip
    )
    gated_out = gate_product(scanned, gate_in.astype(jnp.float32)).astype(jnp.bfloat16)
    middle = residual + product(gated_out, output_weight)
    normed_two = norm_scale(middle, small.expert_gain).astype(jnp.bfloat16)
    logits = cross_cols(normed_two, small.router)
    probability = jax.nn.softmax(logits, axis=-1)
    chosen = routing[:, None] == jnp.arange(expert_count, dtype=jnp.int32)[None, :]
    gate_value = jnp.sum(jnp.where(chosen, probability, 0.0), axis=1)
    slot_index, token_index = dispatch_tables(chosen, capacity)
    padded = jnp.concatenate([normed_two, jnp.zeros((1, model_width), jnp.bfloat16)], axis=0)
    outgoing = padded[token_index].reshape(expert_count, capacity, model_width)
    arrived = lax.all_to_all(outgoing, "expert", split_axis=0, concat_axis=0, tiled=True)
    flat_rows = arrived.reshape(-1, model_width)
    back_arrived = None
    if grad_out is not None:
        back_arrived = dispatch_back(grad_out, gate_value, token_index, expert_count, capacity)
        (flat_rows,) = tie([flat_rows], (back_arrived,))
    pre_act, hidden, result = expert_call(flat_rows, up_weight, down_weight)
    result = result.reshape(arrived.shape)
    returned = lax.all_to_all(result, "expert", split_axis=0, concat_axis=0, tiled=True)
    mixture = returned.reshape(-1, model_width)[slot_index].astype(jnp.float32)
    out_residual = middle + gate_value[:, None] * mixture
    stored = SimpleNamespace(
        residual=residual, normed=normed, wide_in=wide_in, gate_in=gate_in, activated=activated,
        step_low=step_low, step_pre=step_pre, step_size=step_size, in_wide=in_wide,
        out_wide=out_wide, totals=totals, entry_state=entry_state, scanned=scanned,
        gated_out=gated_out, middle=middle, normed_two=normed_two, probability=probability,
        chosen=chosen, gate_value=gate_value, slot_index=slot_index, token_index=token_index,
        pre_act=pre_act, hidden=hidden, flat_rows=flat_rows, mixture=mixture,
        documents=documents, mark=mark, back_arrived=back_arrived,
    )
    return out_residual, stored


def layer_backward(grad_out, kept, small, big, section, earlier, pending, ranks):
    conv_part, gate_part, output_weight, up_weight, down_weight = big
    first = section == 0
    row_count, model_width = grad_out.shape
    tap_count = small.conv.shape[0]
    expert_count = small.router.shape[0]
    capacity = 2 * row_count // expert_count
    back_gate = jnp.sum(grad_out * kept.mixture, axis=1)
    back_arrived = kept.back_arrived
    if back_arrived is None:
        back_arrived = dispatch_back(
            grad_out, kept.gate_value, kept.token_index, expert_count, capacity
        )
    back_flat = back_arrived.reshape(-1, model_width)
    back_pre, back_expert = expert_call(back_flat, up_weight, down_weight, kept.pre_act)
    back_expert = back_expert.reshape(back_arrived.shape)
    if earlier is not None:
        back_expert, *earlier.moving = tie([back_expert, *earlier.moving], ())
        earlier.advance()
    back_returned = lax.all_to_all(back_expert, "expert", split_axis=0, concat_axis=0, tiled=True)
    sources = (kept.hidden, back_pre, back_flat, kept.flat_rows)
    own_part, sent_part = jnp.reshape(section, (1,)), jnp.reshape(1 - section, (1,))
    received = [swap(part) for part in expert_grads(sent_part, *sources)]
    grad_up, grad_down = expert_grads(own_part, *sources, received)
    line = LineSum(grad_up, grad_down)
    line.advance()
    back_tokens = back_returned.reshape(-1, model_width)[kept.slot_index].astype(jnp.float32)
    back_logits = (
        (back_gate * kept.gate_value)[:, None]
        * (kept.chosen.astype(jnp.float32) - kept.probability)
    ).astype(jnp.bfloat16)
    grad_router = cross_rows(back_logits, kept.normed_two)
    back_normed_two = back_tokens + product(back_logits, small.router)
    back_mid_norm, grad_expert_gain = jax.vjp(norm_scale, kept.middle, small.expert_gain)[1](
        back_normed_two
    )
    back_middle = grad_out + back_mid_norm
    back_branch = back_middle.astype(jnp.bfloat16)
    gated_pair = halves(by_expert(kept.gated_out, 2), first, 1)
    grad_output = joined(gated_pair, lambda half: cross_rows(half, back_branch))
    back_gated = cross_cols(back_branch, output_weight)
    back_scanned, back_gate_in = jax.vjp(
        gate_product, kept.scanned, kept.gate_in.astype(jnp.float32)
    )[1](back_gated)
    normed_rows = by_expert(kept.normed, 1)
    part_rows = model_width // (lax.axis_size("dp") * lax.axis_size("expert"))
    back_gate_in = back_gate_in.astype(jnp.bfloat16)
    grad_gate = joined(halves(back_gate_in, first, 1), lambda half: cross_rows(normed_rows, half))
    together = [part.reshape(-1, part_rows, model_width) for part in (grad_gate, grad_output)]
    together = jnp.stack(together, axis=1).reshape(-1, model_width)
    late = settle_expert(together)
    (back_scanned,) = tie([back_scanned], (grad_up, grad_down, together))
    rate = small.rate
    back_ends = entry_call(kept.step_size, kept.mark, kept.out_wide, rate, back_scanned)
    (adjoint,) = carry_call(back_ends, rate, kept.totals)
    back_act, back_step, grad_decay, back_in, back_out = back_call(
        kept.step_size, kept.activated, kept.mark, kept.in_wide, kept.out_wide,
        rate, kept.entry_state, adjoint, small.skip, back_scanned,
    )
    moving = list(line.moving) + ([] if earlier is None else list(earlier.moving))
    back_step, *moving = tie([back_step, *moving], pending)
    line.moving = tuple(moving[:2])
    if earlier is not None:
        earlier.moving = tuple(moving[2:])
    line.advance()
    act_float = kept.activated.astype(jnp.float32)
    grad_skip = jnp.sum(back_scanned * act_float, axis=0, keepdims=True)
    back_step_pre = back_step * jax.nn.sigmoid(kept.step_pre)
    grad_step_bias = jnp.sum(back_step_pre, axis=0, keepdims=True)
    back_step_low = back_step_pre.astype(jnp.bfloat16)
    grad_step = cross_rows(back_step_low, kept.step_low)
    back_rank = product(back_step_low, small.step)
    low_rank = ranks - 2 * rate.shape[0]
    maps = jnp.concatenate([jnp.sum(back_in, axis=2), jnp.sum(back_out, axis=2)], axis=1)
    back_projected = back_rank + jnp.pad(maps, ((0, 0), (low_rank, lanes - ranks)))
    back_projected = back_projected.astype(jnp.bfloat16)
    grad_select = cross_rows(kept.activated, back_projected)
    back_activated = back_act + cross_cols(back_projected, small.select)

    def conv_piece(wide_float, taps_in, bias_in):
        return conv_act(wide_float, taps_in, bias_in, kept.documents)

    back_wide, grad_conv, grad_conv_bias = jax.vjp(
        conv_piece, kept.wide_in.astype(jnp.float32), small.conv, small.conv_bias
    )[1](back_activated)
    rim_back = from_behind(back_wide[: tap_count - 1], "expert", -1)
    back_conv_in = back_wide[tap_count - 1 :] + jnp.pad(
        rim_back, ((row_count - tap_count + 1, 0), (0, 0))
    )
    back_conv_in = back_conv_in.astype(jnp.bfloat16)
    grad_taps_in = joined(halves(back_conv_in, first, 1), lambda half: cross_rows(normed_rows, half))
    back_normed = cross_cols(back_conv_in, conv_part) + cross_cols(back_gate_in, gate_part)
    back_residual_norm, grad_mixer_gain = jax.vjp(
        norm_scale, kept.residual, small.mixer_gain
    )[1](back_normed)
    back_residual = back_middle + back_residual_norm
    if earlier is not None:
        grad_select, grad_step = tie([grad_select, grad_step], (grad_taps_in,))
    small_grads = small_grads_call(
        grad_select, grad_step, grad_conv, grad_decay,
        (grad_conv_bias[None], grad_step_bias, grad_skip),
        (grad_mixer_gain[None], grad_expert_gain[None]), grad_router, ranks, ranks - 2 * rate.shape[0],
    )
    return back_residual, grad_taps_in, late, line, small_grads


def small_outputs(total, taps, states, ranks, low_rank, expert_count, part):
    chan = total.shape[1]
    thin = taps + states + 3

    def body(total_ref, *outs):
        mixer, conv, conv_bias, select, step, step_bias, decay, skip, expert, router = outs
        down = lax.broadcasted_iota(jnp.int32, (lanes, lanes), 0)
        right = lax.broadcasted_iota(jnp.int32, (lanes, lanes), 1)
        same = jnp.where(down == right, 1.0, 0.0).astype(jnp.bfloat16)
        rows = cross_cols(same, total_ref[0])
        others = cross_cols(same, total_ref[1])
        select[0] = total_ref[0].astype(jnp.float32)[:, :ranks]
        step[0] = others[:low_rank]
        conv[0] = rows[ranks : ranks + taps]
        decay[0] = total_ref[0].astype(jnp.float32)[:, ranks + taps : ranks + taps + states]
        for ref, at in ((conv_bias, thin - 3), (step_bias, thin - 2), (skip, thin - 1)):
            ref[...] = rows[ranks + at : ranks + at + 1]
        mixer[...] = others[low_rank : low_rank + 1, :part]
        expert[...] = others[low_rank + 1 : low_rank + 2, :part]
        whole = total_ref[1].astype(jnp.float32)
        router[0] = whole[:part, low_rank + 2 : low_rank + 2 + expert_count]

    line = f32(1, chan)
    return pl.pallas_call(
        body,
        out_shape=[
            f32(1, part), f32(1, taps, chan), line, f32(1, chan, ranks), f32(1, low_rank, chan),
            line, f32(1, chan, states), line, f32(1, part), f32(1, part, expert_count),
        ],
        name="small_outputs",
    )(total)


def expert_outputs(own, got, section):
    width, model_width = own.shape[1:]

    def body(section_ref, own_ref, got_ref, up_ref, down_ref):
        def fill(low, high):
            across = lax.broadcasted_iota(jnp.int32, (2 * width, 2 * width), 0)
            along = lax.broadcasted_iota(jnp.int32, (2 * width, 2 * width), 1)
            same = jnp.where(across == along, 1.0, 0.0).astype(jnp.bfloat16)
            up_ref[...] = rows_rows(jnp.concatenate([low[0], high[0]], axis=0), same)
            down_ref[:width] = low[1].astype(jnp.float32)
            down_ref[width:] = high[1].astype(jnp.float32)

        @pl.when(section_ref[0] == 0)
        def _():
            fill(own_ref, got_ref)

        @pl.when(section_ref[0] != 0)
        def _():
            fill(got_ref, own_ref)

    vmem = pl.BlockSpec(memory_space=pltpu.VMEM)
    return pl.pallas_call(
        body,
        in_specs=[pl.BlockSpec(memory_space=pltpu.SMEM), vmem, vmem],
        out_specs=[vmem, vmem],
        out_shape=[f32(model_width, 2 * width), f32(2 * width, model_width)],
        compiler_params=pltpu.CompilerParams(vmem_limit_bytes=40 * 2**20),
        name="expert_outputs",
    )(jnp.reshape(section, (1,)), own, got)


def doc_marks(documents, tap_count):
    own = documents[tap_count - 1 :]
    begins = own != documents[tap_count - 2 : -1]
    return jnp.broadcast_to(jnp.where(begins, reset, 0.0)[:, None], (own.shape[0], lanes))


def shards(
    inputs,
    cotangent,
    routes,
    lengths,
    mixer_gain,
    input_weight,
    conv_weight,
    conv_bias,
    select_weight,
    step_weight,
    step_bias,
    decay_log,
    skip_gain,
    output_weight,
    expert_gain,
    router_weight,
    up_weight,
    down_weight,
):
    section = lax.axis_index("section")
    first = section == 0
    count = lax.axis_size("dp") * lax.axis_size("expert")
    row_count, model_width = inputs.shape[1:]
    tap_count = conv_weight.shape[1]
    chan = conv_bias.shape[1]
    low_rank = step_weight.shape[1]
    states = decay_log.shape[2]
    ranks = select_weight.shape[2]
    expert_count = router_weight.shape[2]

    thin = tap_count + states + 3
    packed = pack_small(
        (
            mixer_gain, conv_weight, conv_bias, select_weight, step_weight, step_bias, decay_log,
            skip_gain, expert_gain, router_weight,
        )
    )
    wide = input_weight.shape[2] // 2
    experts = expert_parts(up_weight[0, 0], down_weight[0, 0], first)
    early = gather_call(
        0,
        (
            packed,
            input_weight[0, :, :wide].astype(jnp.bfloat16),
            input_weight[0, :, wide:].astype(jnp.bfloat16),
            output_weight[0].astype(jnp.bfloat16),
        ),
    )
    experts = tie(experts, early[:1])
    gathered = gather_call(1, (), early)
    gathered = (gathered[:4], gathered[4:])
    part = model_width // count

    def unpack(layer):
        whole = gathered[layer][0].reshape(count * chan, 3 * lanes)
        select, step, rows = [whole[:, k * lanes : (k + 1) * lanes] for k in range(3)]
        rows = rows.T[: thin + 2 + expert_count].astype(jnp.float32)
        model = rows[thin:].reshape(-1, count, chan)[:, :, :part].reshape(-1, model_width)
        return SimpleNamespace(
            select=select, step=step, conv=rows[:tap_count],
            rate=-jnp.exp(rows[tap_count : tap_count + states]),
            conv_bias=rows[thin - 3], step_bias=rows[thin - 2 : thin - 1],
            skip=rows[thin - 1 : thin], mixer_gain=model[0], expert_gain=model[1],
            router=model[2:].astype(jnp.bfloat16),
        )

    small = [unpack(0), unpack(1)]
    experts_two = [expert_spread(*experts[:2]), expert_spread(*experts[2:])]
    big = [
        (
            gathered[k][1].reshape(model_width, wide),
            gathered[k][2].reshape(model_width, wide),
            gathered[k][3].reshape(wide, model_width),
        )
        + experts_two[k]
        for k in range(2)
    ]

    own_routes, sent_routes = pick(first, routes[0, 0, :, 0], routes[0, 1, :, 0])
    routing = pick(first, own_routes, swap(sent_routes))
    lengths_row = lax.dynamic_index_in_dim(lengths[:, 0, :], section, 0, keepdims=False)
    positions = lax.axis_index("expert") * row_count + jnp.arange(
        1 - tap_count, row_count, dtype=jnp.int32
    )
    documents = doc_ids(lengths_row, positions)
    mark = doc_marks(documents, tap_count)

    residual = lax.dynamic_index_in_dim(inputs, section, 0, keepdims=False).astype(jnp.float32)
    grad_last = lax.dynamic_index_in_dim(cotangent, section, 0, keepdims=False)
    grad_last = grad_last.astype(jnp.float32)
    outputs_seen = []
    kept = []
    for layer in range(2):
        out_residual, stored = layer_forward(
            residual, small[layer], big[layer], routing[layer], documents, mark, low_rank, grad_last if layer else None
        )
        outputs_seen.append(out_residual.astype(jnp.bfloat16))
        residual = outputs_seen[-1].astype(jnp.float32)
        kept.append(stored)

    grad_out = grad_last
    input_grads = [None, None]
    settled = [None, None]
    small_sums = [None, None]
    line, pending = None, ()
    for layer in (1, 0):
        earlier = line
        back_residual, grad_taps_in, late, line, small_grads = layer_backward(
            grad_out, kept[layer], small[layer], big[layer], section, earlier, pending, ranks
        )
        input_grads[layer] = back_residual
        grad_out = back_residual.astype(jnp.bfloat16).astype(jnp.float32)
        if layer == 1:
            pending = (settle_dp(settle_expert(grad_taps_in)), settle_dp(late))
        else:
            settled[1] = pending + (earlier.total(),)
            final_late = settle_dp(late)
        small_sums[layer] = small_grads

    across, along = lax.axis_size("dp"), lax.axis_size("expert")
    own_small, sent_small = pick(first, small_sums[0], small_sums[1])
    own_small = own_small.astype(jnp.float32) + swap(sent_small).astype(jnp.float32)
    last, small_last = settle_call(
        grad_taps_in.reshape(along, across, part, model_width),
        own_small.astype(jnp.bfloat16).reshape(along, across, 2, chan, lanes),
    )
    settled[0] = (last, final_late, line.total())
    small_out = small_outputs(
        small_last, tap_count, states, ranks, low_rank, expert_count, part
    )
    expert_own, expert_sent = pick(first, settled[0][2], settled[1][2])
    up_back, down_back = expert_outputs(expert_own, swap(expert_sent), section)
    both_late = [(late_one[1][:part], late_one[1][part:]) for late_one in settled]

    def whole_input():
        taps = hand_back((settled[0][0], settled[1][0]), first, 1)
        return jnp.concatenate([taps, hand_back([pair[0] for pair in both_late], first, 1)], axis=1)

    def both(array):
        mine, sent = pick(first, array[0], array[1])
        return jnp.stack(pick(first, mine, swap(sent)))[None]

    return (
        both(outputs_seen),
        both(input_grads),
        small_out[0],
        whole_input()[None],
        *small_out[1:8],
        hand_back([pair[1] for pair in both_late], first, 0)[None],
        *small_out[8:],
        up_back[None, None],
        down_back[None, None],
    )


def solution(mesh):
    return jax.shard_map(
        shards,
        mesh=mesh,
        in_specs=(
            P(None, ("dp", "expert"), None),
            P(None, ("dp", "expert"), None),
            P("section", None, ("dp", "expert"), None),
            P(None, "dp", None),
            P("section", ("dp", "expert")),
            P("section", ("dp", "expert"), None),
            P("section", None, ("dp", "expert")),
            P("section", ("dp", "expert")),
            P("section", ("dp", "expert"), None),
            P("section", None, ("dp", "expert")),
            P("section", ("dp", "expert")),
            P("section", ("dp", "expert"), None),
            P("section", ("dp", "expert")),
            P("section", ("dp", "expert"), None),
            P("section", ("dp", "expert")),
            P("section", ("dp", "expert"), None),
            P("section", "expert", None, "dp"),
            P("section", "expert", "dp", None),
        ),
        out_specs=(
            P("section", None, ("dp", "expert"), None),
            P("section", None, ("dp", "expert"), None),
            P("section", ("dp", "expert")),
            P("section", ("dp", "expert"), None),
            P("section", None, ("dp", "expert")),
            P("section", ("dp", "expert")),
            P("section", ("dp", "expert"), None),
            P("section", None, ("dp", "expert")),
            P("section", ("dp", "expert")),
            P("section", ("dp", "expert"), None),
            P("section", ("dp", "expert")),
            P("section", ("dp", "expert"), None),
            P("section", ("dp", "expert")),
            P("section", ("dp", "expert"), None),
            P("section", "expert", None, "dp"),
            P("section", "expert", "dp", None),
        ),
        check_vma=False,
    )
```
